32 devices in a mesh: pb: 4 (over z), kv: 8 (over y, x, core).
Axes of the slice: x: 2, y: 2, z: 4, core: 2. Of those that a mesh axis runs over, the one named last changes fastest.
Arguments:
- queries: bfloat16 [4096, 1024], P(('pb', 'kv')), may hold values from -6 to 6
- key_rows: bfloat16 [4096, 128], P(('pb', 'kv')), may hold values from -6 to 6
- value_rows: bfloat16 [4096, 128], P(('pb', 'kv')), may hold values from -6 to 6
- out_grad: bfloat16 [4096, 1024], P(('pb', 'kv')), may hold values from -6 to 6
- doc_ids: int32 [32], replicated, may hold values from 0 to 15, never falling along the last dimension, each value on 1 to 8 neighbouring positions
Outputs:
- attended: bfloat16 [4096, 1024], P(('pb', 'kv'))
- query_grad: bfloat16 [4096, 1024], P(('pb', 'kv'))
- key_grad: bfloat16 [4096, 128], P(('pb', 'kv'))
- value_grad: bfloat16 [4096, 128], P(('pb', 'kv'))
The draws below stay inside these ranges and needn't reach their ends.
Inputs may be any that keep to these rules, and one draw needn't show every extreme that they name: `doc_ids`: ids never fall along the sequence; each document covers 1 to 8 consecutive blocks, and one covers exactly 8.
All inputs are finite; a program needn't handle non-finite values.
Results may differ from the reference program's by a relative error of at most 0.03.
Values may be sent and summed in bfloat16 or wider, within the bound.
No kernel may reach another device: no remote copies, remote signals or barrier semaphores. Data moves between devices by JAX's collectives and lax.ppermute only.
A program may use at most 64 MiB of HBM per device.

```python
import math
import jax
import jax.numpy as jnp
import numpy as np
from jax import lax

HEADS = 8
HEAD_DIM = 128
BLOCK = 128
LEN = 4096
NBLK = 32
MOST = 8
DOCS = 16


def draw_queries(key, part):
    sample_key = jax.random.fold_in(key, 1)
    sample = jax.random.truncated_normal(sample_key, -6.0, 6.0, (NBLK, BLOCK, HEADS, HEAD_DIM), jnp.float32)
    return sample.reshape(LEN, HEADS * HEAD_DIM).astype(jnp.bfloat16)


def draw_key_rows(key, part):
    sample_key = jax.random.fold_in(key, 2)
    sample = jax.random.truncated_normal(sample_key, -6.0, 6.0, (NBLK, BLOCK, HEAD_DIM), jnp.float32)
    return sample.reshape(LEN, HEAD_DIM).astype(jnp.bfloat16)


def block_levels(key, dims, shards, smallest, high):
    factor_of, own = 1.0, jax.random.fold_in(key, 6)
    for axis_at, shards_of in shards:
        heights = jnp.exp(jax.random.uniform(jax.random.fold_in(own, axis_at), (shards_of,), jnp.float32, smallest / len(shards), high / len(shards)))
        factor_of = factor_of * jnp.repeat(heights, dims[axis_at] // shards_of).reshape([-1 if axis == axis_at else 1 for axis in range(len(dims))])
    return factor_of


def profile(count, total, bound, skew):
    portions = [(1 << 20) // math.isqrt(rank ** skew) + 1 for rank in range(2, count + 1)]
    spare, counts = total - bound - (count - 1), [1] * (count - 1)
    while spare > 0:
        candidates = [i for i in range(count - 1) if counts[i] < bound]
        mass, left = sum([portions[i] for i in candidates]), spare
        for i in candidates:
            more = min(bound - counts[i], max(1, left * portions[i] // mass), spare)
            counts[i] = counts[i] + more
            spare = spare - more
    return np.array([bound] + counts)


def uneven_parts(rng, number_of, total, reach, slope):
    if number_of == 2:
        one = jax.random.randint(rng, (), max(1, total - reach), min(reach, total - 1) + 1)
        return jnp.stack([one, total - one])
    sizes = jnp.asarray(profile(number_of, total, reach, slope), jnp.int32)
    pairs = (number_of - 1) // 2
    giver, receiver = sizes[1:1 + 2 * pairs:2], sizes[2:2 + 2 * pairs:2]
    room = jnp.minimum(giver - 1, reach - receiver)
    shifted = jax.random.randint(jax.random.fold_in(rng, 1), (pairs,), 0, 1 << 20) % (room + 1)
    sizes = sizes.at[1:1 + 2 * pairs:2].set(giver - shifted).at[2:2 + 2 * pairs:2].set(receiver + shifted)
    return sizes[jax.random.permutation(jax.random.fold_in(rng, 2), number_of)]


def centred(key, shape, spread, bound, cuts=(), kind=jnp.bfloat16):
    level = block_levels(key, shape, cuts, -0.22, 0.18) if cuts else 1.0
    drawn = jax.random.normal(key, shape, jnp.float32) * spread * level
    return jnp.minimum(jnp.maximum(drawn, -bound), bound).astype(kind)


def setup_inputs(seed: int = 0) -> dict:
    streams_of = jax.random.split(jax.random.key(seed), 6)
    queries = draw_queries(jax.random.fold_in(streams_of[5], 71), 0)
    key_rows = draw_key_rows(jax.random.fold_in(streams_of[5], 71), 0)
    value_rows = centred(streams_of[2], (LEN, HEAD_DIM), 1.0, 6.0, ((0, 32),))
    out_grad = centred(streams_of[3], (LEN, HEADS * HEAD_DIM), 1.0, 6.0, ((0, 32),))
    doc_ids = jnp.searchsorted(jnp.cumsum(uneven_parts(streams_of[4], DOCS, NBLK, MOST, 1)), jnp.arange(NBLK), side="right").astype(jnp.int32)
    return dict(queries=queries, key_rows=key_rows, value_rows=value_rows, out_grad=out_grad, doc_ids=doc_ids)


NEG_FILL = -1e30


def reference(queries, key_rows, value_rows, out_grad, doc_ids):
    score_scale = HEAD_DIM ** -0.5
    window_len = MOST * BLOCK
    pad_keys = jnp.concatenate([jnp.zeros((window_len, HEAD_DIM), key_rows.dtype), key_rows], axis=0)
    pad_values = jnp.concatenate([jnp.zeros((window_len, HEAD_DIM), value_rows.dtype), value_rows], axis=0)
    pad_docs = jnp.concatenate([jnp.full((MOST,), -1, jnp.int32), doc_ids.astype(jnp.int32)])
    local_pos = jnp.arange(BLOCK, dtype=jnp.int32)
    window_pos = jnp.arange(window_len, dtype=jnp.int32)

    def window(block_idx):
        win_start = ((block_idx + 1) * BLOCK).astype(jnp.int32)
        keys_win = lax.dynamic_slice_in_dim(pad_keys, win_start, window_len, 0)
        values_win = lax.dynamic_slice_in_dim(pad_values, win_start, window_len, 0)
        docs_win = jnp.repeat(lax.dynamic_slice_in_dim(pad_docs, (block_idx + 1).astype(jnp.int32), MOST, 0), BLOCK)
        query_doc = lax.dynamic_index_in_dim(doc_ids.astype(jnp.int32), block_idx, 0, keepdims=False)
        query_pos = block_idx * BLOCK + local_pos
        key_pos = block_idx * BLOCK + BLOCK - window_len + window_pos
        allowed = (docs_win == query_doc)[None, :] & (key_pos[None, :] <= query_pos[:, None])
        allowed = jnp.repeat(allowed, HEADS, axis=0)
        query_blk = lax.dynamic_slice_in_dim(queries, (block_idx * BLOCK).astype(jnp.int32), BLOCK, 0)
        query_blk = query_blk.reshape(BLOCK * HEADS, HEAD_DIM)
        scores = lax.dot_general(query_blk, keys_win, (((1,), (1,)), ((), ())), preferred_element_type=jnp.float32) * score_scale
        scores = jnp.where(allowed, scores, NEG_FILL)
        return keys_win, values_win, allowed, query_blk, scores

    def forward(block_idx):
        keys_win, values_win, allowed, query_blk, scores = window(block_idx)
        row_max = jnp.max(scores, axis=1)
        row_sum = jnp.sum(jnp.where(allowed, jnp.exp(scores - row_max[:, None]), 0.0), axis=1)
        log_total = row_max + jnp.log(row_sum)
        weights = jnp.where(allowed, jnp.exp(scores - log_total[:, None]), 0.0)
        mixed_rows = jnp.dot(weights.astype(jnp.bfloat16), values_win, preferred_element_type=jnp.float32)
        return mixed_rows.reshape(BLOCK, HEADS * HEAD_DIM).astype(jnp.bfloat16), log_total

    block_list = jnp.arange(NBLK, dtype=jnp.int32)
    attended_blocks, log_totals = lax.map(forward, block_list)
    attended = attended_blocks.reshape(LEN, HEADS * HEAD_DIM)
    delta_all = jnp.sum(out_grad.astype(jnp.float32).reshape(NBLK, BLOCK * HEADS, HEAD_DIM)
                        * attended.astype(jnp.float32).reshape(NBLK, BLOCK * HEADS, HEAD_DIM), axis=2)

    def backward(running, inputs):
        key_acc, value_acc = running
        block_idx, log_total, delta_rows = inputs
        keys_win, values_win, allowed, query_blk, scores = window(block_idx)
        weights = jnp.where(allowed, jnp.exp(scores - log_total[:, None]), 0.0)
        weights_b = weights.astype(jnp.bfloat16)
        grad_blk = lax.dynamic_slice_in_dim(out_grad, (block_idx * BLOCK).astype(jnp.int32), BLOCK, 0)
        grad_blk = grad_blk.reshape(BLOCK * HEADS, HEAD_DIM)
        grad_probs = lax.dot_general(grad_blk, values_win, (((1,), (1,)), ((), ())), preferred_element_type=jnp.float32)
        score_grad = (score_scale * weights * (grad_probs - delta_rows[:, None])).astype(jnp.bfloat16)
        query_part = jnp.dot(score_grad, keys_win, preferred_element_type=jnp.float32)
        key_part = lax.dot_general(score_grad, query_blk, (((0,), (0,)), ((), ())), preferred_element_type=jnp.float32)
        value_part = lax.dot_general(weights_b, grad_blk, (((0,), (0,)), ((), ())), preferred_element_type=jnp.float32)
        win_start = ((block_idx + 1) * BLOCK).astype(jnp.int32)
        key_acc = lax.dynamic_update_slice_in_dim(
            key_acc, lax.dynamic_slice_in_dim(key_acc, win_start, window_len, 0) + key_part, win_start, 0)
        value_acc = lax.dynamic_update_slice_in_dim(
            value_acc, lax.dynamic_slice_in_dim(value_acc, win_start, window_len, 0) + value_part, win_start, 0)
        return (key_acc, value_acc), query_part.reshape(BLOCK, HEADS * HEAD_DIM).astype(jnp.bfloat16)

    start_acc = jnp.zeros((window_len + LEN, HEAD_DIM), jnp.float32)
    final_acc, query_grads = lax.scan(backward, (start_acc, start_acc), (block_list, log_totals, delta_all))
    key_acc, value_acc = final_acc
    query_grad = query_grads.reshape(LEN, HEADS * HEAD_DIM)
    return attended, query_grad, key_acc[window_len:].astype(jnp.bfloat16), value_acc[window_len:].astype(jnp.bfloat16)
```

```python
import functools
import math

import jax
import jax.numpy as jnp
from jax import lax
from jax.experimental import pallas as pl
from jax.experimental.pallas import tpu as pltpu
from jax.sharding import PartitionSpec as P

HEADS = 8
HEAD_DIM = 128
BLOCK = 128
AXES = ("pb", "kv")
SCALE = HEAD_DIM ** (-0.5)
SCALE_LOG2 = SCALE / math.log(2.0)
FAR = 1e30
COLS = 256


def dot(left, right, left_dim, right_dim):
    return lax.dot_general(
        left, right, (((left_dim,), (right_dim,)), ((), ())), preferred_element_type=jnp.float32
    )


def attention_kernel(window, refs):
    half = window // 2
    doc_ref, query_ref, grad_ref, own_ref = refs[:4]
    lin_refs = refs[4 : 4 + half - 1]
    sib_refs = refs[4 + half - 1 : 4 + 2 * half - 1]
    sib_own_ref = refs[4 + 2 * half - 1]
    attended_ref, query_grad_ref, kept_ref, lin_out_ref, sib_out_ref = refs[5 + 2 * half - 1 : 10 + 2 * half - 1]
    keys, values, query_rows, grad_rows, weights_s, score_grad_s = refs[10 + 2 * half - 1 :]

    me = lax.axis_index("pb") * lax.axis_size("kv") + lax.axis_index("kv")
    core = lax.rem(me, 2)

    def place(slot, ref):
        keys[slot * BLOCK : (slot + 1) * BLOCK, :] = ref[:BLOCK, :]
        values[slot * BLOCK : (slot + 1) * BLOCK, :] = ref[BLOCK:, :]

    place(0, own_ref)
    for k in range(1, half):
        place(k, lin_refs[k - 1])
        place(half - 1 + k, sib_refs[k - 1])

    @pl.when(core == 0)
    def _():
        place(window - 1, sib_refs[half - 1])

    @pl.when(core == 1)
    def _():
        place(window - 1, sib_own_ref)

    my_doc = doc_ref[me]

    def reach(distance):
        at = me - distance
        return (at >= 0) & (doc_ref[jnp.maximum(at, 0)] == my_doc)

    allowed = [None]
    allowed += [reach(2 * k) for k in range(1, half)]
    allowed += [reach(2 * k - 1 + 2 * core) for k in range(1, half)]
    allowed += [reach(jnp.where(core == 0, window - 1, 1))]

    for h in range(HEADS):
        rows = slice(h * BLOCK, (h + 1) * BLOCK)
        query_rows[rows, :] = query_ref[:, rows]
        grad_rows[rows, :] = grad_ref[:, rows]

    key_row = lax.broadcasted_iota(jnp.int32, (BLOCK, COLS), 0)
    token = lax.broadcasted_iota(jnp.int32, (BLOCK, COLS), 1) % BLOCK
    causal = key_row <= token

    key_all, value_all = keys[...], values[...]
    for tile in range(HEADS * BLOCK // COLS):
        cols = slice(tile * COLS, (tile + 1) * COLS)
        scores = dot(key_all, query_rows[cols, :], 1, 1)
        probs_grad = dot(value_all, grad_rows[cols, :], 1, 1)
        parts = [scores[s * BLOCK : (s + 1) * BLOCK, :] for s in range(window)]
        parts[0] = jnp.where(causal, parts[0], -FAR)
        top = jnp.max(parts[0], axis=0, keepdims=True)
        for s in range(1, window):
            top = jnp.maximum(top, jnp.where(allowed[s], jnp.max(parts[s], axis=0, keepdims=True), -FAR))
        top = top * SCALE_LOG2
        raw, total, mixed = [], 0.0, 0.0
        for s in range(window):
            shift = top if s == 0 else jnp.where(allowed[s], top, FAR)
            e = jnp.exp2(parts[s] * SCALE_LOG2 - shift)
            raw.append(e)
            total = total + jnp.sum(e, axis=0, keepdims=True)
            mixed = mixed + jnp.sum(e * probs_grad[s * BLOCK : (s + 1) * BLOCK, :], axis=0, keepdims=True)
        inverse = 1.0 / total
        delta = mixed * inverse
        for s in range(window):
            rows = slice(s * BLOCK, (s + 1) * BLOCK)
            weights = raw[s] * inverse
            weights_s[rows, cols] = weights.astype(jnp.bfloat16)
            score_grad_s[rows, cols] = (weights * (probs_grad[rows, :] - delta)).astype(jnp.bfloat16)

    attended_t = dot(value_all, weights_s[...], 0, 0)
    query_grad_t = dot(key_all, score_grad_s[...], 0, 0) * SCALE
    for h in range(HEADS):
        rows = slice(h * BLOCK, (h + 1) * BLOCK)
        attended_ref[:, rows] = attended_t[:, rows].T.astype(jnp.bfloat16)
        query_grad_ref[:, rows] = query_grad_t[:, rows].T.astype(jnp.bfloat16)

    key_grad = dot(score_grad_s[...], query_rows[...], 1, 0) * SCALE
    value_grad = dot(weights_s[...], grad_rows[...], 1, 0)

    def hand_out(slot, ref, at):
        rows = slice(slot * BLOCK, (slot + 1) * BLOCK)
        ref[at, :BLOCK, :] = key_grad[rows, :].astype(ref.dtype)
        ref[at, BLOCK:, :] = value_grad[rows, :].astype(ref.dtype)

    hand_out(0, kept_ref, 0)
    for k in range(1, half):
        hand_out(k, lin_out_ref, k - 1)
        hand_out(half - 1 + k, sib_out_ref, k - 1)
    hand_out(window - 1, sib_out_ref, half - 1)


def attention(window, doc_ids, queries, out_grad, own, lins, sibs, sib_own):
    half = window // 2
    rows, width = queries.shape
    flat = HEADS * BLOCK
    vmem = pl.BlockSpec(memory_space=pltpu.VMEM)
    operands = [doc_ids, queries, out_grad, own, *lins, *sibs, sib_own]
    return pl.pallas_call(
        lambda *refs: attention_kernel(window, refs),
        out_shape=[
            jax.ShapeDtypeStruct((rows, width), jnp.bfloat16),
            jax.ShapeDtypeStruct((rows, width), jnp.bfloat16),
            jax.ShapeDtypeStruct((1, 2 * BLOCK, HEAD_DIM), jnp.float32),
            jax.ShapeDtypeStruct((half - 1, 2 * BLOCK, HEAD_DIM), jnp.float32),
            jax.ShapeDtypeStruct((half, 2 * BLOCK, HEAD_DIM), jnp.bfloat16),
        ],
        in_specs=[pl.BlockSpec(memory_space=pltpu.SMEM)] + [vmem] * (len(operands) - 1),
        out_specs=[vmem] * 5,
        scratch_shapes=[
            pltpu.VMEM((window * BLOCK, HEAD_DIM), jnp.bfloat16),
            pltpu.VMEM((window * BLOCK, HEAD_DIM), jnp.bfloat16),
            pltpu.VMEM((flat, HEAD_DIM), jnp.bfloat16),
            pltpu.VMEM((flat, HEAD_DIM), jnp.bfloat16),
            pltpu.VMEM((window * BLOCK, flat), jnp.bfloat16),
            pltpu.VMEM((window * BLOCK, flat), jnp.bfloat16),
        ],
        compiler_params=pltpu.CompilerParams(vmem_limit_bytes=40 * 2**20),
        name="attention",
    )(*operands)


def local(devices, queries, key_rows, value_rows, out_grad, doc_ids):
    window = lax.axis_size("kv")
    half = window // 2

    def ahead(block, k):
        return lax.ppermute(block, AXES, [(i, (i + 2 * k) % devices) for i in range(devices)])

    def swapped(block):
        return lax.ppermute(block, AXES, [(i, i ^ 1) for i in range(devices)])

    own = jnp.concatenate([key_rows, value_rows], axis=0)
    lins = [ahead(own, k) for k in range(1, half + 1)]
    sib_own = swapped(own)
    sibs = [swapped(block) for block in lins]
    attended, query_grad, kept, lin_out, sib_out = attention(
        window, doc_ids, queries, out_grad, own, lins[: half - 1], sibs, sib_own
    )
    from_sib = swapped(sib_out)
    sent = [(lin_out[k] + from_sib[k].astype(jnp.float32)).astype(jnp.bfloat16) for k in range(half - 1)]
    sent.append(from_sib[half - 1])
    back = [ahead(block, -(k + 1)) for k, block in enumerate(sent)]
    core = lax.axis_index("kv") % 2
    total = kept[0]
    for block in back[: half - 1]:
        total = total + block.astype(jnp.float32)
    total = total + jnp.where(core == 0, from_sib[half - 1], back[half - 1]).astype(jnp.float32)
    total = total.astype(jnp.bfloat16)
    return attended, query_grad, total[:BLOCK], total[BLOCK:]


def solution(mesh):
    split = P(AXES, None)
    devices = mesh.shape["pb"] * mesh.shape["kv"]
    return jax.shard_map(
        functools.partial(local, devices),
        mesh=mesh,
        in_specs=(split, split, split, split, P()),
        out_specs=(split, split, split, split),
        check_vma=False,
    )
```

```python
import functools
import math

import jax
import jax.numpy as jnp
from jax import lax
from jax.experimental import pallas as pl
from jax.experimental.pallas import tpu as pltpu
from jax.sharding import PartitionSpec as P

HEADS = 8
HEAD_DIM = 128
BLOCK = 128
FLAT = HEADS * BLOCK
AXES = ("pb", "kv")
SCALE = HEAD_DIM ** (-0.5)
SCALE_LOG2 = SCALE / math.log(2.0)
FAR = 1e30
COLS = 256
MIB = 2**20

VMEM = pl.BlockSpec(memory_space=pltpu.VMEM)
SMEM = pl.BlockSpec(memory_space=pltpu.SMEM)
HBM = pl.BlockSpec(memory_space=pltpu.HBM)


def dot(left, right, left_dim, right_dim):
    return lax.dot_general(
        left, right, (((left_dim,), (right_dim,)), ((), ())), preferred_element_type=jnp.float32
    )


class Slots:
    def __init__(self, window):
        self.window = window
        self.half = half = window // 2
        lins = [("lin", k) for k in range(1, half)]
        sibs = [("sib", k) for k in range(1, half)]
        self.early = ["own"] + lins[:-1] + sibs[:-2]
        self.late = [sibs[-2], lins[-1], sibs[-1], "last"]
        self.order = sibs + ["last"] + ["own"] + lins

    def rows(self, slot):
        at = self.order.index(slot) * BLOCK
        return slice(at, at + BLOCK)

    def distance(self, slot, core):
        if slot == "last":
            return jnp.where(core == 0, self.window - 1, 1)
        return 2 * slot[1] if slot[0] == "lin" else 2 * slot[1] - 1 + 2 * core


def position():
    me = lax.axis_index("pb") * lax.axis_size("kv") + lax.axis_index("kv")
    return me, lax.rem(me, 2)


def reached(doc_ref, slots, slot):
    if slot == "own":
        return None
    me, core = position()
    at = me - slots.distance(slot, core)
    return (at >= 0) & (doc_ref[jnp.maximum(at, 0)] == doc_ref[me])


def stacked(refs, part):
    return jnp.concatenate([ref[part * BLOCK : (part + 1) * BLOCK, :] for ref in refs], axis=0)


def tile_of(column):
    return slice(column * COLS, (column + 1) * COLS)


def absorb(parts, probs_grad, allowed, top, total, mixed):
    new_top = top
    for part, ok in zip(parts, allowed):
        peak = jnp.max(part, axis=0, keepdims=True) * SCALE_LOG2
        new_top = jnp.maximum(new_top, peak if ok is None else jnp.where(ok, peak, -FAR))
    rescale = jnp.exp2(top - new_top)
    total, mixed = total * rescale, mixed * rescale
    powers = []
    for s, (part, ok) in enumerate(zip(parts, allowed)):
        shift = new_top if ok is None else jnp.where(ok, new_top, FAR)
        power = jnp.exp2(part * SCALE_LOG2 - shift)
        powers.append(power)
        total = total + jnp.sum(power, axis=0, keepdims=True)
        mixed = mixed + jnp.sum(power * probs_grad[s * BLOCK : (s + 1) * BLOCK, :], axis=0, keepdims=True)
    return powers, new_top, total, mixed, rescale


def early_kernel(slots, *refs):
    count = len(slots.early)
    doc_ref, query_ref, grad_ref = refs[:3]
    blocks = refs[3 : 3 + count]
    query_rows, grad_rows, powers_ref, probs_ref, stats_ref, sems = refs[3 + count :]
    copies = []
    for h in range(HEADS):
        rows = slice(h * BLOCK, (h + 1) * BLOCK)
        copies.append(pltpu.make_async_copy(query_ref.at[:, rows], query_rows.at[rows, :], sems.at[0, h]))
        copies.append(pltpu.make_async_copy(grad_ref.at[:, rows], grad_rows.at[rows, :], sems.at[1, h]))
    for copy in copies:
        copy.start()
    allowed = [reached(doc_ref, slots, slot) for slot in slots.early]
    key_row = lax.broadcasted_iota(jnp.int32, (BLOCK, COLS), 0)
    token = lax.broadcasted_iota(jnp.int32, (BLOCK, COLS), 1) % BLOCK
    causal = key_row <= token
    keys, values = stacked(blocks, 0), stacked(blocks, 1)
    for copy in copies:
        copy.wait()
    stats_ref[...] = jnp.zeros_like(stats_ref)
    for column in range(FLAT // COLS):
        cols = tile_of(column)
        scores = dot(keys, query_rows[cols, :], 1, 1)
        probs_grad = dot(values, grad_rows[cols, :], 1, 1)
        parts = [scores[s * BLOCK : (s + 1) * BLOCK, :] for s in range(count)]
        parts[0] = jnp.where(causal, parts[0], -FAR)
        start = jnp.full((1, COLS), -FAR, jnp.float32), jnp.zeros((1, COLS)), jnp.zeros((1, COLS))
        powers, top, total, mixed, _ = absorb(parts, probs_grad, allowed, *start)
        for s in range(count):
            powers_ref[s * BLOCK : (s + 1) * BLOCK, cols] = powers[s]
        probs_ref[:, cols] = probs_grad
        stats_ref[0:1, cols] = top
        stats_ref[1:2, cols] = total
        stats_ref[2:3, cols] = mixed


def late_kernel(slots, *refs):
    half = slots.half
    doc_ref, query_rows, grad_rows, powers_ref, probs_ref, stats_ref = refs[:6]
    blocks = list(refs[6 : 6 + len(slots.late)])
    sib_own_ref = refs[6 + len(slots.late)]
    weights_ref, score_grad_ref, sib_out_ref, last_ref = refs[7 + len(slots.late) :]
    _, core = position()

    @pl.when(core == 0)
    def _():
        last_ref[...] = blocks[-1][...]

    @pl.when(core == 1)
    def _():
        last_ref[...] = sib_own_ref[...]

    blocks[-1] = last_ref
    allowed = [reached(doc_ref, slots, slot) for slot in slots.late]
    keys, values = stacked(blocks, 0), stacked(blocks, 1)
    for column in range(FLAT // COLS):
        cols = tile_of(column)
        scores = dot(keys, query_rows[cols, :], 1, 1)
        probs_grad = dot(values, grad_rows[cols, :], 1, 1)
        parts = [scores[s * BLOCK : (s + 1) * BLOCK, :] for s in range(len(blocks))]
        start = tuple(stats_ref[row : row + 1, cols] for row in range(3))
        powers, _, total, mixed, rescale = absorb(parts, probs_grad, allowed, *start)
        inverse = 1.0 / total
        delta = mixed * inverse
        early_factor = rescale * inverse

        def put(slot, weights, probs):
            rows = slots.rows(slot)
            weights_ref[rows, cols] = weights.astype(jnp.bfloat16)
            score_grad_ref[rows, cols] = (weights * (probs - delta)).astype(jnp.bfloat16)

        for s, slot in enumerate(slots.early):
            rows = slice(s * BLOCK, (s + 1) * BLOCK)
            put(slot, powers_ref[rows, cols] * early_factor, probs_ref[rows, cols])
        for s, slot in enumerate(slots.late):
            put(slot, powers[s] * inverse, probs_grad[s * BLOCK : (s + 1) * BLOCK, :])

    rows = slice(0, half * BLOCK)
    key_grad = dot(score_grad_ref[rows, :], query_rows[...], 1, 0) * SCALE
    value_grad = dot(weights_ref[rows, :], grad_rows[...], 1, 0)
    for k in range(half):
        rows = slice(k * BLOCK, (k + 1) * BLOCK)
        sib_out_ref[k, :BLOCK, :] = key_grad[rows, :].astype(jnp.bfloat16)
        sib_out_ref[k, BLOCK:, :] = value_grad[rows, :].astype(jnp.bfloat16)


def mine_kernel(slots, weights_ref, score_grad_ref, query_rows, grad_rows, mine_ref):
    half = slots.half
    rows = slice(half * BLOCK, slots.window * BLOCK)
    key_grad = dot(score_grad_ref[rows, :], query_rows[...], 1, 0) * SCALE
    value_grad = dot(weights_ref[rows, :], grad_rows[...], 1, 0)
    for k in range(half):
        rows = slice(k * BLOCK, (k + 1) * BLOCK)
        mine_ref[k, :BLOCK, :] = key_grad[rows, :]
        mine_ref[k, BLOCK:, :] = value_grad[rows, :]


def query_side_kernel(slots, *refs):
    weights_ref, score_grad_ref, sib_own_ref = refs[:3]
    blocks = list(refs[3 : 3 + slots.window])
    attended_ref, query_grad_ref, last_ref = refs[3 + slots.window :]
    _, core = position()
    at = slots.order.index("last")

    @pl.when(core == 0)
    def _():
        last_ref[...] = blocks[at][...]

    @pl.when(core == 1)
    def _():
        last_ref[...] = sib_own_ref[...]

    blocks[at] = last_ref
    attended_t = dot(stacked(blocks, 1), weights_ref[...], 0, 0)
    query_grad_t = dot(stacked(blocks, 0), score_grad_ref[...], 0, 0) * SCALE
    for h in range(HEADS):
        rows = slice(h * BLOCK, (h + 1) * BLOCK)
        attended_ref[:, rows] = attended_t[:, rows].T.astype(jnp.bfloat16)
        query_grad_ref[:, rows] = query_grad_t[:, rows].T.astype(jnp.bfloat16)


def cost(blocks, products):
    flops = 2 * products * blocks * BLOCK * FLAT * HEAD_DIM
    return pl.CostEstimate(flops=flops, bytes_accessed=blocks * BLOCK * FLAT * 4, transcendentals=0)


def local(devices, queries, key_rows, value_rows, out_grad, doc_ids):
    window = lax.axis_size("kv")
    slots = Slots(window)
    half = slots.half
    bf16, f32 = jnp.bfloat16, jnp.float32
    shape = jax.ShapeDtypeStruct
    params = pltpu.CompilerParams(vmem_limit_bytes=3 * window * MIB)

    def ahead(block, k):
        return lax.ppermute(block, AXES, [(i, (i + 2 * k) % devices) for i in range(devices)])

    def swapped(block):
        return lax.ppermute(block, AXES, [(i, i ^ 1) for i in range(devices)])

    own = jnp.concatenate([key_rows, value_rows], axis=0)
    lins = [ahead(own, k) for k in range(1, half + 1)]
    sib_own = swapped(own)
    sibs = [swapped(block) for block in lins]
    held = {"own": own, "last": sibs[-1]}
    for k in range(1, half):
        held["lin", k] = lins[k - 1]
        held["sib", k] = sibs[k - 1]

    early = len(slots.early)
    query_rows, grad_rows, powers, probs_grad, stats = pl.pallas_call(
        functools.partial(early_kernel, slots),
        out_shape=[
            shape((FLAT, HEAD_DIM), bf16),
            shape((FLAT, HEAD_DIM), bf16),
            shape((early * BLOCK, FLAT), f32),
            shape((early * BLOCK, FLAT), f32),
            shape((8, FLAT), f32),
        ],
        in_specs=[SMEM, HBM, HBM] + [VMEM] * early,
        out_specs=[VMEM] * 5,
        scratch_shapes=[pltpu.SemaphoreType.DMA((2, HEADS))],
        compiler_params=params,
        cost_estimate=cost(early, 2),
        name="early_scores",
    )(doc_ids, queries, out_grad, *[held[slot] for slot in slots.early])

    weights, score_grad, sib_out = pl.pallas_call(
        functools.partial(late_kernel, slots),
        out_shape=[
            shape((window * BLOCK, FLAT), bf16),
            shape((window * BLOCK, FLAT), bf16),
            shape((half, 2 * BLOCK, HEAD_DIM), bf16),
        ],
        in_specs=[SMEM] + [VMEM] * (6 + len(slots.late)),
        out_specs=[VMEM] * 3,
        scratch_shapes=[pltpu.VMEM((2 * BLOCK, HEAD_DIM), bf16)],
        compiler_params=params,
        cost_estimate=cost(window, 3),
        name="late_scores",
    )(
        doc_ids, query_rows, grad_rows, powers, probs_grad, stats,
        *[held[slot] for slot in slots.late], sib_own,
    )
    from_sib = swapped(sib_out)

    mine = pl.pallas_call(
        functools.partial(mine_kernel, slots),
        out_shape=shape((half, 2 * BLOCK, HEAD_DIM), f32),
        in_specs=[VMEM] * 4,
        out_specs=VMEM,
        compiler_params=params,
        cost_estimate=cost(half, 2),
        name="own_parity_grads",
    )(weights, score_grad, query_rows, grad_rows)

    attended, query_grad = pl.pallas_call(
        functools.partial(query_side_kernel, slots),
        out_shape=[shape(queries.shape, bf16), shape(queries.shape, bf16)],
        in_specs=[VMEM] * (3 + window),
        out_specs=[VMEM] * 2,
        scratch_shapes=[pltpu.VMEM((2 * BLOCK, HEAD_DIM), bf16)],
        compiler_params=params,
        cost_estimate=cost(window, 2),
        name="query_side",
    )(weights, score_grad, sib_own, *[held[slot] for slot in slots.order])

    sent = [(mine[k] + from_sib[k - 1].astype(f32)).astype(bf16) for k in range(1, half)]
    sent.append(from_sib[half - 1])
    back = [ahead(block, -(k + 1)) for k, block in enumerate(sent)]
    core = lax.axis_index("kv") % 2
    total = mine[0]
    for block in back[: half - 1]:
        total = total + block.astype(f32)
    total = total + jnp.where(core == 0, from_sib[half - 1], back[half - 1]).astype(f32)
    total = total.astype(bf16)
    return attended, query_grad, total[:BLOCK], total[BLOCK:]


def solution(mesh):
    split = P(AXES, None)
    devices = mesh.shape["pb"] * mesh.shape["kv"]
    return jax.shard_map(
        functools.partial(local, devices),
        mesh=mesh,
        in_specs=(split, split, split, split, P()),
        out_specs=(split, split, split, split),
        check_vma=False,
    )
```

```python
import functools
import math

import jax
import jax.numpy as jnp
from jax import lax
from jax.experimental import pallas as pl
from jax.experimental.pallas import tpu as pltpu
from jax.sharding import PartitionSpec as P

HEADS = 8
HEAD_DIM = 128
BLOCK = 128
FLAT = HEADS * BLOCK
AXES = ("pb", "kv")
SCALE = HEAD_DIM ** (-0.5)
SCALE_LOG2 = SCALE / math.log(2.0)
FAR = 1e30
COLS = 256
MIB = 2**20

VMEM = pl.BlockSpec(memory_space=pltpu.VMEM)
HBM = pl.BlockSpec(memory_space=pltpu.HBM)


def dot(left, right, left_dim, right_dim):
    return lax.dot_general(
        left, right, (((left_dim,), (right_dim,)), ((), ())), preferred_element_type=jnp.float32
    )


class Slots:
    def __init__(self, window):
        self.window = window
        self.half = half = window // 2
        lins = [("lin", k) for k in range(1, half)]
        sibs = [("sib", k) for k in range(1, half)]
        self.middle = lins[:-1]
        self.late = sibs + [lins[-1], "last"]
        self.order = sibs + ["last"] + ["own"] + lins

    def rows(self, slot):
        at = self.order.index(slot) * BLOCK
        return slice(at, at + BLOCK)

    def distance(self, slot, core):
        if slot == "last":
            return jnp.where(core == 0, self.window - 1, 1)
        return 2 * slot[1] if slot[0] == "lin" else 2 * slot[1] - 1 + 2 * core


def position():
    me = lax.axis_index("pb") * lax.axis_size("kv") + lax.axis_index("kv")
    return me, lax.rem(me, 2)


def reached(doc_ref, slots, slot):
    me, core = position()
    at = me - slots.distance(slot, core)
    return (at >= 0) & (doc_ref[jnp.maximum(at, 0)] == doc_ref[me])


def stacked(refs, part):
    return jnp.concatenate([ref[part * BLOCK : (part + 1) * BLOCK, :] for ref in refs], axis=0)


def tile_of(column):
    return slice(column * COLS, (column + 1) * COLS)


def absorb(parts, probs_grad, biases, top, total, mixed):
    new_top = top
    for part, bias in zip(parts, biases):
        new_top = jnp.maximum(new_top, jnp.max(part, axis=0, keepdims=True) * SCALE_LOG2 + bias)
    rescale = jnp.exp2(top - new_top)
    total, mixed = total * rescale, mixed * rescale
    powers = []
    for s, (part, bias) in enumerate(zip(parts, biases)):
        power = jnp.exp2(part * SCALE_LOG2 - (new_top - bias))
        powers.append(power)
        total = total + jnp.sum(power, axis=0, keepdims=True)
        mixed = mixed + jnp.sum(power * probs_grad[s * BLOCK : (s + 1) * BLOCK, :], axis=0, keepdims=True)
    return powers, new_top, total, mixed


def pair_kernel(key_ref, value_ref, pair_ref, sems):
    copies = [
        pltpu.make_async_copy(ref, pair_ref.at[part * BLOCK : (part + 1) * BLOCK, :], sems.at[part])
        for part, ref in enumerate((key_ref, value_ref))
    ]
    for copy in copies:
        copy.start()
    for copy in copies:
        copy.wait()


def own_kernel(
    slots, doc_hbm, query_ref, grad_ref, own_ref,
    query_rows, grad_rows, bias_ref, powers_ref, probs_ref, stats_ref, doc_ref, doc_sem, sems,
):
    copies = [pltpu.make_async_copy(doc_hbm, doc_ref, doc_sem)]
    for h in range(HEADS):
        rows = slice(h * BLOCK, (h + 1) * BLOCK)
        copies.append(pltpu.make_async_copy(query_ref.at[:, rows], query_rows.at[rows, :], sems.at[0, h]))
        copies.append(pltpu.make_async_copy(grad_ref.at[:, rows], grad_rows.at[rows, :], sems.at[1, h]))
    for copy in copies:
        copy.start()
    key_row = lax.broadcasted_iota(jnp.int32, (BLOCK, COLS), 0)
    token = lax.broadcasted_iota(jnp.int32, (BLOCK, COLS), 1) % BLOCK
    causal = key_row <= token
    for copy in copies:
        copy.wait()
    for row, slot in enumerate(slots.middle + slots.late):
        bias = jnp.where(reached(doc_ref, slots, slot), 0.0, -FAR)
        bias_ref[row : row + 1, :] = jnp.full((1, FLAT), bias, jnp.float32)
    for column in range(FLAT // COLS):
        cols = tile_of(column)
        scores = dot(own_ref[:BLOCK, :], query_rows[cols, :], 1, 1)
        probs_grad = dot(own_ref[BLOCK:, :], grad_rows[cols, :], 1, 1)
        scores = jnp.where(causal, scores, -FAR)
        start = jnp.full((1, COLS), -FAR, jnp.float32), jnp.zeros((1, COLS)), jnp.zeros((1, COLS))
        put_stage([scores], probs_grad, [0.0], start, column, powers_ref, probs_ref, stats_ref)


def put_stage(parts, probs_grad, biases, start, column, powers_ref, probs_ref, stats_ref):
    cols = tile_of(column)
    powers, top, total, mixed = absorb(parts, probs_grad, biases, *start)
    for s, power in enumerate(powers):
        powers_ref[s * BLOCK : (s + 1) * BLOCK, cols] = power
    probs_ref[:, cols] = probs_grad
    for row, value in enumerate((top, total, mixed)):
        stats_ref[row : row + 1, cols] = value


def middle_kernel(slots, *refs):
    count = len(slots.middle)
    bias_ref, query_rows, grad_rows, before_ref = refs[:4]
    blocks = refs[4 : 4 + count]
    powers_ref, probs_ref, stats_ref = refs[4 + count :]
    keys, values = stacked(blocks, 0), stacked(blocks, 1)
    for column in range(FLAT // COLS):
        cols = tile_of(column)
        scores = dot(keys, query_rows[cols, :], 1, 1)
        probs_grad = dot(values, grad_rows[cols, :], 1, 1)
        parts = [scores[s * BLOCK : (s + 1) * BLOCK, :] for s in range(count)]
        start = tuple(before_ref[row : row + 1, cols] for row in range(3))
        biases = [bias_ref[row : row + 1, cols] for row in range(count)]
        put_stage(parts, probs_grad, biases, start, column, powers_ref, probs_ref, stats_ref)


def late_kernel(slots, *refs):
    half, count = slots.half, len(slots.late)
    bias_ref, query_rows, grad_rows = refs[:3]
    stages = [refs[3:6], refs[6:9]]
    blocks = list(refs[9 : 9 + count])
    sib_own_ref = refs[9 + count]
    weights_ref, score_grad_ref, sib_out_ref, last_ref = refs[10 + count :]
    _, core = position()

    @pl.when(core == 0)
    def _():
        last_ref[...] = blocks[-1][...]

    @pl.when(core == 1)
    def _():
        last_ref[...] = sib_own_ref[...]

    blocks[-1] = last_ref
    keys, values = stacked(blocks, 0), stacked(blocks, 1)
    for column in range(FLAT // COLS):
        cols = tile_of(column)
        scores = dot(keys, query_rows[cols, :], 1, 1)
        probs_grad = dot(values, grad_rows[cols, :], 1, 1)
        parts = [scores[s * BLOCK : (s + 1) * BLOCK, :] for s in range(count)]
        start = tuple(stages[-1][2][row : row + 1, cols] for row in range(3))
        first = len(slots.middle)
        biases = [bias_ref[row : row + 1, cols] for row in range(first, first + count)]
        powers, top, total, mixed = absorb(parts, probs_grad, biases, *start)
        inverse = 1.0 / total
        delta = mixed * inverse

        def put(slot, weights, probs):
            rows = slots.rows(slot)
            weights_ref[rows, cols] = weights.astype(jnp.bfloat16)
            score_grad_ref[rows, cols] = (weights * (probs - delta)).astype(jnp.bfloat16)

        for (powers_ref, probs_ref, stats_ref), group in zip(stages, (["own"], slots.middle)):
            factor = jnp.exp2(stats_ref[0:1, cols] - top) * inverse
            for s, slot in enumerate(group):
                rows = slice(s * BLOCK, (s + 1) * BLOCK)
                put(slot, powers_ref[rows, cols] * factor, probs_ref[rows, cols])
        for s, slot in enumerate(slots.late):
            put(slot, powers[s] * inverse, probs_grad[s * BLOCK : (s + 1) * BLOCK, :])

    rows = slice(0, half * BLOCK)
    key_grad = dot(score_grad_ref[rows, :], query_rows[...], 1, 0) * SCALE
    value_grad = dot(weights_ref[rows, :], grad_rows[...], 1, 0)
    for k in range(half):
        rows = slice(k * BLOCK, (k + 1) * BLOCK)
        sib_out_ref[k, :BLOCK, :] = key_grad[rows, :].astype(jnp.bfloat16)
        sib_out_ref[k, BLOCK:, :] = value_grad[rows, :].astype(jnp.bfloat16)


def mine_kernel(slots, weights_ref, score_grad_ref, query_rows, grad_rows, mine_ref):
    half = slots.half
    rows = slice(half * BLOCK, slots.window * BLOCK)
    key_grad = dot(score_grad_ref[rows, :], query_rows[...], 1, 0) * SCALE
    value_grad = dot(weights_ref[rows, :], grad_rows[...], 1, 0)
    for k in range(half):
        rows = slice(k * BLOCK, (k + 1) * BLOCK)
        mine_ref[k, :BLOCK, :] = key_grad[rows, :]
        mine_ref[k, BLOCK:, :] = value_grad[rows, :]


def query_side_kernel(slots, *refs):
    weights_ref, score_grad_ref, sib_own_ref = refs[:3]
    blocks = list(refs[3 : 3 + slots.window])
    attended_ref, query_grad_ref, last_ref = refs[3 + slots.window :]
    _, core = position()
    at = slots.order.index("last")

    @pl.when(core == 0)
    def _():
        last_ref[...] = blocks[at][...]

    @pl.when(core == 1)
    def _():
        last_ref[...] = sib_own_ref[...]

    blocks[at] = last_ref
    attended_t = dot(stacked(blocks, 1), weights_ref[...], 0, 0)
    query_grad_t = dot(stacked(blocks, 0), score_grad_ref[...], 0, 0) * SCALE
    for h in range(HEADS):
        rows = slice(h * BLOCK, (h + 1) * BLOCK)
        attended_ref[:, rows] = attended_t[:, rows].T.astype(jnp.bfloat16)
        query_grad_ref[:, rows] = query_grad_t[:, rows].T.astype(jnp.bfloat16)


def merge_kernel(mine_ref, from_sib_ref, *sent_refs):
    for k, ref in enumerate(sent_refs[:-1]):
        ref[...] = (mine_ref[k + 1] + from_sib_ref[k].astype(jnp.float32)).astype(jnp.bfloat16)
    sent_refs[-1][...] = from_sib_ref[len(sent_refs) - 1]


def total_kernel(mine_ref, from_sib_ref, *refs):
    back, (key_ref, value_ref) = refs[:-2], refs[-2:]
    _, core = position()
    near = from_sib_ref[len(back) - 1].astype(jnp.float32)
    total = mine_ref[0] + jnp.where(core == 0, near, back[-1][...].astype(jnp.float32))
    for ref in back[:-1]:
        total = total + ref[...].astype(jnp.float32)
    key_ref[...] = total[:BLOCK].astype(jnp.bfloat16)
    value_ref[...] = total[BLOCK:].astype(jnp.bfloat16)


def in_vmem(array):
    return pltpu.with_memory_space_constraint(array, pltpu.VMEM)


def in_hbm(array):
    return pltpu.with_memory_space_constraint(array, pltpu.HBM)


def cost(blocks, products):
    flops = 2 * products * blocks * BLOCK * FLAT * HEAD_DIM
    return pl.CostEstimate(flops=flops, bytes_accessed=blocks * BLOCK * FLAT * 4, transcendentals=0)


def local(devices, queries, key_rows, value_rows, out_grad, doc_ids):
    window = lax.axis_size("kv")
    slots = Slots(window)
    half = slots.half
    bf16, f32 = jnp.bfloat16, jnp.float32
    shape = jax.ShapeDtypeStruct
    small = pltpu.CompilerParams(vmem_limit_bytes=window * MIB // 4)
    params = pltpu.CompilerParams(vmem_limit_bytes=window * MIB)

    def ahead(block, k):
        return lax.ppermute(block, AXES, [(i, (i + 2 * k) % devices) for i in range(devices)])

    def swapped(block):
        return lax.ppermute(block, AXES, [(i, i ^ 1) for i in range(devices)])

    own = pl.pallas_call(
        pair_kernel,
        out_shape=pltpu.VMEM((2 * BLOCK, HEAD_DIM), bf16),
        in_specs=[HBM, HBM],
        out_specs=VMEM,
        scratch_shapes=[pltpu.SemaphoreType.DMA((2,))],
        compiler_params=small,
        name="pair_up",
    )(in_hbm(key_rows), in_hbm(value_rows))
    lins = [ahead(own, k) for k in range(1, half + 1)]
    sib_own = swapped(own)

    def stage(blocks):
        return [
            pltpu.VMEM((blocks * BLOCK, FLAT), f32),
            pltpu.VMEM((blocks * BLOCK, FLAT), f32),
            pltpu.VMEM((8, FLAT), f32),
        ]

    query_rows, grad_rows, bias, *own_stage = pl.pallas_call(
        functools.partial(own_kernel, slots),
        out_shape=[pltpu.VMEM((FLAT, HEAD_DIM), bf16)] * 2 + [pltpu.VMEM((window, FLAT), f32)] + stage(1),
        in_specs=[HBM, HBM, HBM, VMEM],
        out_specs=[VMEM] * 6,
        scratch_shapes=[
            pltpu.SMEM(doc_ids.shape, jnp.int32),
            pltpu.SemaphoreType.DMA,
            pltpu.SemaphoreType.DMA((2, HEADS)),
        ],
        compiler_params=params,
        cost_estimate=cost(1, 2),
        name="own_scores",
    )(in_hbm(doc_ids), in_hbm(queries), in_hbm(out_grad), own)

    lins[0], own_stage[2] = lax.optimization_barrier((lins[0], own_stage[2]))
    sibs = [swapped(block) for block in lins[: half - 2]]
    held = {("lin", k): lins[k - 1] for k in range(1, half - 1)}
    middle = len(slots.middle)
    *middle_stage, = pl.pallas_call(
        functools.partial(middle_kernel, slots),
        out_shape=stage(middle),
        in_specs=[VMEM] * (4 + middle),
        out_specs=[VMEM] * 3,
        compiler_params=params,
        cost_estimate=cost(middle, 2),
        name="middle_scores",
    )(bias, query_rows, grad_rows, own_stage[2], *[held[slot] for slot in slots.middle])

    lins[half - 2], lins[half - 1], middle_stage[2] = lax.optimization_barrier(
        (lins[half - 2], lins[half - 1], middle_stage[2])
    )
    sibs += [swapped(block) for block in lins[half - 2 :]]
    held |= {"own": own, "last": sibs[-1]}
    for k in range(1, half):
        held["lin", k] = lins[k - 1]
        held["sib", k] = sibs[k - 1]

    weights, score_grad, sib_out = pl.pallas_call(
        functools.partial(late_kernel, slots),
        out_shape=[
            pltpu.VMEM((window * BLOCK, FLAT), bf16),
            pltpu.VMEM((window * BLOCK, FLAT), bf16),
            pltpu.VMEM((half, 2 * BLOCK, HEAD_DIM), bf16),
        ],
        in_specs=[VMEM] * (10 + len(slots.late)),
        out_specs=[VMEM] * 3,
        scratch_shapes=[pltpu.VMEM((2 * BLOCK, HEAD_DIM), bf16)],
        compiler_params=params,
        cost_estimate=cost(window, 3),
        name="late_scores",
    )(
        bias, query_rows, grad_rows, *own_stage, *middle_stage,
        *[held[slot] for slot in slots.late], sib_own,
    )
    from_sib = swapped(sib_out)

    mine = pl.pallas_call(
        functools.partial(mine_kernel, slots),
        out_shape=pltpu.VMEM((half, 2 * BLOCK, HEAD_DIM), f32),
        in_specs=[VMEM] * 4,
        out_specs=VMEM,
        compiler_params=params,
        cost_estimate=cost(half, 2),
        name="own_parity_grads",
    )(weights, score_grad, query_rows, grad_rows)

    attended, query_grad = pl.pallas_call(
        functools.partial(query_side_kernel, slots),
        out_shape=[shape(queries.shape, bf16), shape(queries.shape, bf16)],
        in_specs=[VMEM] * (3 + window),
        out_specs=[VMEM] * 2,
        scratch_shapes=[pltpu.VMEM((2 * BLOCK, HEAD_DIM), bf16)],
        compiler_params=params,
        cost_estimate=cost(window, 2),
        name="query_side",
    )(in_vmem(weights), in_vmem(score_grad), sib_own, *[held[slot] for slot in slots.order])

    sent = pl.pallas_call(
        merge_kernel,
        out_shape=[pltpu.VMEM((2 * BLOCK, HEAD_DIM), bf16)] * half,
        in_specs=[VMEM] * 2,
        out_specs=[VMEM] * half,
        compiler_params=small,
        name="merge_siblings",
    )(mine, from_sib)
    back = [ahead(block, -(k + 1)) for k, block in enumerate(sent)]
    key_grad, value_grad = pl.pallas_call(
        total_kernel,
        out_shape=[shape((BLOCK, HEAD_DIM), bf16)] * 2,
        in_specs=[VMEM] * (2 + half),
        out_specs=[VMEM] * 2,
        compiler_params=small,
        name="total_grads",
    )(mine, from_sib, *back)
    return attended, query_grad, key_grad, value_grad


def solution(mesh):
    split = P(AXES, None)
    devices = mesh.shape["pb"] * mesh.shape["kv"]
    return jax.shard_map(
        functools.partial(local, devices),
        mesh=mesh,
        in_specs=(split, split, split, split, P()),
        out_specs=(split, split, split, split),
        check_vma=False,
    )
```

```python
import functools
import math

import jax
import jax.numpy as jnp
from jax import lax
from jax.experimental import pallas as pl
from jax.experimental.pallas import tpu as pltpu
from jax.sharding import PartitionSpec as P

HEADS = 8
HEAD_DIM = 128
BLOCK = 128
FLAT = HEADS * BLOCK
AXES = ("pb", "kv")
SCALE = HEAD_DIM ** (-0.5)
SCALE_LOG2 = SCALE / math.log(2.0)
FAR = 1e30
COLS = 256
MIB = 2**20

VMEM = pl.BlockSpec(memory_space=pltpu.VMEM)
HBM = pl.BlockSpec(memory_space=pltpu.HBM)


def dot(left, right, left_dim, right_dim):
    return lax.dot_general(
        left, right, (((left_dim,), (right_dim,)), ((), ())), preferred_element_type=jnp.float32
    )


def rows_of(block):
    return slice(block * BLOCK, (block + 1) * BLOCK)


class Slots:
    def __init__(self, window):
        self.window = window
        self.half = half = window // 2
        lins = [("lin", k) for k in range(1, half)]
        sibs = [("sib", k) for k in range(1, half)]
        self.middle = lins[:-1]
        self.closing = sibs[:-1] + lins[-1:]
        self.late = [sibs[-1], "last"]
        self.stages = [["own"], self.middle, self.closing, self.late]
        self.sibs = sibs + ["last"]
        self.mine = ["own"] + lins

    def place(self, slot):
        for at, group in enumerate(self.stages):
            if slot in group:
                return at, rows_of(group.index(slot))

    def distance(self, slot, core):
        if slot == "last":
            return jnp.where(core == 0, self.window - 1, 1)
        return 2 * slot[1] if slot[0] == "lin" else 2 * slot[1] - 1 + 2 * core


def position():
    me = lax.axis_index("pb") * lax.axis_size("kv") + lax.axis_index("kv")
    return me, lax.rem(me, 2)


def reached(doc_ref, slots, slot):
    me, core = position()
    at = me - slots.distance(slot, core)
    return (at >= 0) & (doc_ref[jnp.maximum(at, 0)] == doc_ref[me])


def stacked(refs, part):
    return jnp.concatenate([ref[part * BLOCK : (part + 1) * BLOCK, :] for ref in refs], axis=0)


def tile_of(column):
    return slice(column * COLS, (column + 1) * COLS)


def absorb(parts, probs_grad, biases, top, total, mixed):
    new_top = top
    for part, bias in zip(parts, biases):
        new_top = jnp.maximum(new_top, jnp.max(part, axis=0, keepdims=True) * SCALE_LOG2 + bias)
    rescale = jnp.exp2(top - new_top)
    total, mixed = total * rescale, mixed * rescale
    powers = []
    for s, (part, bias) in enumerate(zip(parts, biases)):
        power = jnp.exp2(part * SCALE_LOG2 - (new_top - bias))
        powers.append(power)
        total = total + jnp.sum(power, axis=0, keepdims=True)
        mixed = mixed + jnp.sum(power * probs_grad[s * BLOCK : (s + 1) * BLOCK, :], axis=0, keepdims=True)
    return powers, new_top, total, mixed


def pair_kernel(key_ref, value_ref, pair_ref, sems):
    copies = [
        pltpu.make_async_copy(ref, pair_ref.at[part * BLOCK : (part + 1) * BLOCK, :], sems.at[part])
        for part, ref in enumerate((key_ref, value_ref))
    ]
    for copy in copies:
        copy.start()
    for copy in copies:
        copy.wait()


def own_kernel(
    slots, doc_hbm, query_ref, grad_ref, own_ref,
    query_rows, grad_rows, bias_ref, powers_ref, probs_ref, stats_ref, doc_ref, doc_sem, sems,
):
    copies = [pltpu.make_async_copy(doc_hbm, doc_ref, doc_sem)]
    for h in range(HEADS):
        rows = slice(h * BLOCK, (h + 1) * BLOCK)
        copies.append(pltpu.make_async_copy(query_ref.at[:, rows], query_rows.at[rows, :], sems.at[0, h]))
        copies.append(pltpu.make_async_copy(grad_ref.at[:, rows], grad_rows.at[rows, :], sems.at[1, h]))
    for copy in copies:
        copy.start()
    key_row = lax.broadcasted_iota(jnp.int32, (BLOCK, COLS), 0)
    token = lax.broadcasted_iota(jnp.int32, (BLOCK, COLS), 1) % BLOCK
    causal = key_row <= token
    for copy in copies:
        copy.wait()
    for row, slot in enumerate(slots.middle + slots.closing + slots.late):
        bias = jnp.where(reached(doc_ref, slots, slot), 0.0, -FAR)
        bias_ref[row : row + 1, :] = jnp.full((1, FLAT), bias, jnp.float32)
    for column in range(FLAT // COLS):
        cols = tile_of(column)
        scores = dot(own_ref[:BLOCK, :], query_rows[cols, :], 1, 1)
        probs_grad = dot(own_ref[BLOCK:, :], grad_rows[cols, :], 1, 1)
        scores = jnp.where(causal, scores, -FAR)
        start = jnp.full((1, COLS), -FAR, jnp.float32), jnp.zeros((1, COLS)), jnp.zeros((1, COLS))
        put_stage([scores], probs_grad, [0.0], start, column, powers_ref, probs_ref, stats_ref)


def put_stage(parts, probs_grad, biases, start, column, powers_ref, probs_ref, stats_ref):
    cols = tile_of(column)
    powers, top, total, mixed = absorb(parts, probs_grad, biases, *start)
    for s, power in enumerate(powers):
        powers_ref[s * BLOCK : (s + 1) * BLOCK, cols] = power
    probs_ref[:, cols] = probs_grad
    for row, value in enumerate((top, total, mixed)):
        stats_ref[row : row + 1, cols] = value


def stage_kernel(first, count, *refs):
    bias_ref, query_rows, grad_rows, before_ref = refs[:4]
    blocks = refs[4 : 4 + count]
    powers_ref, probs_ref, stats_ref = refs[4 + count :]
    keys, values = stacked(blocks, 0), stacked(blocks, 1)
    for column in range(FLAT // COLS):
        cols = tile_of(column)
        scores = dot(keys, query_rows[cols, :], 1, 1)
        probs_grad = dot(values, grad_rows[cols, :], 1, 1)
        parts = [scores[rows_of(s), :] for s in range(count)]
        start = tuple(before_ref[row : row + 1, cols] for row in range(3))
        biases = [bias_ref[row : row + 1, cols] for row in range(first, first + count)]
        put_stage(parts, probs_grad, biases, start, column, powers_ref, probs_ref, stats_ref)


def put_weights(slot_rows, cols, powers, factor, probs, delta, weights_ref, score_grad_ref):
    weights = powers * factor
    weights_ref[slot_rows, cols] = weights.astype(jnp.bfloat16)
    score_grad_ref[slot_rows, cols] = (weights * (probs - delta)).astype(jnp.bfloat16)


def put_grads(weights_ref, score_grad_ref, query_rows, grad_rows, out_ref):
    key_grad = dot(score_grad_ref[...], query_rows[...], 1, 0) * SCALE
    value_grad = dot(weights_ref[...], grad_rows[...], 1, 0)
    for k in range(out_ref.shape[0]):
        out_ref[k, :BLOCK, :] = key_grad[rows_of(k), :].astype(out_ref.dtype)
        out_ref[k, BLOCK:, :] = value_grad[rows_of(k), :].astype(out_ref.dtype)


def late_kernel(slots, *refs):
    count = len(slots.late)
    bias_ref, query_rows, grad_rows, powers_ref, probs_ref, before_ref = refs[:6]
    blocks = list(refs[6 : 6 + count])
    sib_own_ref = refs[6 + count]
    weights_ref, score_grad_ref, sib_out_ref, stats_ref, last_ref = refs[7 + count :]
    _, core = position()

    @pl.when(core == 0)
    def _():
        last_ref[...] = blocks[-1][...]

    @pl.when(core == 1)
    def _():
        last_ref[...] = sib_own_ref[...]

    blocks[-1] = last_ref
    keys, values = stacked(blocks, 0), stacked(blocks, 1)
    first = slots.window - 1 - count
    for column in range(FLAT // COLS):
        cols = tile_of(column)
        scores = dot(keys, query_rows[cols, :], 1, 1)
        probs_grad = dot(values, grad_rows[cols, :], 1, 1)
        parts = [scores[rows_of(s), :] for s in range(count)]
        start = tuple(before_ref[row : row + 1, cols] for row in range(3))
        biases = [bias_ref[row : row + 1, cols] for row in range(first, first + count)]
        powers, top, total, mixed = absorb(parts, probs_grad, biases, *start)
        inverse = 1.0 / total
        delta = mixed * inverse
        for row, value in enumerate((top, inverse, delta)):
            stats_ref[row : row + 1, cols] = value
        factor = jnp.exp2(start[0] - top) * inverse
        for s, slot in enumerate(slots.sibs):
            at, rows = slots.place(slot)
            if slot in slots.late:
                piece = powers[slots.late.index(slot)], inverse, probs_grad[rows, :]
            else:
                piece = powers_ref[rows, cols], factor, probs_ref[rows, cols]
            put_weights(rows_of(s), cols, *piece, delta, weights_ref, score_grad_ref)
    put_grads(weights_ref, score_grad_ref, query_rows, grad_rows, sib_out_ref)


def mine_kernel(slots, *refs):
    query_rows, grad_rows, final_ref = refs[:3]
    stages = [refs[3 + 3 * at : 6 + 3 * at] for at in range(3)]
    weights_ref, score_grad_ref, mine_ref = refs[12:]
    for column in range(FLAT // COLS):
        cols = tile_of(column)
        top, inverse, delta = (final_ref[row : row + 1, cols] for row in range(3))
        factors = [jnp.exp2(stats_ref[0:1, cols] - top) * inverse for _, _, stats_ref in stages]
        for s, slot in enumerate(slots.mine):
            at, rows = slots.place(slot)
            piece = stages[at][0][rows, cols], factors[at], stages[at][1][rows, cols]
            put_weights(rows_of(s), cols, *piece, delta, weights_ref, score_grad_ref)
    put_grads(weights_ref, score_grad_ref, query_rows, grad_rows, mine_ref)


def query_side_kernel(slots, *refs):
    sib_weights, sib_score_grad, mine_weights, mine_score_grad, sib_own_ref = refs[:5]
    blocks = list(refs[5 : 5 + slots.window])
    attended_ref, query_grad_ref, last_ref = refs[5 + slots.window :]
    _, core = position()
    half = slots.half

    @pl.when(core == 0)
    def _():
        last_ref[...] = blocks[half - 1][...]

    @pl.when(core == 1)
    def _():
        last_ref[...] = sib_own_ref[...]

    blocks[half - 1] = last_ref

    def mixed(part, sib_ref, mine_ref):
        sib = dot(stacked(blocks[:half], part), sib_ref[...], 0, 0)
        return sib + dot(stacked(blocks[half:], part), mine_ref[...], 0, 0)

    attended_t = mixed(1, sib_weights, mine_weights)
    query_grad_t = mixed(0, sib_score_grad, mine_score_grad) * SCALE
    for h in range(HEADS):
        rows = slice(h * BLOCK, (h + 1) * BLOCK)
        attended_ref[:, rows] = attended_t[:, rows].T.astype(jnp.bfloat16)
        query_grad_ref[:, rows] = query_grad_t[:, rows].T.astype(jnp.bfloat16)


def merge_kernel(mine_ref, from_sib_ref, *sent_refs):
    for k, ref in enumerate(sent_refs[:-1]):
        ref[...] = (mine_ref[k + 1] + from_sib_ref[k].astype(jnp.float32)).astype(jnp.bfloat16)
    sent_refs[-1][...] = from_sib_ref[len(sent_refs) - 1]


def total_kernel(mine_ref, from_sib_ref, *refs):
    back, (key_ref, value_ref) = refs[:-2], refs[-2:]
    _, core = position()
    near = from_sib_ref[len(back) - 1].astype(jnp.float32)
    total = mine_ref[0] + jnp.where(core == 0, near, back[-1][...].astype(jnp.float32))
    for ref in back[:-1]:
        total = total + ref[...].astype(jnp.float32)
    key_ref[...] = total[:BLOCK].astype(jnp.bfloat16)
    value_ref[...] = total[BLOCK:].astype(jnp.bfloat16)


def in_vmem(array):
    return pltpu.with_memory_space_constraint(array, pltpu.VMEM)


def in_hbm(array):
    return pltpu.with_memory_space_constraint(array, pltpu.HBM)


def cost(blocks, products):
    flops = 2 * products * blocks * BLOCK * FLAT * HEAD_DIM
    return pl.CostEstimate(flops=flops, bytes_accessed=blocks * BLOCK * FLAT * 4, transcendentals=0)


def local(devices, queries, key_rows, value_rows, out_grad, doc_ids):
    window = lax.axis_size("kv")
    slots = Slots(window)
    half = slots.half
    bf16, f32 = jnp.bfloat16, jnp.float32
    shape = jax.ShapeDtypeStruct
    small = pltpu.CompilerParams(vmem_limit_bytes=window * MIB // 4)
    params = pltpu.CompilerParams(vmem_limit_bytes=window * MIB)

    def ahead(block, k):
        return lax.ppermute(block, AXES, [(i, (i + 2 * k) % devices) for i in range(devices)])

    def ahead_odd(block, k, back=False):
        route = [(i, i + 2 * k if i + 2 * k < devices else i ^ 1) for i in range(1, devices, 2)]
        route += [(i, i - 2 * k if i >= 2 * k else i ^ 1) for i in range(0, devices, 2)]
        return lax.ppermute(block, AXES, [pair[::-1] for pair in route] if back else route)

    def swapped(block):
        return lax.ppermute(block, AXES, [(i, i ^ 1) for i in range(devices)])

    own = pl.pallas_call(
        pair_kernel,
        out_shape=pltpu.VMEM((2 * BLOCK, HEAD_DIM), bf16),
        in_specs=[HBM, HBM],
        out_specs=VMEM,
        scratch_shapes=[pltpu.SemaphoreType.DMA((2,))],
        compiler_params=small,
        name="pair_up",
    )(in_hbm(key_rows), in_hbm(value_rows))
    lins = [ahead(own, k) for k in range(1, half)] + [ahead_odd(own, half)]
    sib_own = swapped(own)

    def stage(blocks):
        return [
            pltpu.VMEM((blocks * BLOCK, FLAT), f32),
            pltpu.VMEM((blocks * BLOCK, FLAT), f32),
            pltpu.VMEM((8, FLAT), f32),
        ]

    query_rows, grad_rows, bias, *own_stage = pl.pallas_call(
        functools.partial(own_kernel, slots),
        out_shape=[pltpu.VMEM((FLAT, HEAD_DIM), bf16)] * 2 + [pltpu.VMEM((window, FLAT), f32)] + stage(1),
        in_specs=[HBM, HBM, HBM, VMEM],
        out_specs=[VMEM] * 6,
        scratch_shapes=[
            pltpu.SMEM(doc_ids.shape, jnp.int32),
            pltpu.SemaphoreType.DMA,
            pltpu.SemaphoreType.DMA((2, HEADS)),
        ],
        compiler_params=params,
        cost_estimate=cost(1, 2),
        name="own_scores",
    )(in_hbm(doc_ids), in_hbm(queries), in_hbm(out_grad), own)

    lins[0], own_stage[2] = lax.optimization_barrier((lins[0], own_stage[2]))
    sibs = [swapped(block) for block in lins[: half - 2]]
    held = {("lin", k): lins[k - 1] for k in range(1, half - 1)}

    def next_stage(at, before):
        group = slots.stages[at]
        first = sum(len(earlier) for earlier in slots.stages[1:at])
        return list(
            pl.pallas_call(
                functools.partial(stage_kernel, first, len(group)),
                out_shape=stage(len(group)),
                in_specs=[VMEM] * (4 + len(group)),
                out_specs=[VMEM] * 3,
                compiler_params=params,
                cost_estimate=cost(len(group), 2),
                name="stage_scores",
            )(bias, query_rows, grad_rows, before, *[held[slot] for slot in group])
        )

    middle_stage = next_stage(1, own_stage[2])
    lins[half - 2], lins[half - 1], middle_stage[2] = lax.optimization_barrier(
        (lins[half - 2], lins[half - 1], middle_stage[2])
    )
    sibs += [swapped(block) for block in lins[half - 2 :]]
    held |= {"own": own, "last": sibs[-1]}
    for k in range(1, half):
        held["lin", k] = lins[k - 1]
        held["sib", k] = sibs[k - 1]
    closing_stage = next_stage(2, middle_stage[2])

    weights = [pltpu.VMEM((half * BLOCK, FLAT), bf16)] * 2
    sib_weights, sib_score_grad, sib_out, final = pl.pallas_call(
        functools.partial(late_kernel, slots),
        out_shape=weights + [pltpu.VMEM((half, 2 * BLOCK, HEAD_DIM), bf16), pltpu.VMEM((8, FLAT), f32)],
        in_specs=[VMEM] * (7 + len(slots.late)),
        out_specs=[VMEM] * 4,
        scratch_shapes=[pltpu.VMEM((2 * BLOCK, HEAD_DIM), bf16)],
        compiler_params=params,
        cost_estimate=cost(window, 2),
        name="late_scores",
    )(bias, query_rows, grad_rows, *closing_stage, *[held[slot] for slot in slots.late], sib_own)
    from_sib = swapped(sib_out)

    mine_weights, mine_score_grad, mine = pl.pallas_call(
        functools.partial(mine_kernel, slots),
        out_shape=weights + [pltpu.VMEM((half, 2 * BLOCK, HEAD_DIM), f32)],
        in_specs=[VMEM] * 12,
        out_specs=[VMEM] * 3,
        compiler_params=params,
        cost_estimate=cost(half, 2),
        name="own_parity_grads",
    )(query_rows, grad_rows, final, *own_stage, *middle_stage, *closing_stage)

    attended, query_grad = pl.pallas_call(
        functools.partial(query_side_kernel, slots),
        out_shape=[shape(queries.shape, bf16), shape(queries.shape, bf16)],
        in_specs=[VMEM] * (5 + window),
        out_specs=[VMEM] * 2,
        scratch_shapes=[pltpu.VMEM((2 * BLOCK, HEAD_DIM), bf16)],
        compiler_params=params,
        cost_estimate=cost(window, 2),
        name="query_side",
    )(
        *[in_vmem(part) for part in (sib_weights, sib_score_grad, mine_weights, mine_score_grad)],
        sib_own, *[held[slot] for slot in slots.sibs + slots.mine],
    )

    sent = pl.pallas_call(
        merge_kernel,
        out_shape=[pltpu.VMEM((2 * BLOCK, HEAD_DIM), bf16)] * half,
        in_specs=[VMEM] * 2,
        out_specs=[VMEM] * half,
        compiler_params=small,
        name="merge_siblings",
    )(mine, from_sib)
    back = [ahead(block, -(k + 1)) for k, block in enumerate(sent)]
    key_grad, value_grad = pl.pallas_call(
        total_kernel,
        out_shape=[shape((BLOCK, HEAD_DIM), bf16)] * 2,
        in_specs=[VMEM] * (2 + half),
        out_specs=[VMEM] * 2,
        compiler_params=small,
        name="total_grads",
    )(mine, from_sib, *back)
    return attended, query_grad, key_grad, value_grad


def solution(mesh):
    split = P(AXES, None)
    devices = mesh.shape["pb"] * mesh.shape["kv"]
    return jax.shard_map(
        functools.partial(local, devices),
        mesh=mesh,
        in_specs=(split, split, split, split, P()),
        out_specs=(split, split, split, split),
        check_vma=False,
    )
```

```python
import functools
import math

import jax
import jax.numpy as jnp
from jax import lax
from jax.experimental import pallas as pl
from jax.experimental.pallas import tpu as pltpu
from jax.sharding import PartitionSpec as P

HEADS = 8
HEAD_DIM = 128
BLOCK = 128
FLAT = HEADS * BLOCK
AXES = ("pb", "kv")
SCALE = HEAD_DIM ** (-0.5)
SCALE_LOG2 = SCALE / math.log(2.0)
FAR = 1e30
COLS = 256
MIB = 2**20

VMEM = pl.BlockSpec(memory_space=pltpu.VMEM)
HBM = pl.BlockSpec(memory_space=pltpu.HBM)


def dot(left, right, left_dim, right_dim):
    return lax.dot_general(
        left, right, (((left_dim,), (right_dim,)), ((), ())), preferred_element_type=jnp.float32
    )


def rows_of(block):
    return slice(block * BLOCK, (block + 1) * BLOCK)


class Slots:
    def __init__(self, window):
        self.window = window
        self.half = half = window // 2
        self.arrival = list(range(1, half))
        lins = [("lin", k) for k in self.arrival]
        sibs = [("sib", k) for k in self.arrival]
        self.middle = lins[:-1]
        self.closing = sibs[:-1] + lins[-1:]
        self.late = [sibs[-1], "last"]
        self.stages = [["own"], self.middle, self.closing, self.late]
        self.sibs = [("sib", k) for k in range(1, half)] + ["last"]
        self.mine = ["own"] + [("lin", k) for k in range(1, half)]

    def place(self, slot):
        for at, group in enumerate(self.stages):
            if slot in group:
                return at, rows_of(group.index(slot))

    def distance(self, slot):
        _, chip, core = position()
        if slot == "last":
            return jnp.where(core == 0, self.window - 1, 1)
        kind, m = slot
        chips = lax.rem(chip - lax.bitwise_xor(chip, m) + self.half, self.half)
        return 2 * chips if kind == "lin" else 2 * chips - 1 + 2 * core


def position():
    column = lax.axis_index("kv")
    return lax.axis_index("pb") * lax.axis_size("kv") + column, column // 2, lax.rem(column, 2)


def reached(doc_ref, slots, slot):
    me, _, _ = position()
    at = me - slots.distance(slot)
    return (at >= 0) & (doc_ref[jnp.maximum(at, 0)] == doc_ref[me])


def stacked(refs, part):
    return jnp.concatenate([ref[part * BLOCK : (part + 1) * BLOCK, :] for ref in refs], axis=0)


def tile_of(column):
    return slice(column * COLS, (column + 1) * COLS)


def absorb(parts, probs_grad, biases, top, total, mixed):
    new_top = top
    for part, bias in zip(parts, biases):
        new_top = jnp.maximum(new_top, jnp.max(part, axis=0, keepdims=True) * SCALE_LOG2 + bias)
    rescale = jnp.exp2(top - new_top)
    total, mixed = total * rescale, mixed * rescale
    powers = []
    for s, (part, bias) in enumerate(zip(parts, biases)):
        power = jnp.exp2(part * SCALE_LOG2 - (new_top - bias))
        powers.append(power)
        total = total + jnp.sum(power, axis=0, keepdims=True)
        mixed = mixed + jnp.sum(power * probs_grad[s * BLOCK : (s + 1) * BLOCK, :], axis=0, keepdims=True)
    return powers, new_top, total, mixed


def pair_kernel(key_ref, value_ref, pair_ref, sems):
    copies = [
        pltpu.make_async_copy(ref, pair_ref.at[part * BLOCK : (part + 1) * BLOCK, :], sems.at[part])
        for part, ref in enumerate((key_ref, value_ref))
    ]
    for copy in copies:
        copy.start()
    for copy in copies:
        copy.wait()


def own_kernel(
    slots, doc_hbm, query_ref, grad_ref, own_ref,
    query_rows, grad_rows, bias_ref, powers_ref, probs_ref, stats_ref, doc_ref, doc_sem, sems,
):
    copies = [pltpu.make_async_copy(doc_hbm, doc_ref, doc_sem)]
    for h in range(HEADS):
        rows = slice(h * BLOCK, (h + 1) * BLOCK)
        copies.append(pltpu.make_async_copy(query_ref.at[:, rows], query_rows.at[rows, :], sems.at[0, h]))
        copies.append(pltpu.make_async_copy(grad_ref.at[:, rows], grad_rows.at[rows, :], sems.at[1, h]))
    for copy in copies:
        copy.start()
    key_row = lax.broadcasted_iota(jnp.int32, (BLOCK, COLS), 0)
    token = lax.broadcasted_iota(jnp.int32, (BLOCK, COLS), 1) % BLOCK
    causal = key_row <= token
    for copy in copies:
        copy.wait()
    for row, slot in enumerate(slots.middle + slots.closing + slots.late):
        bias = jnp.where(reached(doc_ref, slots, slot), 0.0, -FAR)
        bias_ref[row : row + 1, :] = jnp.full((1, FLAT), bias, jnp.float32)
    for column in range(FLAT // COLS):
        cols = tile_of(column)
        scores = dot(own_ref[:BLOCK, :], query_rows[cols, :], 1, 1)
        probs_grad = dot(own_ref[BLOCK:, :], grad_rows[cols, :], 1, 1)
        scores = jnp.where(causal, scores, -FAR)
        start = jnp.full((1, COLS), -FAR, jnp.float32), jnp.zeros((1, COLS)), jnp.zeros((1, COLS))
        put_stage([scores], probs_grad, [0.0], start, column, powers_ref, probs_ref, stats_ref)


def put_stage(parts, probs_grad, biases, start, column, powers_ref, probs_ref, stats_ref):
    cols = tile_of(column)
    powers, top, total, mixed = absorb(parts, probs_grad, biases, *start)
    for s, power in enumerate(powers):
        powers_ref[s * BLOCK : (s + 1) * BLOCK, cols] = power
    probs_ref[:, cols] = probs_grad
    for row, value in enumerate((top, total, mixed)):
        stats_ref[row : row + 1, cols] = value


def stage_kernel(first, count, *refs):
    bias_ref, query_rows, grad_rows, before_ref = refs[:4]
    blocks = refs[4 : 4 + count]
    powers_ref, probs_ref, stats_ref = refs[4 + count :]
    keys, values = stacked(blocks, 0), stacked(blocks, 1)
    for column in range(FLAT // COLS):
        cols = tile_of(column)
        scores = dot(keys, query_rows[cols, :], 1, 1)
        probs_grad = dot(values, grad_rows[cols, :], 1, 1)
        parts = [scores[rows_of(s), :] for s in range(count)]
        start = tuple(before_ref[row : row + 1, cols] for row in range(3))
        biases = [bias_ref[row : row + 1, cols] for row in range(first, first + count)]
        put_stage(parts, probs_grad, biases, start, column, powers_ref, probs_ref, stats_ref)


def put_weights(slot_rows, cols, powers, factor, probs, delta, weights_ref, score_grad_ref):
    weights = powers * factor
    weights_ref[slot_rows, cols] = weights.astype(jnp.bfloat16)
    score_grad_ref[slot_rows, cols] = (weights * (probs - delta)).astype(jnp.bfloat16)


def put_grads(weights_ref, score_grad_ref, query_rows, grad_rows, out_ref):
    key_grad = dot(score_grad_ref[...], query_rows[...], 1, 0) * SCALE
    value_grad = dot(weights_ref[...], grad_rows[...], 1, 0)
    for k in range(out_ref.shape[0]):
        out_ref[k, :BLOCK, :] = key_grad[rows_of(k), :].astype(out_ref.dtype)
        out_ref[k, BLOCK:, :] = value_grad[rows_of(k), :].astype(out_ref.dtype)


def late_kernel(slots, *refs):
    count = len(slots.late)
    bias_ref, query_rows, grad_rows, powers_ref, probs_ref, before_ref = refs[:6]
    blocks = list(refs[6 : 6 + count])
    sib_own_ref = refs[6 + count]
    weights_ref, score_grad_ref, sib_out_ref, stats_ref, last_ref = refs[7 + count :]
    _, _, core = position()

    @pl.when(core == 0)
    def _():
        last_ref[...] = blocks[-1][...]

    @pl.when(core == 1)
    def _():
        last_ref[...] = sib_own_ref[...]

    blocks[-1] = last_ref
    keys, values = stacked(blocks, 0), stacked(blocks, 1)
    first = slots.window - 1 - count
    for column in range(FLAT // COLS):
        cols = tile_of(column)
        scores = dot(keys, query_rows[cols, :], 1, 1)
        probs_grad = dot(values, grad_rows[cols, :], 1, 1)
        parts = [scores[rows_of(s), :] for s in range(count)]
        start = tuple(before_ref[row : row + 1, cols] for row in range(3))
        biases = [bias_ref[row : row + 1, cols] for row in range(first, first + count)]
        powers, top, total, mixed = absorb(parts, probs_grad, biases, *start)
        inverse = 1.0 / total
        delta = mixed * inverse
        for row, value in enumerate((top, inverse, delta)):
            stats_ref[row : row + 1, cols] = value
        factor = jnp.exp2(start[0] - top) * inverse
        for s, slot in enumerate(slots.sibs):
            at, rows = slots.place(slot)
            if slot in slots.late:
                piece = powers[slots.late.index(slot)], inverse, probs_grad[rows, :]
            else:
                piece = powers_ref[rows, cols], factor, probs_ref[rows, cols]
            put_weights(rows_of(s), cols, *piece, delta, weights_ref, score_grad_ref)
    put_grads(weights_ref, score_grad_ref, query_rows, grad_rows, sib_out_ref)


def mine_kernel(slots, *refs):
    query_rows, grad_rows, final_ref = refs[:3]
    stages = [refs[3 + 3 * at : 6 + 3 * at] for at in range(3)]
    weights_ref, score_grad_ref, mine_ref = refs[12:]
    for column in range(FLAT // COLS):
        cols = tile_of(column)
        top, inverse, delta = (final_ref[row : row + 1, cols] for row in range(3))
        factors = [jnp.exp2(stats_ref[0:1, cols] - top) * inverse for _, _, stats_ref in stages]
        for s, slot in enumerate(slots.mine):
            at, rows = slots.place(slot)
            piece = stages[at][0][rows, cols], factors[at], stages[at][1][rows, cols]
            put_weights(rows_of(s), cols, *piece, delta, weights_ref, score_grad_ref)
    put_grads(weights_ref, score_grad_ref, query_rows, grad_rows, mine_ref)


def query_side_kernel(slots, *refs):
    sib_weights, sib_score_grad, mine_weights, mine_score_grad, sib_own_ref = refs[:5]
    blocks = list(refs[5 : 5 + slots.window])
    attended_ref, query_grad_ref, last_ref = refs[5 + slots.window :]
    _, _, core = position()
    half = slots.half

    @pl.when(core == 0)
    def _():
        last_ref[...] = blocks[half - 1][...]

    @pl.when(core == 1)
    def _():
        last_ref[...] = sib_own_ref[...]

    blocks[half - 1] = last_ref

    def mixed(part, sib_ref, mine_ref):
        sib = dot(stacked(blocks[:half], part), sib_ref[...], 0, 0)
        return sib + dot(stacked(blocks[half:], part), mine_ref[...], 0, 0)

    attended_t = mixed(1, sib_weights, mine_weights)
    query_grad_t = mixed(0, sib_score_grad, mine_score_grad) * SCALE
    for h in range(HEADS):
        rows = slice(h * BLOCK, (h + 1) * BLOCK)
        attended_ref[:, rows] = attended_t[:, rows].T.astype(jnp.bfloat16)
        query_grad_ref[:, rows] = query_grad_t[:, rows].T.astype(jnp.bfloat16)


def merge_kernel(mine_ref, from_sib_ref, *sent_refs):
    for k, ref in enumerate(sent_refs[:-1]):
        ref[...] = (mine_ref[k + 1] + from_sib_ref[k].astype(jnp.float32)).astype(jnp.bfloat16)
    _, _, core = position()
    far = from_sib_ref[len(sent_refs) - 1]
    sent_refs[-1][...] = jnp.where(core == 1, far, jnp.zeros_like(far))


def total_kernel(order, mine_ref, from_sib_ref, *refs):
    back, (key_ref, value_ref) = refs[:-2], refs[-2:]
    _, _, core = position()
    half = len(order)
    near = from_sib_ref[half - 1].astype(jnp.float32)
    total = mine_ref[0] + jnp.where(core == 0, near, back[order.index(half)][...].astype(jnp.float32))
    for k, ref in zip(order, back):
        if k < half:
            total = total + ref[...].astype(jnp.float32)
    key_ref[...] = total[:BLOCK].astype(jnp.bfloat16)
    value_ref[...] = total[BLOCK:].astype(jnp.bfloat16)


def in_vmem(array):
    return pltpu.with_memory_space_constraint(array, pltpu.VMEM)


def in_hbm(array):
    return pltpu.with_memory_space_constraint(array, pltpu.HBM)


def cost(blocks, products):
    flops = 2 * products * blocks * BLOCK * FLAT * HEAD_DIM
    return pl.CostEstimate(flops=flops, bytes_accessed=blocks * BLOCK * FLAT * 4, transcendentals=0)


def local(devices, queries, key_rows, value_rows, out_grad, doc_ids):
    window = lax.axis_size("kv")
    slots = Slots(window)
    half = slots.half
    bf16, f32 = jnp.bfloat16, jnp.float32
    shape = jax.ShapeDtypeStruct
    small = pltpu.CompilerParams(vmem_limit_bytes=window * MIB // 4)
    params = pltpu.CompilerParams(vmem_limit_bytes=window * MIB)

    def ahead(block, m, back=False):
        top = 1 << (m.bit_length() - 1)
        route = []
        for i in range(devices):
            run, chip, core = i // window, i // 2 % half, i % 2
            run, to = (run, chip ^ m) if not chip & top else (run + 1, chip ^ m)
            if run * window == devices:
                run, to = 0, chip ^ top
            route.append((i, run * window + 2 * to + core))
        return lax.ppermute(block, AXES, [pair[::-1] for pair in route] if back else route)

    def ahead_odd(block, k, back=False):
        route = [(i, i + 2 * k if i + 2 * k < devices else i ^ 1) for i in range(1, devices, 2)]
        route += [(i, i - 2 * k if i >= 2 * k else i ^ 1) for i in range(0, devices, 2)]
        return lax.ppermute(block, AXES, [pair[::-1] for pair in route] if back else route)

    def swapped(block):
        return lax.ppermute(block, AXES, [(i, i ^ 1) for i in range(devices)])

    own = pl.pallas_call(
        pair_kernel,
        out_shape=pltpu.VMEM((2 * BLOCK, HEAD_DIM), bf16),
        in_specs=[HBM, HBM],
        out_specs=VMEM,
        scratch_shapes=[pltpu.SemaphoreType.DMA((2,))],
        compiler_params=small,
        name="pair_up",
    )(in_hbm(key_rows), in_hbm(value_rows))
    lins = [ahead(own, k) for k in slots.arrival] + [ahead_odd(own, half)]
    sib_own = swapped(own)

    def stage(blocks):
        return [
            pltpu.VMEM((blocks * BLOCK, FLAT), f32),
            pltpu.VMEM((blocks * BLOCK, FLAT), f32),
            pltpu.VMEM((8, FLAT), f32),
        ]

    query_rows, grad_rows, bias, *own_stage = pl.pallas_call(
        functools.partial(own_kernel, slots),
        out_shape=[pltpu.VMEM((FLAT, HEAD_DIM), bf16)] * 2 + [pltpu.VMEM((window, FLAT), f32)] + stage(1),
        in_specs=[HBM, HBM, HBM, VMEM],
        out_specs=[VMEM] * 6,
        scratch_shapes=[
            pltpu.SMEM(doc_ids.shape, jnp.int32),
            pltpu.SemaphoreType.DMA,
            pltpu.SemaphoreType.DMA((2, HEADS)),
        ],
        compiler_params=params,
        cost_estimate=cost(1, 2),
        name="own_scores",
    )(in_hbm(doc_ids), in_hbm(queries), in_hbm(out_grad), own)

    lins[0], own_stage[2] = lax.optimization_barrier((lins[0], own_stage[2]))
    sibs = [swapped(block) for block in lins[: half - 2]]
    held = {("lin", k): block for k, block in zip(slots.arrival[:-1], lins)}

    def next_stage(at, before):
        group = slots.stages[at]
        first = sum(len(earlier) for earlier in slots.stages[1:at])
        return list(
            pl.pallas_call(
                functools.partial(stage_kernel, first, len(group)),
                out_shape=stage(len(group)),
                in_specs=[VMEM] * (4 + len(group)),
                out_specs=[VMEM] * 3,
                compiler_params=params,
                cost_estimate=cost(len(group), 2),
                name="stage_scores",
            )(bias, query_rows, grad_rows, before, *[held[slot] for slot in group])
        )

    middle_stage = next_stage(1, own_stage[2])
    lins[half - 1], lins[half - 2], middle_stage[2] = lax.optimization_barrier(
        (lins[half - 1], lins[half - 2], middle_stage[2])
    )
    sibs += [swapped(block) for block in lins[half - 2 :]]
    held |= {"own": own, "last": sibs[-1]}
    for k, block, swap in zip(slots.arrival, lins, sibs):
        held["lin", k] = block
        held["sib", k] = swap
    closing_stage = next_stage(2, middle_stage[2])

    weights = [pltpu.VMEM((half * BLOCK, FLAT), bf16)] * 2
    sib_weights, sib_score_grad, sib_out, final = pl.pallas_call(
        functools.partial(late_kernel, slots),
        out_shape=weights + [pltpu.VMEM((half, 2 * BLOCK, HEAD_DIM), bf16), pltpu.VMEM((8, FLAT), f32)],
        in_specs=[VMEM] * (7 + len(slots.late)),
        out_specs=[VMEM] * 4,
        scratch_shapes=[pltpu.VMEM((2 * BLOCK, HEAD_DIM), bf16)],
        compiler_params=params,
        cost_estimate=cost(window, 2),
        name="late_scores",
    )(bias, query_rows, grad_rows, *closing_stage, *[held[slot] for slot in slots.late], sib_own)
    from_sib = swapped(sib_out)

    mine_weights, mine_score_grad, mine = pl.pallas_call(
        functools.partial(mine_kernel, slots),
        out_shape=weights + [pltpu.VMEM((half, 2 * BLOCK, HEAD_DIM), f32)],
        in_specs=[VMEM] * 12,
        out_specs=[VMEM] * 3,
        compiler_params=params,
        cost_estimate=cost(half, 2),
        name="own_parity_grads",
    )(query_rows, grad_rows, final, *own_stage, *middle_stage, *closing_stage)

    attended, query_grad = pl.pallas_call(
        functools.partial(query_side_kernel, slots),
        out_shape=[shape(queries.shape, bf16), shape(queries.shape, bf16)],
        in_specs=[VMEM] * (5 + window),
        out_specs=[VMEM] * 2,
        scratch_shapes=[pltpu.VMEM((2 * BLOCK, HEAD_DIM), bf16)],
        compiler_params=params,
        cost_estimate=cost(window, 2),
        name="query_side",
    )(
        *[in_vmem(part) for part in (sib_weights, sib_score_grad, mine_weights, mine_score_grad)],
        sib_own, *[held[slot] for slot in slots.sibs + slots.mine],
    )

    sent = pl.pallas_call(
        merge_kernel,
        out_shape=[pltpu.VMEM((2 * BLOCK, HEAD_DIM), bf16)] * half,
        in_specs=[VMEM] * 2,
        out_specs=[VMEM] * half,
        compiler_params=small,
        name="merge_siblings",
    )(mine, from_sib)
    order = list(range(half, 0, -1))[1:] + [half]
    back = [
        ahead(sent[k - 1], k, back=True) if k < half else ahead_odd(sent[k - 1], half, back=True) for k in order
    ]
    key_grad, value_grad = pl.pallas_call(
        functools.partial(total_kernel, order),
        out_shape=[shape((BLOCK, HEAD_DIM), bf16)] * 2,
        in_specs=[VMEM] * (2 + half),
        out_specs=[VMEM] * 2,
        compiler_params=small,
        name="total_grads",
    )(mine, from_sib, *back)
    return attended, query_grad, key_grad, value_grad


def solution(mesh):
    split = P(AXES, None)
    devices = mesh.shape["pb"] * mesh.shape["kv"]
    return jax.shard_map(
        functools.partial(local, devices),
        mesh=mesh,
        in_specs=(split, split, split, split, P()),
        out_specs=(split, split, split, split),
        check_vma=False,
    )
```

```python
import functools
import math

import jax
import jax.numpy as jnp
from jax import lax
from jax.experimental import pallas as pl
from jax.experimental.pallas import tpu as pltpu
from jax.sharding import PartitionSpec as P

HEADS = 8
HEAD_DIM = 128
BLOCK = 128
FLAT = HEADS * BLOCK
AXES = ("pb", "kv")
SCALE = HEAD_DIM ** (-0.5)
SCALE_LOG2 = SCALE / math.log(2.0)
FAR = 1e30
COLS = 256
MIB = 2**20

VMEM = pl.BlockSpec(memory_space=pltpu.VMEM)
HBM = pl.BlockSpec(memory_space=pltpu.HBM)


def dot(left, right, left_dim, right_dim):
    return lax.dot_general(
        left, right, (((left_dim,), (right_dim,)), ((), ())), preferred_element_type=jnp.float32
    )


def rows_of(block):
    return slice(block * BLOCK, (block + 1) * BLOCK)


class Slots:
    def __init__(self, window):
        self.window = window
        self.half = half = window // 2
        self.arrival = list(range(1, half))
        lins = [("lin", k) for k in self.arrival]
        sibs = [("sib", k) for k in self.arrival]
        self.middle = lins[:-1]
        self.closing = sibs[:-1] + lins[-1:]
        self.late = [sibs[-1], "last"]
        self.stages = [["own"], self.middle, self.closing, self.late]
        self.swapped = self.closing[:-1] + ["swap"] + self.closing[-1:]
        self.mine = ["own"] + self.middle + ["keep"]

    def place(self, slot):
        for at, group in enumerate([*self.stages[:-1], ["keep"]]):
            if slot in group:
                return at, rows_of(group.index(slot))

    def distance(self, slot):
        _, chip, core = position()
        if slot == "last":
            return jnp.where(core == 0, self.window - 1, 1)
        kind, m = slot
        chips = lax.rem(chip - lax.bitwise_xor(chip, m) + self.half, self.half)
        return 2 * chips if kind == "lin" else 2 * chips - 1 + 2 * core


def position():
    column = lax.axis_index("kv")
    return lax.axis_index("pb") * lax.axis_size("kv") + column, column // 2, lax.rem(column, 2)


def reached(doc_ref, slots, slot):
    me, _, _ = position()
    at = me - slots.distance(slot)
    return (at >= 0) & (doc_ref[jnp.maximum(at, 0)] == doc_ref[me])


def stacked(refs, part):
    return jnp.concatenate([ref[part * BLOCK : (part + 1) * BLOCK, :] for ref in refs], axis=0)


def tile_of(column):
    return slice(column * COLS, (column + 1) * COLS)


def absorb(parts, probs_grad, biases, top, total, mixed):
    new_top = top
    for part, bias in zip(parts, biases):
        new_top = jnp.maximum(new_top, jnp.max(part, axis=0, keepdims=True) * SCALE_LOG2 + bias)
    rescale = jnp.exp2(top - new_top)
    total, mixed = total * rescale, mixed * rescale
    powers = []
    for s, (part, bias) in enumerate(zip(parts, biases)):
        power = jnp.exp2(part * SCALE_LOG2 - (new_top - bias))
        powers.append(power)
        total = total + jnp.sum(power, axis=0, keepdims=True)
        mixed = mixed + jnp.sum(power * probs_grad[s * BLOCK : (s + 1) * BLOCK, :], axis=0, keepdims=True)
    return powers, new_top, total, mixed


def pair_kernel(key_ref, value_ref, pair_ref, sems):
    copies = [
        pltpu.make_async_copy(ref, pair_ref.at[part * BLOCK : (part + 1) * BLOCK, :], sems.at[part])
        for part, ref in enumerate((key_ref, value_ref))
    ]
    for copy in copies:
        copy.start()
    for copy in copies:
        copy.wait()


def own_kernel(
    slots, doc_hbm, query_ref, grad_ref, own_ref,
    query_rows, grad_rows, bias_ref, powers_ref, probs_ref, stats_ref, doc_ref, doc_sem, sems,
):
    copies = [pltpu.make_async_copy(doc_hbm, doc_ref, doc_sem)]
    for h in range(HEADS):
        rows = slice(h * BLOCK, (h + 1) * BLOCK)
        copies.append(pltpu.make_async_copy(query_ref.at[:, rows], query_rows.at[rows, :], sems.at[0, h]))
        copies.append(pltpu.make_async_copy(grad_ref.at[:, rows], grad_rows.at[rows, :], sems.at[1, h]))
    for copy in copies:
        copy.start()
    key_row = lax.broadcasted_iota(jnp.int32, (BLOCK, COLS), 0)
    token = lax.broadcasted_iota(jnp.int32, (BLOCK, COLS), 1) % BLOCK
    causal = key_row <= token
    for copy in copies:
        copy.wait()
    for row, slot in enumerate(slots.middle + slots.closing + slots.late):
        bias = jnp.where(reached(doc_ref, slots, slot), 0.0, -FAR)
        bias_ref[row : row + 1, :] = jnp.full((1, FLAT), bias, jnp.float32)
    for column in range(FLAT // COLS):
        cols = tile_of(column)
        scores = dot(own_ref[:BLOCK, :], query_rows[cols, :], 1, 1)
        probs_grad = dot(own_ref[BLOCK:, :], grad_rows[cols, :], 1, 1)
        scores = jnp.where(causal, scores, -FAR)
        start = jnp.full((1, COLS), -FAR, jnp.float32), jnp.zeros((1, COLS)), jnp.zeros((1, COLS))
        put_stage([scores], probs_grad, [0.0], start, column, powers_ref, probs_ref, stats_ref)


def put_stage(parts, probs_grad, biases, start, column, powers_ref, probs_ref, stats_ref):
    cols = tile_of(column)
    powers, top, total, mixed = absorb(parts, probs_grad, biases, *start)
    for s, power in enumerate(powers):
        powers_ref[s * BLOCK : (s + 1) * BLOCK, cols] = power
    probs_ref[:, cols] = probs_grad
    for row, value in enumerate((top, total, mixed)):
        stats_ref[row : row + 1, cols] = value


def stage_kernel(first, count, *refs):
    bias_ref, query_rows, grad_rows, before_ref = refs[:4]
    blocks = refs[4 : 4 + count]
    powers_ref, probs_ref, stats_ref = refs[4 + count :]
    keys, values = stacked(blocks, 0), stacked(blocks, 1)
    for column in range(FLAT // COLS):
        cols = tile_of(column)
        scores = dot(keys, query_rows[cols, :], 1, 1)
        probs_grad = dot(values, grad_rows[cols, :], 1, 1)
        parts = [scores[rows_of(s), :] for s in range(count)]
        start = tuple(before_ref[row : row + 1, cols] for row in range(3))
        biases = [bias_ref[row : row + 1, cols] for row in range(first, first + count)]
        put_stage(parts, probs_grad, biases, start, column, powers_ref, probs_ref, stats_ref)


def put_weights(slot_rows, cols, powers, factor, probs, delta, weights_ref, score_grad_ref):
    weights = powers * factor
    weights_ref[slot_rows, cols] = weights.astype(jnp.bfloat16)
    score_grad_ref[slot_rows, cols] = (weights * (probs - delta)).astype(jnp.bfloat16)


def put_grads(weights_ref, score_grad_ref, query_rows, grad_rows, out_ref):
    key_grad = dot(score_grad_ref[...], query_rows[...], 1, 0) * SCALE
    value_grad = dot(weights_ref[...], grad_rows[...], 1, 0)
    for k in range(out_ref.shape[0]):
        out_ref[k, :BLOCK, :] = key_grad[rows_of(k), :].astype(out_ref.dtype)
        out_ref[k, BLOCK:, :] = value_grad[rows_of(k), :].astype(out_ref.dtype)


def put_either(core, even, odd, ref):
    @pl.when(core == 0)
    def _():
        ref[...] = even[...]

    @pl.when(core == 1)
    def _():
        ref[...] = odd[...]


def late_kernel(slots, *refs):
    bias_ref, query_rows, grad_rows, powers_ref, probs_ref, before_ref = refs[:6]
    sib_ref, far_ref, sib_own_ref = refs[6:9]
    keep_powers, keep_probs, final_ref, weights_ref, score_grad_ref, swap_ref, lin_ref, last_ref = refs[9:]
    _, _, core = position()
    even = core == 0
    half = slots.half
    put_either(core, far_ref, sib_own_ref, last_ref)
    blocks = [sib_ref, last_ref]
    keys, values = stacked(blocks, 0), stacked(blocks, 1)
    first = slots.window - 1 - len(blocks)
    for column in range(FLAT // COLS):
        cols = tile_of(column)
        scores = dot(keys, query_rows[cols, :], 1, 1)
        probs_grad = dot(values, grad_rows[cols, :], 1, 1)
        parts = [scores[rows_of(s), :] for s in range(2)]
        start = tuple(before_ref[row : row + 1, cols] for row in range(3))
        biases = [bias_ref[row : row + 1, cols] for row in range(first, first + 2)]
        powers, top, total, mixed = absorb(parts, probs_grad, biases, *start)
        inverse = 1.0 / total
        delta = mixed * inverse
        for row, value in enumerate((top, inverse, delta)):
            final_ref[row : row + 1, cols] = value
        sib_probs, last_probs = probs_grad[rows_of(0), :], probs_grad[rows_of(1), :]
        keep_powers[:, cols] = jnp.where(even, powers[0], powers[1])
        keep_probs[:, cols] = jnp.where(even, sib_probs, last_probs)
        factor = jnp.exp2(start[0] - top) * inverse
        for s, slot in enumerate(slots.swapped):
            if slot == "swap":
                piece = jnp.where(even, powers[1], powers[0]), inverse, jnp.where(even, last_probs, sib_probs)
            else:
                _, rows = slots.place(slot)
                piece = powers_ref[rows, cols], factor, probs_ref[rows, cols]
            put_weights(rows_of(s), cols, *piece, delta, weights_ref, score_grad_ref)
    key_grad = dot(score_grad_ref[...], query_rows[...], 1, 0) * SCALE
    value_grad = dot(weights_ref[...], grad_rows[...], 1, 0)
    for k in range(half):
        swap_ref[k, :BLOCK, :] = key_grad[rows_of(k), :].astype(jnp.bfloat16)
        swap_ref[k, BLOCK:, :] = value_grad[rows_of(k), :].astype(jnp.bfloat16)
    lin_ref[:BLOCK, :] = key_grad[rows_of(half - 1), :]
    lin_ref[BLOCK:, :] = value_grad[rows_of(half - 1), :]


def mine_kernel(slots, *refs):
    query_rows, grad_rows, final_ref = refs[:3]
    stages = {0: refs[3:6], 1: refs[6:9], 3: (*refs[9:11], final_ref)}
    weights_ref, score_grad_ref, mine_ref = refs[11:]
    for column in range(FLAT // COLS):
        cols = tile_of(column)
        top, inverse, delta = (final_ref[row : row + 1, cols] for row in range(3))
        for s, slot in enumerate(slots.mine):
            at, rows = slots.place(slot)
            powers_ref, probs_ref, stats_ref = stages[at]
            factor = jnp.exp2(stats_ref[0:1, cols] - top) * inverse
            piece = powers_ref[rows, cols], factor, probs_ref[rows, cols]
            put_weights(rows_of(s), cols, *piece, delta, weights_ref, score_grad_ref)
    key_grad = dot(score_grad_ref[...], query_rows[...], 1, 0) * SCALE
    value_grad = dot(weights_ref[...], grad_rows[...], 1, 0)
    for k in range(slots.half):
        mine_ref[k, :BLOCK, :] = key_grad[rows_of(k), :]
        mine_ref[k, BLOCK:, :] = value_grad[rows_of(k), :]


def query_side_kernel(slots, *refs):
    half = slots.half
    swap_weights, swap_score_grad, mine_weights, mine_score_grad = refs[:4]
    swapped, mine = list(refs[4 : 3 + half]), list(refs[3 + half : 2 + 2 * half])
    sib_ref, far_ref, sib_own_ref, attended_out, query_grad_out = refs[2 + 2 * half : 7 + 2 * half]
    swap_ref, keep_ref, attended_ref, query_grad_ref, sems = refs[7 + 2 * half :]
    _, _, core = position()
    put_either(core, far_ref, sib_ref, swap_ref)
    put_either(core, sib_ref, sib_own_ref, keep_ref)
    swapped.insert(half - 2, swap_ref)
    mine.append(keep_ref)

    def mixed(part, swap_part, mine_part):
        return dot(stacked(swapped, part), swap_part[...], 0, 0) + dot(stacked(mine, part), mine_part[...], 0, 0)

    def put(result_t, ref, out, sem):
        for h in range(HEADS):
            ref[:, rows_of(h)] = result_t[:, rows_of(h)].T.astype(jnp.bfloat16)
        copy = pltpu.make_async_copy(ref, out, sem)
        copy.start()
        return copy

    attended_copy = put(mixed(1, swap_weights, mine_weights), attended_ref, attended_out, sems.at[0])
    query_grad_t = mixed(0, swap_score_grad, mine_score_grad) * SCALE
    query_grad_copy = put(query_grad_t, query_grad_ref, query_grad_out, sems.at[1])
    attended_copy.wait()
    query_grad_copy.wait()


def merge_kernel(mine_ref, lin_ref, from_sib_ref, *sent_refs):
    half = mine_ref.shape[0]
    f32, bf16 = jnp.float32, jnp.bfloat16
    for k, ref in enumerate(sent_refs[:-1]):
        ref[...] = (mine_ref[k + 1] + from_sib_ref[k].astype(f32)).astype(bf16)
    _, _, core = position()
    far = from_sib_ref[half - 2].astype(f32)
    sent_refs[-1][: 2 * BLOCK, :] = (jnp.where(core == 0, lin_ref[...], 0.0) + far).astype(bf16)
    sent_refs[-1][2 * BLOCK :, :] = (mine_ref[half - 1] + from_sib_ref[half - 1].astype(f32)).astype(bf16)


def pass_kernel(mine_ref, far_ref, out_ref):
    _, _, core = position()
    near = mine_ref[mine_ref.shape[0] - 1].astype(jnp.bfloat16)
    out_ref[...] = jnp.where(core == 0, far_ref[2 * BLOCK :, :], near)


def total_kernel(mine_ref, far_ref, passed_ref, *refs):
    back, (key_ref, value_ref) = refs[:-2], refs[-2:]
    total = mine_ref[0] + far_ref[: 2 * BLOCK, :].astype(jnp.float32) + passed_ref[...].astype(jnp.float32)
    for ref in back:
        total = total + ref[...].astype(jnp.float32)
    key_ref[...] = total[:BLOCK].astype(jnp.bfloat16)
    value_ref[...] = total[BLOCK:].astype(jnp.bfloat16)


def in_vmem(array):
    return pltpu.with_memory_space_constraint(array, pltpu.VMEM)


def in_hbm(array):
    return pltpu.with_memory_space_constraint(array, pltpu.HBM)


def cost(blocks, products):
    flops = 2 * products * blocks * BLOCK * FLAT * HEAD_DIM
    return pl.CostEstimate(flops=flops, bytes_accessed=blocks * BLOCK * FLAT * 4, transcendentals=0)


def local(devices, queries, key_rows, value_rows, out_grad, doc_ids):
    window = lax.axis_size("kv")
    slots = Slots(window)
    half = slots.half
    bf16, f32 = jnp.bfloat16, jnp.float32
    shape = jax.ShapeDtypeStruct
    small = pltpu.CompilerParams(vmem_limit_bytes=window * MIB // 4)
    params = pltpu.CompilerParams(vmem_limit_bytes=window * MIB)

    def target(i, m):
        top = 1 << (m.bit_length() - 1)
        run, chip, core = i // window, i // 2 % half, i % 2
        run, to = (run, chip ^ m) if not chip & top else (run + 1, chip ^ m)
        if run * window == devices:
            run, to = 0, chip ^ top
        return run * window + 2 * to + core

    def ahead(block, m, back=False):
        route = [(i, target(i, m)) for i in range(devices)]
        return lax.ppermute(block, AXES, [pair[::-1] for pair in route] if back else route)

    def back_mixed(block):
        route = [(target(i, half - 1), i) for i in range(0, devices, 2)]
        route += [((i + window) % devices, i) for i in range(1, devices, 2)]
        return lax.ppermute(block, AXES, route)

    def ahead_odd(block):
        route = [(i, i + window if i + window < devices else i ^ 1) for i in range(1, devices, 2)]
        route += [(i, i - window if i >= window else i ^ 1) for i in range(0, devices, 2)]
        return lax.ppermute(block, AXES, route)

    def swapped(block):
        return lax.ppermute(block, AXES, [(i, i ^ 1) for i in range(devices)])

    own = pl.pallas_call(
        pair_kernel,
        out_shape=pltpu.VMEM((2 * BLOCK, HEAD_DIM), bf16),
        in_specs=[HBM, HBM],
        out_specs=VMEM,
        scratch_shapes=[pltpu.SemaphoreType.DMA((2,))],
        compiler_params=small,
        name="pair_up",
    )(in_hbm(key_rows), in_hbm(value_rows))
    lins = [ahead(own, k) for k in slots.arrival] + [ahead_odd(own)]
    sib_own = swapped(own)

    def stage(blocks):
        return [
            pltpu.VMEM((blocks * BLOCK, FLAT), f32),
            pltpu.VMEM((blocks * BLOCK, FLAT), f32),
            pltpu.VMEM((8, FLAT), f32),
        ]

    query_rows, grad_rows, bias, *own_stage = pl.pallas_call(
        functools.partial(own_kernel, slots),
        out_shape=[pltpu.VMEM((FLAT, HEAD_DIM), bf16)] * 2 + [pltpu.VMEM((window, FLAT), f32)] + stage(1),
        in_specs=[HBM, HBM, HBM, VMEM],
        out_specs=[VMEM] * 6,
        scratch_shapes=[
            pltpu.SMEM(doc_ids.shape, jnp.int32),
            pltpu.SemaphoreType.DMA,
            pltpu.SemaphoreType.DMA((2, HEADS)),
        ],
        compiler_params=params,
        cost_estimate=cost(1, 2),
        name="own_scores",
    )(in_hbm(doc_ids), in_hbm(queries), in_hbm(out_grad), own)

    lins[0], own_stage[2] = lax.optimization_barrier((lins[0], own_stage[2]))
    sibs = [swapped(block) for block in lins[: half - 2]]
    held = {("lin", k): block for k, block in zip(slots.arrival[:-1], lins)}

    def next_stage(at, before):
        group = slots.stages[at]
        first = sum(len(earlier) for earlier in slots.stages[1:at])
        return list(
            pl.pallas_call(
                functools.partial(stage_kernel, first, len(group)),
                out_shape=stage(len(group)),
                in_specs=[VMEM] * (4 + len(group)),
                out_specs=[VMEM] * 3,
                compiler_params=params,
                cost_estimate=cost(len(group), 2),
                name="stage_scores",
            )(bias, query_rows, grad_rows, before, *[held[slot] for slot in group])
        )

    middle_stage = next_stage(1, own_stage[2])
    lins[half - 1], lins[half - 2], middle_stage[2] = lax.optimization_barrier(
        (lins[half - 1], lins[half - 2], middle_stage[2])
    )
    sibs += [swapped(block) for block in lins[half - 2 :]]
    held |= {"own": own, "last": sibs[-1]}
    for k, block, swap in zip(slots.arrival, lins, sibs):
        held["lin", k] = block
        held["sib", k] = swap
    closing_stage = next_stage(2, middle_stage[2])

    sib, far, near = held[slots.late[0]], held["last"], sib_own
    weights = [pltpu.VMEM((half * BLOCK, FLAT), bf16)] * 2
    *keep, final, swap_weights, swap_score_grad, swap_out, lin_out = pl.pallas_call(
        functools.partial(late_kernel, slots),
        out_shape=stage(1)
        + weights
        + [pltpu.VMEM((half, 2 * BLOCK, HEAD_DIM), bf16), pltpu.VMEM((2 * BLOCK, HEAD_DIM), f32)],
        in_specs=[VMEM] * 9,
        out_specs=[VMEM] * 7,
        scratch_shapes=[pltpu.VMEM((2 * BLOCK, HEAD_DIM), bf16)],
        compiler_params=params,
        cost_estimate=cost(window, 2),
        name="late_scores",
    )(bias, query_rows, grad_rows, *closing_stage, sib, far, near)
    from_sib = swapped(swap_out)

    mine_weights, mine_score_grad, mine = pl.pallas_call(
        functools.partial(mine_kernel, slots),
        out_shape=weights + [pltpu.VMEM((half, 2 * BLOCK, HEAD_DIM), f32)],
        in_specs=[VMEM] * 11,
        out_specs=[VMEM] * 3,
        compiler_params=params,
        cost_estimate=cost(half, 2),
        name="other_grads",
    )(query_rows, grad_rows, final, *own_stage, *middle_stage, *keep)

    attended, query_grad = pl.pallas_call(
        functools.partial(query_side_kernel, slots),
        out_shape=[shape(queries.shape, bf16)] * 2,
        in_specs=[VMEM] * (5 + 2 * half),
        out_specs=[HBM] * 2,
        scratch_shapes=[
            pltpu.VMEM((2 * BLOCK, HEAD_DIM), bf16),
            pltpu.VMEM((2 * BLOCK, HEAD_DIM), bf16),
            pltpu.VMEM(queries.shape, bf16),
            pltpu.VMEM(queries.shape, bf16),
            pltpu.SemaphoreType.DMA((2,)),
        ],
        compiler_params=params,
        cost_estimate=cost(window, 2),
        name="query_side",
    )(
        *[in_vmem(part) for part in (swap_weights, swap_score_grad, mine_weights, mine_score_grad)],
        *[held[slot] for slot in slots.closing + ["own"] + slots.middle],
        sib, far, near,
    )

    block = pltpu.VMEM((2 * BLOCK, HEAD_DIM), bf16)
    *sent, sent_far = pl.pallas_call(
        merge_kernel,
        out_shape=[block] * (half - 2) + [pltpu.VMEM((4 * BLOCK, HEAD_DIM), bf16)],
        in_specs=[VMEM] * 3,
        out_specs=[VMEM] * (half - 1),
        compiler_params=small,
        name="merge_siblings",
    )(mine, lin_out, from_sib)
    back_far = back_mixed(sent_far)
    passed = swapped(
        pl.pallas_call(
            pass_kernel,
            out_shape=block,
            in_specs=[VMEM] * 2,
            out_specs=VMEM,
            compiler_params=small,
            name="pass_on",
        )(mine, back_far)
    )
    back = [ahead(sent[m - 1], m, back=True) for m in range(half - 2, 0, -1)]
    key_grad, value_grad = pl.pallas_call(
        total_kernel,
        out_shape=[shape((BLOCK, HEAD_DIM), bf16)] * 2,
        in_specs=[VMEM] * (1 + half),
        out_specs=[VMEM] * 2,
        compiler_params=small,
        name="total_grads",
    )(mine, back_far, passed, *back)
    return attended, query_grad, key_grad, value_grad


def solution(mesh):
    split = P(AXES, None)
    devices = mesh.shape["pb"] * mesh.shape["kv"]
    return jax.shard_map(
        functools.partial(local, devices),
        mesh=mesh,
        in_specs=(split, split, split, split, P()),
        out_specs=(split, split, split, split),
        check_vma=False,
    )
```

```python
import functools
import math

import jax
import jax.numpy as jnp
from jax import lax
from jax.experimental import pallas as pl
from jax.experimental.pallas import tpu as pltpu
from jax.sharding import PartitionSpec as P

HEADS = 8
HEAD_DIM = 128
BLOCK = 128
FLAT = HEADS * BLOCK
AXES = ("pb", "kv")
SCALE = HEAD_DIM ** (-0.5)
SCALE_LOG2 = SCALE / math.log(2.0)
FAR = 1e30
COLS = 256
MIB = 2**20

VMEM = pl.BlockSpec(memory_space=pltpu.VMEM)
HBM = pl.BlockSpec(memory_space=pltpu.HBM)


def dot(left, right, left_dim, right_dim):
    return lax.dot_general(
        left, right, (((left_dim,), (right_dim,)), ((), ())), preferred_element_type=jnp.float32
    )


def rows_of(block):
    return slice(block * BLOCK, (block + 1) * BLOCK)


class Slots:
    def __init__(self, window):
        self.window = window
        self.half = half = window // 2
        self.arrival = list(range(1, half))
        lins = [("lin", k) for k in self.arrival]
        sibs = [("sib", k) for k in self.arrival]
        self.middle = lins[:-1]
        self.closing = sibs[:-1] + lins[-1:]
        self.late = [sibs[-1], "last"]
        self.stages = [["own"], self.middle, self.closing, self.late]
        self.swapped = self.closing[:-1] + ["swap"] + self.closing[-1:]
        self.mine = ["own"] + self.middle + ["keep"]

    def place(self, slot):
        for at, group in enumerate([*self.stages[:-1], ["keep"]]):
            if slot in group:
                return at, rows_of(group.index(slot))

    def distance(self, slot):
        _, chip, core = position()
        if slot == "last":
            return jnp.where(core == 0, self.window - 1, 1)
        kind, m = slot
        chips = lax.rem(chip - lax.bitwise_xor(chip, m) + self.half, self.half)
        return 2 * chips if kind == "lin" else 2 * chips - 1 + 2 * core


def position():
    column = lax.axis_index("kv")
    return lax.axis_index("pb") * lax.axis_size("kv") + column, column // 2, lax.rem(column, 2)


def reached(doc_ref, slots, slot):
    me, _, _ = position()
    at = me - slots.distance(slot)
    return (at >= 0) & (doc_ref[jnp.maximum(at, 0)] == doc_ref[me])


def stacked(refs, part):
    return jnp.concatenate([ref[part * BLOCK : (part + 1) * BLOCK, :] for ref in refs], axis=0)


def tile_of(column):
    return slice(column * COLS, (column + 1) * COLS)


def absorb(parts, probs_grad, biases, top, total, mixed):
    new_top = top
    for part, bias in zip(parts, biases):
        new_top = jnp.maximum(new_top, jnp.max(part, axis=0, keepdims=True) * SCALE_LOG2 + bias)
    rescale = jnp.exp2(top - new_top)
    total, mixed = total * rescale, mixed * rescale
    powers = []
    for s, (part, bias) in enumerate(zip(parts, biases)):
        power = jnp.exp2(part * SCALE_LOG2 - (new_top - bias))
        powers.append(power)
        total = total + jnp.sum(power, axis=0, keepdims=True)
        mixed = mixed + jnp.sum(power * probs_grad[s * BLOCK : (s + 1) * BLOCK, :], axis=0, keepdims=True)
    return powers, new_top, total, mixed


def pair_kernel(key_ref, value_ref, pair_ref, sems):
    copies = [
        pltpu.make_async_copy(ref, pair_ref.at[part * BLOCK : (part + 1) * BLOCK, :], sems.at[part])
        for part, ref in enumerate((key_ref, value_ref))
    ]
    for copy in copies:
        copy.start()
    for copy in copies:
        copy.wait()


def own_kernel(
    slots, doc_hbm, query_ref, grad_ref, own_ref,
    query_rows, grad_rows, bias_ref, powers_ref, probs_ref, stats_ref, doc_ref, doc_sem, sems,
):
    copies = [pltpu.make_async_copy(doc_hbm, doc_ref, doc_sem)]
    for h in range(HEADS):
        rows = slice(h * BLOCK, (h + 1) * BLOCK)
        copies.append(pltpu.make_async_copy(query_ref.at[:, rows], query_rows.at[rows, :], sems.at[0, h]))
        copies.append(pltpu.make_async_copy(grad_ref.at[:, rows], grad_rows.at[rows, :], sems.at[1, h]))
    for copy in copies:
        copy.start()
    key_row = lax.broadcasted_iota(jnp.int32, (BLOCK, COLS), 0)
    token = lax.broadcasted_iota(jnp.int32, (BLOCK, COLS), 1) % BLOCK
    causal = key_row <= token
    for copy in copies:
        copy.wait()
    for row, slot in enumerate(slots.middle + slots.closing + slots.late):
        bias = jnp.where(reached(doc_ref, slots, slot), 0.0, -FAR)
        bias_ref[row : row + 1, :] = jnp.full((1, FLAT), bias, jnp.float32)
    for column in range(FLAT // COLS):
        cols = tile_of(column)
        scores = dot(own_ref[:BLOCK, :], query_rows[cols, :], 1, 1)
        probs_grad = dot(own_ref[BLOCK:, :], grad_rows[cols, :], 1, 1)
        scores = jnp.where(causal, scores, -FAR)
        start = jnp.full((1, COLS), -FAR, jnp.float32), jnp.zeros((1, COLS)), jnp.zeros((1, COLS))
        put_stage([scores], probs_grad, [0.0], start, column, powers_ref, probs_ref, stats_ref)


def put_stage(parts, probs_grad, biases, start, column, powers_ref, probs_ref, stats_ref):
    cols = tile_of(column)
    powers, top, total, mixed = absorb(parts, probs_grad, biases, *start)
    for s, power in enumerate(powers):
        powers_ref[s * BLOCK : (s + 1) * BLOCK, cols] = power
    probs_ref[:, cols] = probs_grad
    for row, value in enumerate((top, total, mixed)):
        stats_ref[row : row + 1, cols] = value


def stage_kernel(first, count, *refs):
    bias_ref, query_rows, grad_rows, before_ref = refs[:4]
    blocks = refs[4 : 4 + count]
    powers_ref, probs_ref, stats_ref = refs[4 + count :]
    keys, values = stacked(blocks, 0), stacked(blocks, 1)
    for column in range(FLAT // COLS):
        cols = tile_of(column)
        scores = dot(keys, query_rows[cols, :], 1, 1)
        probs_grad = dot(values, grad_rows[cols, :], 1, 1)
        parts = [scores[rows_of(s), :] for s in range(count)]
        start = tuple(before_ref[row : row + 1, cols] for row in range(3))
        biases = [bias_ref[row : row + 1, cols] for row in range(first, first + count)]
        put_stage(parts, probs_grad, biases, start, column, powers_ref, probs_ref, stats_ref)


def put_weights(slot_rows, cols, powers, factor, probs, delta, weights_ref, score_grad_ref):
    weights = powers * factor
    weights_ref[slot_rows, cols] = weights.astype(jnp.bfloat16)
    score_grad_ref[slot_rows, cols] = (weights * (probs - delta)).astype(jnp.bfloat16)


def put_grads(weights_ref, score_grad_ref, query_rows, grad_rows, out_ref):
    key_grad = dot(score_grad_ref[...], query_rows[...], 1, 0) * SCALE
    value_grad = dot(weights_ref[...], grad_rows[...], 1, 0)
    for k in range(out_ref.shape[0]):
        out_ref[k, :BLOCK, :] = key_grad[rows_of(k), :].astype(out_ref.dtype)
        out_ref[k, BLOCK:, :] = value_grad[rows_of(k), :].astype(out_ref.dtype)


def put_either(core, even, odd, ref):
    @pl.when(core == 0)
    def _():
        ref[...] = even[...]

    @pl.when(core == 1)
    def _():
        ref[...] = odd[...]


def late_kernel(slots, *refs):
    bias_ref, query_rows, grad_rows, powers_ref, probs_ref, before_ref = refs[:6]
    sib_ref, far_ref, sib_own_ref = refs[6:9]
    keep_powers, keep_probs, final_ref, weights_ref, score_grad_ref, far_out, rest_out, lin_ref, last_ref = refs[9:]
    _, _, core = position()
    even = core == 0
    half = slots.half
    put_either(core, far_ref, sib_own_ref, last_ref)
    blocks = [sib_ref, last_ref]
    keys, values = stacked(blocks, 0), stacked(blocks, 1)
    first = slots.window - 1 - len(blocks)
    for column in range(FLAT // COLS):
        cols = tile_of(column)
        scores = dot(keys, query_rows[cols, :], 1, 1)
        probs_grad = dot(values, grad_rows[cols, :], 1, 1)
        parts = [scores[rows_of(s), :] for s in range(2)]
        start = tuple(before_ref[row : row + 1, cols] for row in range(3))
        biases = [bias_ref[row : row + 1, cols] for row in range(first, first + 2)]
        powers, top, total, mixed = absorb(parts, probs_grad, biases, *start)
        inverse = 1.0 / total
        delta = mixed * inverse
        for row, value in enumerate((top, inverse, delta)):
            final_ref[row : row + 1, cols] = value
        sib_probs, last_probs = probs_grad[rows_of(0), :], probs_grad[rows_of(1), :]
        keep_powers[:, cols] = jnp.where(even, powers[0], powers[1])
        keep_probs[:, cols] = jnp.where(even, sib_probs, last_probs)
        factor = jnp.exp2(start[0] - top) * inverse
        for s, slot in enumerate(slots.swapped):
            if slot == "swap":
                piece = jnp.where(even, powers[1], powers[0]), inverse, jnp.where(even, last_probs, sib_probs)
            else:
                _, rows = slots.place(slot)
                piece = powers_ref[rows, cols], factor, probs_ref[rows, cols]
            put_weights(rows_of(s), cols, *piece, delta, weights_ref, score_grad_ref)
    key_grad = dot(score_grad_ref[...], query_rows[...], 1, 0) * SCALE
    value_grad = dot(weights_ref[...], grad_rows[...], 1, 0)
    for k in range(half):
        ref, at = (rest_out, k) if k < half - 2 else (far_out, k - (half - 2))
        ref[at, :BLOCK, :] = key_grad[rows_of(k), :].astype(jnp.bfloat16)
        ref[at, BLOCK:, :] = value_grad[rows_of(k), :].astype(jnp.bfloat16)
    lin_ref[:BLOCK, :] = key_grad[rows_of(half - 1), :]
    lin_ref[BLOCK:, :] = value_grad[rows_of(half - 1), :]


def mine_kernel(slots, *refs):
    query_rows, grad_rows, final_ref = refs[:3]
    stages = {0: refs[3:6], 1: refs[6:9], 3: (*refs[9:11], final_ref)}
    weights_ref, score_grad_ref, mine_ref = refs[11:]
    for column in range(FLAT // COLS):
        cols = tile_of(column)
        top, inverse, delta = (final_ref[row : row + 1, cols] for row in range(3))
        for s, slot in enumerate(slots.mine):
            at, rows = slots.place(slot)
            powers_ref, probs_ref, stats_ref = stages[at]
            factor = jnp.exp2(stats_ref[0:1, cols] - top) * inverse
            piece = powers_ref[rows, cols], factor, probs_ref[rows, cols]
            put_weights(rows_of(s), cols, *piece, delta, weights_ref, score_grad_ref)
    key_grad = dot(score_grad_ref[...], query_rows[...], 1, 0) * SCALE
    value_grad = dot(weights_ref[...], grad_rows[...], 1, 0)
    for k in range(slots.half):
        mine_ref[k, :BLOCK, :] = key_grad[rows_of(k), :]
        mine_ref[k, BLOCK:, :] = value_grad[rows_of(k), :]


def query_side_kernel(slots, *refs):
    half = slots.half
    swap_weights, swap_score_grad, mine_weights, mine_score_grad = refs[:4]
    swapped, mine = list(refs[4 : 3 + half]), list(refs[3 + half : 2 + 2 * half])
    sib_ref, far_ref, sib_own_ref, attended_out, query_grad_out = refs[2 + 2 * half : 7 + 2 * half]
    swap_ref, keep_ref, attended_ref, query_grad_ref, sems = refs[7 + 2 * half :]
    _, _, core = position()
    put_either(core, far_ref, sib_ref, swap_ref)
    put_either(core, sib_ref, sib_own_ref, keep_ref)
    swapped.insert(half - 2, swap_ref)
    mine.append(keep_ref)

    def mixed(part, swap_part, mine_part):
        return dot(stacked(swapped, part), swap_part[...], 0, 0) + dot(stacked(mine, part), mine_part[...], 0, 0)

    def put(result_t, ref, out, sem):
        for h in range(HEADS):
            ref[:, rows_of(h)] = result_t[:, rows_of(h)].T.astype(jnp.bfloat16)
        copy = pltpu.make_async_copy(ref, out, sem)
        copy.start()
        return copy

    attended_copy = put(mixed(1, swap_weights, mine_weights), attended_ref, attended_out, sems.at[0])
    query_grad_t = mixed(0, swap_score_grad, mine_score_grad) * SCALE
    query_grad_copy = put(query_grad_t, query_grad_ref, query_grad_out, sems.at[1])
    attended_copy.wait()
    query_grad_copy.wait()


def merge_far_kernel(mine_ref, lin_ref, from_sib_ref, sent_ref):
    _, _, core = position()
    far = from_sib_ref[0].astype(jnp.float32) + jnp.where(core == 0, lin_ref[...], 0.0)
    other = from_sib_ref[1].astype(jnp.float32) + mine_ref[mine_ref.shape[0] - 1]
    sent_ref[: 2 * BLOCK, :] = far.astype(jnp.bfloat16)
    sent_ref[2 * BLOCK :, :] = other.astype(jnp.bfloat16)


def merge_rest_kernel(mine_ref, from_sib_ref, *sent_refs):
    for k, ref in enumerate(sent_refs):
        ref[...] = (mine_ref[k + 1] + from_sib_ref[k].astype(jnp.float32)).astype(jnp.bfloat16)


def pass_kernel(mine_ref, far_ref, out_ref):
    _, _, core = position()
    near = mine_ref[mine_ref.shape[0] - 1].astype(jnp.bfloat16)
    out_ref[...] = jnp.where(core == 0, far_ref[2 * BLOCK :, :], near)


def total_kernel(mine_ref, far_ref, passed_ref, *refs):
    back, (key_ref, value_ref) = refs[:-2], refs[-2:]
    total = mine_ref[0] + far_ref[: 2 * BLOCK, :].astype(jnp.float32) + passed_ref[...].astype(jnp.float32)
    for ref in back:
        total = total + ref[...].astype(jnp.float32)
    key_ref[...] = total[:BLOCK].astype(jnp.bfloat16)
    value_ref[...] = total[BLOCK:].astype(jnp.bfloat16)


def in_vmem(array):
    return pltpu.with_memory_space_constraint(array, pltpu.VMEM)


def in_hbm(array):
    return pltpu.with_memory_space_constraint(array, pltpu.HBM)


def cost(blocks, products):
    flops = 2 * products * blocks * BLOCK * FLAT * HEAD_DIM
    return pl.CostEstimate(flops=flops, bytes_accessed=blocks * BLOCK * FLAT * 4, transcendentals=0)


def local(devices, queries, key_rows, value_rows, out_grad, doc_ids):
    window = lax.axis_size("kv")
    slots = Slots(window)
    half = slots.half
    bf16, f32 = jnp.bfloat16, jnp.float32
    shape = jax.ShapeDtypeStruct
    small = pltpu.CompilerParams(vmem_limit_bytes=window * MIB // 4)
    params = pltpu.CompilerParams(vmem_limit_bytes=window * MIB)

    def target(i, m):
        top = 1 << (m.bit_length() - 1)
        run, chip, core = i // window, i // 2 % half, i % 2
        run, to = (run, chip ^ m) if not chip & top else (run + 1, chip ^ m)
        if run * window == devices:
            run, to = 0, chip ^ top
        return run * window + 2 * to + core

    def ahead(block, m, back=False):
        route = [(i, target(i, m)) for i in range(devices)]
        return lax.ppermute(block, AXES, [pair[::-1] for pair in route] if back else route)

    def back_mixed(block):
        route = [(target(i, half - 1), i) for i in range(0, devices, 2)]
        route += [((i + window) % devices, i) for i in range(1, devices, 2)]
        return lax.ppermute(block, AXES, route)

    def ahead_odd(block):
        route = [(i, i + window if i + window < devices else i ^ 1) for i in range(1, devices, 2)]
        route += [(i, i - window if i >= window else i ^ 1) for i in range(0, devices, 2)]
        return lax.ppermute(block, AXES, route)

    def swapped(block):
        return lax.ppermute(block, AXES, [(i, i ^ 1) for i in range(devices)])

    own = pl.pallas_call(
        pair_kernel,
        out_shape=pltpu.VMEM((2 * BLOCK, HEAD_DIM), bf16),
        in_specs=[HBM, HBM],
        out_specs=VMEM,
        scratch_shapes=[pltpu.SemaphoreType.DMA((2,))],
        compiler_params=small,
        name="pair_up",
    )(in_hbm(key_rows), in_hbm(value_rows))
    lins = [ahead(own, k) for k in slots.arrival] + [ahead_odd(own)]
    sib_own = swapped(own)

    def stage(blocks):
        return [
            pltpu.VMEM((blocks * BLOCK, FLAT), f32),
            pltpu.VMEM((blocks * BLOCK, FLAT), f32),
            pltpu.VMEM((8, FLAT), f32),
        ]

    query_rows, grad_rows, bias, *own_stage = pl.pallas_call(
        functools.partial(own_kernel, slots),
        out_shape=[pltpu.VMEM((FLAT, HEAD_DIM), bf16)] * 2 + [pltpu.VMEM((window, FLAT), f32)] + stage(1),
        in_specs=[HBM, HBM, HBM, VMEM],
        out_specs=[VMEM] * 6,
        scratch_shapes=[
            pltpu.SMEM(doc_ids.shape, jnp.int32),
            pltpu.SemaphoreType.DMA,
            pltpu.SemaphoreType.DMA((2, HEADS)),
        ],
        compiler_params=params,
        cost_estimate=cost(1, 2),
        name="own_scores",
    )(in_hbm(doc_ids), in_hbm(queries), in_hbm(out_grad), own)

    lins[0], own_stage[2] = lax.optimization_barrier((lins[0], own_stage[2]))
    sibs = [swapped(block) for block in lins[: half - 2]]
    held = {("lin", k): block for k, block in zip(slots.arrival[:-1], lins)}

    def next_stage(at, before):
        group = slots.stages[at]
        first = sum(len(earlier) for earlier in slots.stages[1:at])
        return list(
            pl.pallas_call(
                functools.partial(stage_kernel, first, len(group)),
                out_shape=stage(len(group)),
                in_specs=[VMEM] * (4 + len(group)),
                out_specs=[VMEM] * 3,
                compiler_params=params,
                cost_estimate=cost(len(group), 2),
                name="stage_scores",
            )(bias, query_rows, grad_rows, before, *[held[slot] for slot in group])
        )

    middle_stage = next_stage(1, own_stage[2])
    lins[half - 1], lins[half - 2], middle_stage[2] = lax.optimization_barrier(
        (lins[half - 1], lins[half - 2], middle_stage[2])
    )
    sibs += [swapped(block) for block in lins[half - 2 :]]
    held |= {"own": own, "last": sibs[-1]}
    for k, block, swap in zip(slots.arrival, lins, sibs):
        held["lin", k] = block
        held["sib", k] = swap
    closing_stage = next_stage(2, middle_stage[2])

    sib, far, near = held[slots.late[0]], held["last"], sib_own
    weights = [pltpu.VMEM((half * BLOCK, FLAT), bf16)] * 2
    *keep, final, swap_weights, swap_score_grad, far_out, rest_out, lin_out = pl.pallas_call(
        functools.partial(late_kernel, slots),
        out_shape=stage(1)
        + weights
        + [pltpu.VMEM((blocks, 2 * BLOCK, HEAD_DIM), bf16) for blocks in (2, half - 2)]
        + [pltpu.VMEM((2 * BLOCK, HEAD_DIM), f32)],
        in_specs=[VMEM] * 9,
        out_specs=[VMEM] * 8,
        scratch_shapes=[pltpu.VMEM((2 * BLOCK, HEAD_DIM), bf16)],
        compiler_params=params,
        cost_estimate=cost(window, 2),
        name="late_scores",
    )(bias, query_rows, grad_rows, *closing_stage, sib, far, near)
    far_from_sib, rest_from_sib = swapped(far_out), swapped(rest_out)

    mine_weights, mine_score_grad, mine = pl.pallas_call(
        functools.partial(mine_kernel, slots),
        out_shape=weights + [pltpu.VMEM((half, 2 * BLOCK, HEAD_DIM), f32)],
        in_specs=[VMEM] * 11,
        out_specs=[VMEM] * 3,
        compiler_params=params,
        cost_estimate=cost(half, 2),
        name="other_grads",
    )(query_rows, grad_rows, final, *own_stage, *middle_stage, *keep)

    attended, query_grad = pl.pallas_call(
        functools.partial(query_side_kernel, slots),
        out_shape=[shape(queries.shape, bf16)] * 2,
        in_specs=[VMEM] * (5 + 2 * half),
        out_specs=[HBM] * 2,
        scratch_shapes=[
            pltpu.VMEM((2 * BLOCK, HEAD_DIM), bf16),
            pltpu.VMEM((2 * BLOCK, HEAD_DIM), bf16),
            pltpu.VMEM(queries.shape, bf16),
            pltpu.VMEM(queries.shape, bf16),
            pltpu.SemaphoreType.DMA((2,)),
        ],
        compiler_params=params,
        cost_estimate=cost(window, 2),
        name="query_side",
    )(
        *[in_vmem(part) for part in (swap_weights, swap_score_grad, mine_weights, mine_score_grad)],
        *[held[slot] for slot in slots.closing + ["own"] + slots.middle],
        sib, far, near,
    )

    block = pltpu.VMEM((2 * BLOCK, HEAD_DIM), bf16)
    sent_far = pl.pallas_call(
        merge_far_kernel,
        out_shape=pltpu.VMEM((4 * BLOCK, HEAD_DIM), bf16),
        in_specs=[VMEM] * 3,
        out_specs=VMEM,
        compiler_params=small,
        name="merge_far",
    )(mine, lin_out, far_from_sib)
    sent = pl.pallas_call(
        merge_rest_kernel,
        out_shape=[block] * (half - 2),
        in_specs=[VMEM] * 2,
        out_specs=[VMEM] * (half - 2),
        compiler_params=small,
        name="merge_rest",
    )(mine, rest_from_sib)
    back_far = back_mixed(sent_far)
    passed = swapped(
        pl.pallas_call(
            pass_kernel,
            out_shape=block,
            in_specs=[VMEM] * 2,
            out_specs=VMEM,
            compiler_params=small,
            name="pass_on",
        )(mine, back_far)
    )
    back = [ahead(sent[m - 1], m, back=True) for m in range(half - 2, 0, -1)]
    key_grad, value_grad = pl.pallas_call(
        total_kernel,
        out_shape=[shape((BLOCK, HEAD_DIM), bf16)] * 2,
        in_specs=[VMEM] * (1 + half),
        out_specs=[VMEM] * 2,
        compiler_params=small,
        name="total_grads",
    )(mine, back_far, passed, *back)
    return attended, query_grad, key_grad, value_grad


def solution(mesh):
    split = P(AXES, None)
    devices = mesh.shape["pb"] * mesh.shape["kv"]
    return jax.shard_map(
        functools.partial(local, devices),
        mesh=mesh,
        in_specs=(split, split, split, split, P()),
        out_specs=(split, split, split, split),
        check_vma=False,
    )
```

```python
import functools
import math

import jax
import jax.numpy as jnp
from jax import lax
from jax.experimental import pallas as pl
from jax.experimental.pallas import tpu as pltpu
from jax.sharding import PartitionSpec as P

HEADS = 8
HEAD_DIM = 128
BLOCK = 128
FLAT = HEADS * BLOCK
AXES = ("pb", "kv")
SCALE = HEAD_DIM ** (-0.5)
SCALE_LOG2 = SCALE / math.log(2.0)
FAR = 1e30
COLS = 256
MIB = 2**20

VMEM = pl.BlockSpec(memory_space=pltpu.VMEM)
HBM = pl.BlockSpec(memory_space=pltpu.HBM)


def dot(left, right, left_dim, right_dim):
    return lax.dot_general(
        left, right, (((left_dim,), (right_dim,)), ((), ())), preferred_element_type=jnp.float32
    )


def rows_of(block):
    return slice(block * BLOCK, (block + 1) * BLOCK)


class Slots:
    def __init__(self, window):
        self.window = window
        self.half = half = window // 2
        self.arrival = list(range(1, half))
        lins = [("lin", k) for k in self.arrival]
        sibs = [("sib", k) for k in self.arrival]
        self.middle = lins[:-1]
        self.closing = sibs[:-1] + lins[-1:]
        self.late = [sibs[-1], "last"]
        self.stages = [["own"], self.middle, self.closing, self.late]
        self.swapped = self.closing[:-1] + ["swap"] + self.closing[-1:]
        self.mine = ["own"] + self.middle + ["keep"]

    def place(self, slot):
        for at, group in enumerate([*self.stages[:-1], ["keep"]]):
            if slot in group:
                return at, rows_of(group.index(slot))

    def distance(self, slot):
        _, chip, core = position()
        if slot == "last":
            return jnp.where(core == 0, self.window - 1, 1)
        kind, m = slot
        chips = lax.rem(chip - lax.bitwise_xor(chip, m) + self.half, self.half)
        return 2 * chips if kind == "lin" else 2 * chips - 1 + 2 * core


def position():
    column = lax.axis_index("kv")
    return lax.axis_index("pb") * lax.axis_size("kv") + column, column // 2, lax.rem(column, 2)


def reached(doc_ref, slots, slot):
    me, _, _ = position()
    at = me - slots.distance(slot)
    return (at >= 0) & (doc_ref[jnp.maximum(at, 0)] == doc_ref[me])


def stacked(refs, part):
    return jnp.concatenate([ref[part * BLOCK : (part + 1) * BLOCK, :] for ref in refs], axis=0)


def tile_of(column):
    return slice(column * COLS, (column + 1) * COLS)


def absorb(parts, probs_grad, biases, top, total, mixed):
    new_top = top
    for part, bias in zip(parts, biases):
        new_top = jnp.maximum(new_top, jnp.max(part, axis=0, keepdims=True) * SCALE_LOG2 + bias)
    rescale = jnp.exp2(top - new_top)
    total, mixed = total * rescale, mixed * rescale
    powers = []
    for s, (part, bias) in enumerate(zip(parts, biases)):
        power = jnp.exp2(part * SCALE_LOG2 - (new_top - bias))
        powers.append(power)
        total = total + jnp.sum(power, axis=0, keepdims=True)
        mixed = mixed + jnp.sum(power * probs_grad[s * BLOCK : (s + 1) * BLOCK, :], axis=0, keepdims=True)
    return powers, new_top, total, mixed


def pair_kernel(key_ref, value_ref, pair_ref, sems):
    copies = [
        pltpu.make_async_copy(ref, pair_ref.at[part * BLOCK : (part + 1) * BLOCK, :], sems.at[part])
        for part, ref in enumerate((key_ref, value_ref))
    ]
    for copy in copies:
        copy.start()
    for copy in copies:
        copy.wait()


def own_kernel(
    slots, doc_hbm, query_ref, grad_ref, own_ref,
    query_rows, grad_rows, bias_ref, powers_ref, probs_ref, stats_ref, doc_ref, doc_sem, sems,
):
    copies = [pltpu.make_async_copy(doc_hbm, doc_ref, doc_sem)]
    for h in range(HEADS):
        rows = slice(h * BLOCK, (h + 1) * BLOCK)
        copies.append(pltpu.make_async_copy(query_ref.at[:, rows], query_rows.at[rows, :], sems.at[0, h]))
        copies.append(pltpu.make_async_copy(grad_ref.at[:, rows], grad_rows.at[rows, :], sems.at[1, h]))
    for copy in copies:
        copy.start()
    key_row = lax.broadcasted_iota(jnp.int32, (BLOCK, COLS), 0)
    token = lax.broadcasted_iota(jnp.int32, (BLOCK, COLS), 1) % BLOCK
    causal = key_row <= token
    for copy in copies:
        copy.wait()
    for row, slot in enumerate(slots.middle + slots.closing + slots.late):
        bias = jnp.where(reached(doc_ref, slots, slot), 0.0, -FAR)
        bias_ref[row : row + 1, :] = jnp.full((1, FLAT), bias, jnp.float32)
    for column in range(FLAT // COLS):
        cols = tile_of(column)
        scores = dot(own_ref[:BLOCK, :], query_rows[cols, :], 1, 1)
        probs_grad = dot(own_ref[BLOCK:, :], grad_rows[cols, :], 1, 1)
        scores = jnp.where(causal, scores, -FAR)
        start = jnp.full((1, COLS), -FAR, jnp.float32), jnp.zeros((1, COLS)), jnp.zeros((1, COLS))
        put_stage([scores], probs_grad, [0.0], start, column, powers_ref, probs_ref, stats_ref)


def put_stage(parts, probs_grad, biases, start, column, powers_ref, probs_ref, stats_ref):
    cols = tile_of(column)
    powers, top, total, mixed = absorb(parts, probs_grad, biases, *start)
    for s, power in enumerate(powers):
        powers_ref[s * BLOCK : (s + 1) * BLOCK, cols] = power
    probs_ref[:, cols] = probs_grad
    for row, value in enumerate((top, total, mixed)):
        stats_ref[row : row + 1, cols] = value


def stage_kernel(first, count, *refs):
    bias_ref, query_rows, grad_rows, before_ref = refs[:4]
    blocks = refs[4 : 4 + count]
    powers_ref, probs_ref, stats_ref = refs[4 + count :]
    keys, values = stacked(blocks, 0), stacked(blocks, 1)
    for column in range(FLAT // COLS):
        cols = tile_of(column)
        scores = dot(keys, query_rows[cols, :], 1, 1)
        probs_grad = dot(values, grad_rows[cols, :], 1, 1)
        parts = [scores[rows_of(s), :] for s in range(count)]
        start = tuple(before_ref[row : row + 1, cols] for row in range(3))
        biases = [bias_ref[row : row + 1, cols] for row in range(first, first + count)]
        put_stage(parts, probs_grad, biases, start, column, powers_ref, probs_ref, stats_ref)


def put_weights(slot_rows, cols, powers, factor, probs, delta, weights_ref, score_grad_ref):
    weights = powers * factor
    weights_ref[slot_rows, cols] = weights.astype(jnp.bfloat16)
    score_grad_ref[slot_rows, cols] = (weights * (probs - delta)).astype(jnp.bfloat16)


def put_grads(weights_ref, score_grad_ref, query_rows, grad_rows, out_ref):
    key_grad = dot(score_grad_ref[...], query_rows[...], 1, 0) * SCALE
    value_grad = dot(weights_ref[...], grad_rows[...], 1, 0)
    for k in range(out_ref.shape[0]):
        out_ref[k, :BLOCK, :] = key_grad[rows_of(k), :].astype(out_ref.dtype)
        out_ref[k, BLOCK:, :] = value_grad[rows_of(k), :].astype(out_ref.dtype)


def put_either(core, even, odd, ref):
    @pl.when(core == 0)
    def _():
        ref[...] = even[...]

    @pl.when(core == 1)
    def _():
        ref[...] = odd[...]


def late_kernel(slots, *refs):
    bias_ref, query_rows, grad_rows, powers_ref, probs_ref, before_ref = refs[:6]
    sib_ref, far_ref, sib_own_ref = refs[6:9]
    keep_powers, keep_probs, final_ref, weights_ref, score_grad_ref, far_out, rest_out, lin_ref, last_ref = refs[9:]
    _, _, core = position()
    even = core == 0
    half = slots.half
    put_either(core, far_ref, sib_own_ref, last_ref)
    blocks = [sib_ref, last_ref]
    keys, values = stacked(blocks, 0), stacked(blocks, 1)
    first = slots.window - 1 - len(blocks)
    for column in range(FLAT // COLS):
        cols = tile_of(column)
        scores = dot(keys, query_rows[cols, :], 1, 1)
        probs_grad = dot(values, grad_rows[cols, :], 1, 1)
        parts = [scores[rows_of(s), :] for s in range(2)]
        start = tuple(before_ref[row : row + 1, cols] for row in range(3))
        biases = [bias_ref[row : row + 1, cols] for row in range(first, first + 2)]
        powers, top, total, mixed = absorb(parts, probs_grad, biases, *start)
        inverse = 1.0 / total
        delta = mixed * inverse
        for row, value in enumerate((top, inverse, delta)):
            final_ref[row : row + 1, cols] = value
        sib_probs, last_probs = probs_grad[rows_of(0), :], probs_grad[rows_of(1), :]
        keep_powers[:, cols] = jnp.where(even, powers[1], powers[0])
        keep_probs[:, cols] = jnp.where(even, last_probs, sib_probs)
        factor = jnp.exp2(start[0] - top) * inverse
        for s, slot in enumerate(slots.swapped):
            if slot == "swap":
                piece = jnp.where(even, powers[0], powers[1]), inverse, jnp.where(even, sib_probs, last_probs)
            else:
                _, rows = slots.place(slot)
                piece = powers_ref[rows, cols], factor, probs_ref[rows, cols]
            put_weights(rows_of(s), cols, *piece, delta, weights_ref, score_grad_ref)
    key_grad = dot(score_grad_ref[...], query_rows[...], 1, 0) * SCALE
    value_grad = dot(weights_ref[...], grad_rows[...], 1, 0)
    for k in range(half):
        ref, at = (rest_out, k) if k < half - 2 else (far_out, k - (half - 2))
        ref[at, :BLOCK, :] = key_grad[rows_of(k), :].astype(jnp.bfloat16)
        ref[at, BLOCK:, :] = value_grad[rows_of(k), :].astype(jnp.bfloat16)
    lin_ref[:BLOCK, :] = key_grad[rows_of(half - 1), :]
    lin_ref[BLOCK:, :] = value_grad[rows_of(half - 1), :]


def mine_kernel(slots, *refs):
    query_rows, grad_rows, final_ref = refs[:3]
    stages = {0: refs[3:6], 1: refs[6:9], 3: (*refs[9:11], final_ref)}
    weights_ref, score_grad_ref, mine_ref = refs[11:]
    for column in range(FLAT // COLS):
        cols = tile_of(column)
        top, inverse, delta = (final_ref[row : row + 1, cols] for row in range(3))
        for s, slot in enumerate(slots.mine):
            at, rows = slots.place(slot)
            powers_ref, probs_ref, stats_ref = stages[at]
            factor = jnp.exp2(stats_ref[0:1, cols] - top) * inverse
            piece = powers_ref[rows, cols], factor, probs_ref[rows, cols]
            put_weights(rows_of(s), cols, *piece, delta, weights_ref, score_grad_ref)
    key_grad = dot(score_grad_ref[...], query_rows[...], 1, 0) * SCALE
    value_grad = dot(weights_ref[...], grad_rows[...], 1, 0)
    for k in range(slots.half):
        mine_ref[k, :BLOCK, :] = key_grad[rows_of(k), :]
        mine_ref[k, BLOCK:, :] = value_grad[rows_of(k), :]


def query_side_kernel(slots, *refs):
    half = slots.half
    swap_weights, swap_score_grad, mine_weights, mine_score_grad = refs[:4]
    swapped, mine = list(refs[4 : 3 + half]), list(refs[3 + half : 2 + 2 * half])
    sib_ref, far_ref, sib_own_ref, attended_out, query_grad_out = refs[2 + 2 * half : 7 + 2 * half]
    swap_ref, keep_ref, attended_ref, query_grad_ref, sems = refs[7 + 2 * half :]
    _, _, core = position()
    put_either(core, sib_ref, sib_own_ref, swap_ref)
    put_either(core, far_ref, sib_ref, keep_ref)
    swapped.insert(half - 2, swap_ref)
    mine.append(keep_ref)

    def mixed(part, swap_part, mine_part):
        return dot(stacked(swapped, part), swap_part[...], 0, 0) + dot(stacked(mine, part), mine_part[...], 0, 0)

    def put(result_t, ref, out, sem):
        for h in range(HEADS):
            ref[:, rows_of(h)] = result_t[:, rows_of(h)].T.astype(jnp.bfloat16)
        copy = pltpu.make_async_copy(ref, out, sem)
        copy.start()
        return copy

    attended_copy = put(mixed(1, swap_weights, mine_weights), attended_ref, attended_out, sems.at[0])
    query_grad_t = mixed(0, swap_score_grad, mine_score_grad) * SCALE
    query_grad_copy = put(query_grad_t, query_grad_ref, query_grad_out, sems.at[1])
    attended_copy.wait()
    query_grad_copy.wait()


def merge_far_kernel(mine_ref, lin_ref, from_sib_ref, sent_ref):
    _, _, core = position()
    keep = mine_ref[mine_ref.shape[0] - 1]
    far = jnp.where(core == 1, from_sib_ref[0].astype(jnp.float32) + lin_ref[...], keep)
    other = from_sib_ref[1].astype(jnp.float32) + keep
    sent_ref[: 2 * BLOCK, :] = far.astype(jnp.bfloat16)
    sent_ref[2 * BLOCK :, :] = other.astype(jnp.bfloat16)


def merge_rest_kernel(mine_ref, from_sib_ref, *sent_refs):
    for k, ref in enumerate(sent_refs):
        ref[...] = (mine_ref[k + 1] + from_sib_ref[k].astype(jnp.float32)).astype(jnp.bfloat16)


def pass_kernel(far_ref, out_ref):
    _, _, core = position()
    out_ref[...] = jnp.where(core == 1, far_ref[2 * BLOCK :, :], far_ref[: 2 * BLOCK, :])


def total_kernel(mine_ref, from_sib_ref, far_ref, passed_ref, *refs):
    back, (key_ref, value_ref) = refs[:-2], refs[-2:]
    _, _, core = position()
    total = mine_ref[0] + jnp.where(core == 0, from_sib_ref[0], far_ref[: 2 * BLOCK, :]).astype(jnp.float32)
    total = total + passed_ref[...].astype(jnp.float32)
    for ref in back:
        total = total + ref[...].astype(jnp.float32)
    key_ref[...] = total[:BLOCK].astype(jnp.bfloat16)
    value_ref[...] = total[BLOCK:].astype(jnp.bfloat16)


def in_vmem(array):
    return pltpu.with_memory_space_constraint(array, pltpu.VMEM)


def in_hbm(array):
    return pltpu.with_memory_space_constraint(array, pltpu.HBM)


def cost(blocks, products):
    flops = 2 * products * blocks * BLOCK * FLAT * HEAD_DIM
    return pl.CostEstimate(flops=flops, bytes_accessed=blocks * BLOCK * FLAT * 4, transcendentals=0)


def local(devices, queries, key_rows, value_rows, out_grad, doc_ids):
    window = lax.axis_size("kv")
    slots = Slots(window)
    half = slots.half
    bf16, f32 = jnp.bfloat16, jnp.float32
    shape = jax.ShapeDtypeStruct
    small = pltpu.CompilerParams(vmem_limit_bytes=window * MIB // 4)
    params = pltpu.CompilerParams(vmem_limit_bytes=window * MIB)

    def target(i, m):
        top = 1 << (m.bit_length() - 1)
        run, chip, core = i // window, i // 2 % half, i % 2
        run, to = (run, chip ^ m) if not chip & top else (run + 1, chip ^ m)
        if run * window == devices:
            run, to = 0, chip ^ top
        return run * window + 2 * to + core

    def ahead(block, m, back=False):
        route = [(i, target(i, m)) for i in range(devices)]
        return lax.ppermute(block, AXES, [pair[::-1] for pair in route] if back else route)

    def back_mixed(block):
        route = [(target(i, half - 1), i) for i in range(1, devices, 2)]
        route += [((i + window) % devices, i) for i in range(0, devices, 2)]
        return lax.ppermute(block, AXES, route)

    def ahead_odd(block):
        route = [(i, i + window if i + window < devices else i ^ 1) for i in range(1, devices, 2)]
        route += [(i, i - window if i >= window else i ^ 1) for i in range(0, devices, 2)]
        return lax.ppermute(block, AXES, route)

    def swapped(block):
        return lax.ppermute(block, AXES, [(i, i ^ 1) for i in range(devices)])

    own = pl.pallas_call(
        pair_kernel,
        out_shape=pltpu.VMEM((2 * BLOCK, HEAD_DIM), bf16),
        in_specs=[HBM, HBM],
        out_specs=VMEM,
        scratch_shapes=[pltpu.SemaphoreType.DMA((2,))],
        compiler_params=small,
        name="pair_up",
    )(in_hbm(key_rows), in_hbm(value_rows))
    lins = [ahead(own, k) for k in slots.arrival] + [ahead_odd(own)]
    sib_own = swapped(own)

    def stage(blocks):
        return [
            pltpu.VMEM((blocks * BLOCK, FLAT), f32),
            pltpu.VMEM((blocks * BLOCK, FLAT), f32),
            pltpu.VMEM((8, FLAT), f32),
        ]

    query_rows, grad_rows, bias, *own_stage = pl.pallas_call(
        functools.partial(own_kernel, slots),
        out_shape=[pltpu.VMEM((FLAT, HEAD_DIM), bf16)] * 2 + [pltpu.VMEM((window, FLAT), f32)] + stage(1),
        in_specs=[HBM, HBM, HBM, VMEM],
        out_specs=[VMEM] * 6,
        scratch_shapes=[
            pltpu.SMEM(doc_ids.shape, jnp.int32),
            pltpu.SemaphoreType.DMA,
            pltpu.SemaphoreType.DMA((2, HEADS)),
        ],
        compiler_params=params,
        cost_estimate=cost(1, 2),
        name="own_scores",
    )(in_hbm(doc_ids), in_hbm(queries), in_hbm(out_grad), own)

    lins[0], lins[1], own_stage[2] = lax.optimization_barrier((lins[0], lins[1], own_stage[2]))
    sibs = [swapped(block) for block in lins[: half - 2]]
    held = {("lin", k): block for k, block in zip(slots.arrival[:-1], lins)}

    def next_stage(at, before):
        group = slots.stages[at]
        first = sum(len(earlier) for earlier in slots.stages[1:at])
        return list(
            pl.pallas_call(
                functools.partial(stage_kernel, first, len(group)),
                out_shape=stage(len(group)),
                in_specs=[VMEM] * (4 + len(group)),
                out_specs=[VMEM] * 3,
                compiler_params=params,
                cost_estimate=cost(len(group), 2),
                name="stage_scores",
            )(bias, query_rows, grad_rows, before, *[held[slot] for slot in group])
        )

    middle_stage = next_stage(1, own_stage[2])
    lins[half - 1], lins[half - 2], middle_stage[2] = lax.optimization_barrier(
        (lins[half - 1], lins[half - 2], middle_stage[2])
    )
    sibs += [swapped(block) for block in lins[half - 2 :]]
    held |= {"own": own, "last": sibs[-1]}
    for k, block, swap in zip(slots.arrival, lins, sibs):
        held["lin", k] = block
        held["sib", k] = swap
    closing_stage = next_stage(2, middle_stage[2])

    sib, far, near = held[slots.late[0]], held["last"], sib_own
    weights = [pltpu.VMEM((half * BLOCK, FLAT), bf16)] * 2
    *keep, final, swap_weights, swap_score_grad, far_out, rest_out, lin_out = pl.pallas_call(
        functools.partial(late_kernel, slots),
        out_shape=stage(1)
        + weights
        + [pltpu.VMEM((blocks, 2 * BLOCK, HEAD_DIM), bf16) for blocks in (2, half - 2)]
        + [pltpu.VMEM((2 * BLOCK, HEAD_DIM), f32)],
        in_specs=[VMEM] * 9,
        out_specs=[VMEM] * 8,
        scratch_shapes=[pltpu.VMEM((2 * BLOCK, HEAD_DIM), bf16)],
        compiler_params=params,
        cost_estimate=cost(window, 2),
        name="late_scores",
    )(bias, query_rows, grad_rows, *closing_stage, sib, far, near)
    far_from_sib, rest_from_sib = swapped(far_out), swapped(rest_out)

    mine_weights, mine_score_grad, mine = pl.pallas_call(
        functools.partial(mine_kernel, slots),
        out_shape=weights + [pltpu.VMEM((half, 2 * BLOCK, HEAD_DIM), f32)],
        in_specs=[VMEM] * 11,
        out_specs=[VMEM] * 3,
        compiler_params=params,
        cost_estimate=cost(half, 2),
        name="other_grads",
    )(query_rows, grad_rows, final, *own_stage, *middle_stage, *keep)

    attended, query_grad = pl.pallas_call(
        functools.partial(query_side_kernel, slots),
        out_shape=[shape(queries.shape, bf16)] * 2,
        in_specs=[VMEM] * (5 + 2 * half),
        out_specs=[HBM] * 2,
        scratch_shapes=[
            pltpu.VMEM((2 * BLOCK, HEAD_DIM), bf16),
            pltpu.VMEM((2 * BLOCK, HEAD_DIM), bf16),
            pltpu.VMEM(queries.shape, bf16),
            pltpu.VMEM(queries.shape, bf16),
            pltpu.SemaphoreType.DMA((2,)),
        ],
        compiler_params=params,
        cost_estimate=cost(window, 2),
        name="query_side",
    )(
        *[in_vmem(part) for part in (swap_weights, swap_score_grad, mine_weights, mine_score_grad)],
        *[held[slot] for slot in slots.closing + ["own"] + slots.middle],
        sib, far, near,
    )

    block = pltpu.VMEM((2 * BLOCK, HEAD_DIM), bf16)
    sent_far = pl.pallas_call(
        merge_far_kernel,
        out_shape=pltpu.VMEM((4 * BLOCK, HEAD_DIM), bf16),
        in_specs=[VMEM] * 3,
        out_specs=VMEM,
        compiler_params=small,
        name="merge_far",
    )(mine, lin_out, far_from_sib)
    sent = pl.pallas_call(
        merge_rest_kernel,
        out_shape=[block] * (half - 2),
        in_specs=[VMEM] * 2,
        out_specs=[VMEM] * (half - 2),
        compiler_params=small,
        name="merge_rest",
    )(mine, rest_from_sib)
    back_far = back_mixed(sent_far)
    passed = swapped(
        pl.pallas_call(
            pass_kernel,
            out_shape=block,
            in_specs=[VMEM],
            out_specs=VMEM,
            compiler_params=small,
            name="pass_on",
        )(back_far)
    )
    back = [ahead(sent[m - 1], m, back=True) for m in range(half - 2, 0, -1)]
    key_grad, value_grad = pl.pallas_call(
        total_kernel,
        out_shape=[shape((BLOCK, HEAD_DIM), bf16)] * 2,
        in_specs=[VMEM] * (2 + half),
        out_specs=[VMEM] * 2,
        compiler_params=small,
        name="total_grads",
    )(mine, far_from_sib, back_far, passed, *back)
    return attended, query_grad, key_grad, value_grad


def solution(mesh):
    split = P(AXES, None)
    devices = mesh.shape["pb"] * mesh.shape["kv"]
    return jax.shard_map(
        functools.partial(local, devices),
        mesh=mesh,
        in_specs=(split, split, split, split, P()),
        out_specs=(split, split, split, split),
        check_vma=False,
    )
```

```python
import functools
import math

import jax
import jax.numpy as jnp
from jax import lax
from jax.experimental import pallas as pl
from jax.experimental.pallas import tpu as pltpu
from jax.sharding import PartitionSpec as P

HEADS = 8
HEAD_DIM = 128
BLOCK = 128
FLAT = HEADS * BLOCK
AXES = ("pb", "kv")
SCALE = HEAD_DIM ** (-0.5)
SCALE_LOG2 = SCALE / math.log(2.0)
FAR = 1e30
COLS = 256
MIB = 2**20

VMEM = pl.BlockSpec(memory_space=pltpu.VMEM)
HBM = pl.BlockSpec(memory_space=pltpu.HBM)


def dot(left, right, left_dim, right_dim):
    return lax.dot_general(
        left, right, (((left_dim,), (right_dim,)), ((), ())), preferred_element_type=jnp.float32
    )


def rows_of(block):
    return slice(block * BLOCK, (block + 1) * BLOCK)


class Slots:
    def __init__(self, window):
        self.window = window
        self.half = half = window // 2
        self.arrival = list(range(1, half))
        lins = [("lin", k) for k in self.arrival]
        sibs = [("sib", k) for k in self.arrival]
        self.middle = lins[:-1]
        self.closing = sibs[:-1] + lins[-1:]
        self.late = [sibs[-1], "last"]
        self.stages = [["own"], self.middle, self.closing, self.late]
        self.swapped = self.closing[:-1] + ["swap"] + self.closing[-1:]
        self.mine = ["own"] + self.middle + ["keep"]

    def place(self, slot):
        for at, group in enumerate([*self.stages[:-1], ["keep"]]):
            if slot in group:
                return at, rows_of(group.index(slot))

    def distance(self, slot):
        _, chip, core = position()
        if slot == "last":
            return jnp.where(core == 0, self.window - 1, 1)
        kind, m = slot
        chips = lax.rem(chip - lax.bitwise_xor(chip, m) + self.half, self.half)
        return 2 * chips if kind == "lin" else 2 * chips - 1 + 2 * core


def position():
    column = lax.axis_index("kv")
    return lax.axis_index("pb") * lax.axis_size("kv") + column, column // 2, lax.rem(column, 2)


def reached(doc_ref, slots, slot):
    me, _, _ = position()
    at = me - slots.distance(slot)
    return (at >= 0) & (doc_ref[jnp.maximum(at, 0)] == doc_ref[me])


def stacked(refs, part):
    return jnp.concatenate([ref[part * BLOCK : (part + 1) * BLOCK, :] for ref in refs], axis=0)


def tile_of(column):
    return slice(column * COLS, (column + 1) * COLS)


def absorb(parts, probs_grad, biases, top, total, mixed):
    new_top = top
    for part, bias in zip(parts, biases):
        new_top = jnp.maximum(new_top, jnp.max(part, axis=0, keepdims=True) * SCALE_LOG2 + bias)
    rescale = jnp.exp2(top - new_top)
    total, mixed = total * rescale, mixed * rescale
    powers = []
    for s, (part, bias) in enumerate(zip(parts, biases)):
        power = jnp.exp2(part * SCALE_LOG2 - (new_top - bias))
        powers.append(power)
        total = total + jnp.sum(power, axis=0, keepdims=True)
        mixed = mixed + jnp.sum(power * probs_grad[s * BLOCK : (s + 1) * BLOCK, :], axis=0, keepdims=True)
    return powers, new_top, total, mixed


def pair_kernel(key_ref, value_ref, pair_ref, sems):
    copies = [
        pltpu.make_async_copy(ref, pair_ref.at[part * BLOCK : (part + 1) * BLOCK, :], sems.at[part])
        for part, ref in enumerate((key_ref, value_ref))
    ]
    for copy in copies:
        copy.start()
    for copy in copies:
        copy.wait()


def own_kernel(
    slots, doc_hbm, query_ref, grad_ref, own_ref,
    query_rows, grad_rows, bias_ref, powers_ref, probs_ref, stats_ref, doc_ref, doc_sem, sems,
):
    copies = [pltpu.make_async_copy(doc_hbm, doc_ref, doc_sem)]
    for h in range(HEADS):
        rows = slice(h * BLOCK, (h + 1) * BLOCK)
        copies.append(pltpu.make_async_copy(query_ref.at[:, rows], query_rows.at[rows, :], sems.at[0, h]))
        copies.append(pltpu.make_async_copy(grad_ref.at[:, rows], grad_rows.at[rows, :], sems.at[1, h]))
    for copy in copies:
        copy.start()
    key_row = lax.broadcasted_iota(jnp.int32, (BLOCK, COLS), 0)
    token = lax.broadcasted_iota(jnp.int32, (BLOCK, COLS), 1) % BLOCK
    causal = key_row <= token
    for copy in copies:
        copy.wait()
    for row, slot in enumerate(slots.middle + slots.closing + slots.late):
        bias = jnp.where(reached(doc_ref, slots, slot), 0.0, -FAR)
        bias_ref[row : row + 1, :] = jnp.full((1, FLAT), bias, jnp.float32)
    for column in range(FLAT // COLS):
        cols = tile_of(column)
        scores = dot(own_ref[:BLOCK, :], query_rows[cols, :], 1, 1)
        probs_grad = dot(own_ref[BLOCK:, :], grad_rows[cols, :], 1, 1)
        scores = jnp.where(causal, scores, -FAR)
        start = jnp.full((1, COLS), -FAR, jnp.float32), jnp.zeros((1, COLS)), jnp.zeros((1, COLS))
        put_stage([scores], probs_grad, [0.0], start, column, powers_ref, probs_ref, stats_ref)


def put_stage(parts, probs_grad, biases, start, column, powers_ref, probs_ref, stats_ref):
    cols = tile_of(column)
    powers, top, total, mixed = absorb(parts, probs_grad, biases, *start)
    for s, power in enumerate(powers):
        powers_ref[s * BLOCK : (s + 1) * BLOCK, cols] = power
    probs_ref[:, cols] = probs_grad
    for row, value in enumerate((top, total, mixed)):
        stats_ref[row : row + 1, cols] = value


def stage_kernel(first, count, *refs):
    bias_ref, query_rows, grad_rows, before_ref = refs[:4]
    blocks = refs[4 : 4 + count]
    powers_ref, probs_ref, stats_ref = refs[4 + count :]
    keys, values = stacked(blocks, 0), stacked(blocks, 1)
    for column in range(FLAT // COLS):
        cols = tile_of(column)
        scores = dot(keys, query_rows[cols, :], 1, 1)
        probs_grad = dot(values, grad_rows[cols, :], 1, 1)
        parts = [scores[rows_of(s), :] for s in range(count)]
        start = tuple(before_ref[row : row + 1, cols] for row in range(3))
        biases = [bias_ref[row : row + 1, cols] for row in range(first, first + count)]
        put_stage(parts, probs_grad, biases, start, column, powers_ref, probs_ref, stats_ref)


def put_weights(slot_rows, cols, powers, factor, probs, delta, weights_ref, score_grad_ref):
    weights = powers * factor
    weights_ref[slot_rows, cols] = weights.astype(jnp.bfloat16)
    score_grad_ref[slot_rows, cols] = (weights * (probs - delta)).astype(jnp.bfloat16)


def put_grads(weights_ref, score_grad_ref, query_rows, grad_rows, out_ref):
    key_grad = dot(score_grad_ref[...], query_rows[...], 1, 0) * SCALE
    value_grad = dot(weights_ref[...], grad_rows[...], 1, 0)
    for k in range(out_ref.shape[0]):
        out_ref[k, :BLOCK, :] = key_grad[rows_of(k), :].astype(out_ref.dtype)
        out_ref[k, BLOCK:, :] = value_grad[rows_of(k), :].astype(out_ref.dtype)


def put_either(core, even, odd, ref):
    @pl.when(core == 0)
    def _():
        ref[...] = even[...]

    @pl.when(core == 1)
    def _():
        ref[...] = odd[...]


def late_kernel(slots, *refs):
    bias_ref, query_rows, grad_rows, powers_ref, probs_ref, before_ref = refs[:6]
    sib_ref, far_ref, sib_own_ref = refs[6:9]
    keep_powers, keep_probs, final_ref, weights_ref, score_grad_ref, far_out, rest_out, lin_ref, last_ref = refs[9:]
    _, _, core = position()
    even = core == 0
    half = slots.half
    put_either(core, far_ref, sib_own_ref, last_ref)
    blocks = [sib_ref, last_ref]
    keys, values = stacked(blocks, 0), stacked(blocks, 1)
    first = slots.window - 1 - len(blocks)
    for column in range(FLAT // COLS):
        cols = tile_of(column)
        scores = dot(keys, query_rows[cols, :], 1, 1)
        probs_grad = dot(values, grad_rows[cols, :], 1, 1)
        parts = [scores[rows_of(s), :] for s in range(2)]
        start = tuple(before_ref[row : row + 1, cols] for row in range(3))
        biases = [bias_ref[row : row + 1, cols] for row in range(first, first + 2)]
        powers, top, total, mixed = absorb(parts, probs_grad, biases, *start)
        inverse = 1.0 / total
        delta = mixed * inverse
        for row, value in enumerate((top, inverse, delta)):
            final_ref[row : row + 1, cols] = value
        sib_probs, last_probs = probs_grad[rows_of(0), :], probs_grad[rows_of(1), :]
        keep_powers[:, cols] = jnp.where(even, powers[1], powers[0])
        keep_probs[:, cols] = jnp.where(even, last_probs, sib_probs)
        factor = jnp.exp2(start[0] - top) * inverse
        for s, slot in enumerate(slots.swapped):
            if slot == "swap":
                piece = jnp.where(even, powers[0], powers[1]), inverse, jnp.where(even, sib_probs, last_probs)
            else:
                _, rows = slots.place(slot)
                piece = powers_ref[rows, cols], factor, probs_ref[rows, cols]
            put_weights(rows_of(s), cols, *piece, delta, weights_ref, score_grad_ref)
    key_grad = dot(score_grad_ref[...], query_rows[...], 1, 0) * SCALE
    value_grad = dot(weights_ref[...], grad_rows[...], 1, 0)
    for k in range(half):
        ref, at = (rest_out, k) if k < half - 2 else (far_out, k - (half - 2))
        ref[at, :BLOCK, :] = key_grad[rows_of(k), :].astype(jnp.bfloat16)
        ref[at, BLOCK:, :] = value_grad[rows_of(k), :].astype(jnp.bfloat16)
    lin_ref[:BLOCK, :] = key_grad[rows_of(half - 1), :]
    lin_ref[BLOCK:, :] = value_grad[rows_of(half - 1), :]


def mine_kernel(slots, *refs):
    query_rows, grad_rows, final_ref = refs[:3]
    stages = {0: refs[3:6], 1: refs[6:9], 3: (*refs[9:11], final_ref)}
    weights_ref, score_grad_ref, mine_ref = refs[11:]
    for column in range(FLAT // COLS):
        cols = tile_of(column)
        top, inverse, delta = (final_ref[row : row + 1, cols] for row in range(3))
        for s, slot in enumerate(slots.mine):
            at, rows = slots.place(slot)
            powers_ref, probs_ref, stats_ref = stages[at]
            factor = jnp.exp2(stats_ref[0:1, cols] - top) * inverse
            piece = powers_ref[rows, cols], factor, probs_ref[rows, cols]
            put_weights(rows_of(s), cols, *piece, delta, weights_ref, score_grad_ref)
    key_grad = dot(score_grad_ref[...], query_rows[...], 1, 0) * SCALE
    value_grad = dot(weights_ref[...], grad_rows[...], 1, 0)
    for k in range(slots.half):
        mine_ref[k, :BLOCK, :] = key_grad[rows_of(k), :]
        mine_ref[k, BLOCK:, :] = value_grad[rows_of(k), :]


def query_side_kernel(slots, *refs):
    half = slots.half
    swap_weights, swap_score_grad, mine_weights, mine_score_grad = refs[:4]
    swapped, mine = list(refs[4 : 3 + half]), list(refs[3 + half : 2 + 2 * half])
    sib_ref, far_ref, sib_own_ref, attended_out, query_grad_out = refs[2 + 2 * half : 7 + 2 * half]
    swap_ref, keep_ref, attended_ref, query_grad_ref, sems = refs[7 + 2 * half :]
    _, _, core = position()
    put_either(core, sib_ref, sib_own_ref, swap_ref)
    put_either(core, far_ref, sib_ref, keep_ref)
    swapped.insert(half - 2, swap_ref)
    mine.append(keep_ref)

    def mixed(part, swap_part, mine_part):
        return dot(stacked(swapped, part), swap_part[...], 0, 0) + dot(stacked(mine, part), mine_part[...], 0, 0)

    def put(result_t, ref, out, sem):
        for h in range(HEADS):
            ref[:, rows_of(h)] = result_t[:, rows_of(h)].T.astype(jnp.bfloat16)
        copy = pltpu.make_async_copy(ref, out, sem)
        copy.start()
        return copy

    attended_copy = put(mixed(1, swap_weights, mine_weights), attended_ref, attended_out, sems.at[0])
    query_grad_t = mixed(0, swap_score_grad, mine_score_grad) * SCALE
    query_grad_copy = put(query_grad_t, query_grad_ref, query_grad_out, sems.at[1])
    attended_copy.wait()
    query_grad_copy.wait()


def merge_far_kernel(mine_ref, lin_ref, from_sib_ref, sent_ref):
    _, _, core = position()
    keep = mine_ref[mine_ref.shape[0] - 1]
    far = jnp.where(core == 1, from_sib_ref[0].astype(jnp.float32) + lin_ref[...], keep)
    other = from_sib_ref[1].astype(jnp.float32) + keep
    sent_ref[: 2 * BLOCK, :] = far.astype(jnp.bfloat16)
    sent_ref[2 * BLOCK :, :] = other.astype(jnp.bfloat16)


def merge_rest_kernel(mine_ref, from_sib_ref, *sent_refs):
    for k, ref in enumerate(sent_refs):
        ref[...] = (mine_ref[k + 1] + from_sib_ref[k].astype(jnp.float32)).astype(jnp.bfloat16)


def pass_kernel(far_ref, out_ref):
    _, _, core = position()
    out_ref[...] = jnp.where(core == 1, far_ref[2 * BLOCK :, :], far_ref[: 2 * BLOCK, :])


def total_kernel(mine_ref, from_sib_ref, far_ref, passed_ref, *refs):
    back, (key_ref, value_ref) = refs[:-2], refs[-2:]
    _, _, core = position()
    total = mine_ref[0] + jnp.where(core == 0, from_sib_ref[0], far_ref[: 2 * BLOCK, :]).astype(jnp.float32)
    total = total + passed_ref[...].astype(jnp.float32)
    for ref in back:
        total = total + ref[...].astype(jnp.float32)
    key_ref[...] = total[:BLOCK].astype(jnp.bfloat16)
    value_ref[...] = total[BLOCK:].astype(jnp.bfloat16)


def in_vmem(array):
    return pltpu.with_memory_space_constraint(array, pltpu.VMEM)


def in_hbm(array):
    return pltpu.with_memory_space_constraint(array, pltpu.HBM)


def cost(blocks, products):
    flops = 2 * products * blocks * BLOCK * FLAT * HEAD_DIM
    return pl.CostEstimate(flops=flops, bytes_accessed=blocks * BLOCK * FLAT * 4, transcendentals=0)


def local(devices, queries, key_rows, value_rows, out_grad, doc_ids):
    window = lax.axis_size("kv")
    slots = Slots(window)
    half = slots.half
    bf16, f32 = jnp.bfloat16, jnp.float32
    shape = jax.ShapeDtypeStruct
    small = pltpu.CompilerParams(vmem_limit_bytes=window * MIB // 4)
    params = pltpu.CompilerParams(vmem_limit_bytes=window * MIB)

    def target(i, m):
        top = 1 << (m.bit_length() - 1)
        run, chip, core = i // window, i // 2 % half, i % 2
        run, to = (run, chip ^ m) if not chip & top else (run + 1, chip ^ m)
        if run * window == devices:
            run, to = 0, chip ^ top
        return run * window + 2 * to + core

    def ahead(block, m, back=False):
        route = [(i, target(i, m)) for i in range(devices)]
        return lax.ppermute(block, AXES, [pair[::-1] for pair in route] if back else route)

    def back_mixed(block):
        route = [(target(i, half - 1), i) for i in range(1, devices, 2)]
        route += [((i + window) % devices, i) for i in range(0, devices, 2)]
        return lax.ppermute(block, AXES, route)

    def ahead_even(block):
        route = [(i, i + window if i + window < devices else i ^ 1) for i in range(0, devices, 2)]
        route += [(i, i - window if i >= window else i ^ 1) for i in range(1, devices, 2)]
        return lax.ppermute(block, AXES, route)

    def swapped(block):
        return lax.ppermute(block, AXES, [(i, i ^ 1) for i in range(devices)])

    own = pl.pallas_call(
        pair_kernel,
        out_shape=pltpu.VMEM((2 * BLOCK, HEAD_DIM), bf16),
        in_specs=[HBM, HBM],
        out_specs=VMEM,
        scratch_shapes=[pltpu.SemaphoreType.DMA((2,))],
        compiler_params=small,
        name="pair_up",
    )(in_hbm(key_rows), in_hbm(value_rows))
    sib_own = swapped(own)
    lins = [ahead(own, k) for k in slots.arrival] + [ahead_even(sib_own)]

    def stage(blocks):
        return [
            pltpu.VMEM((blocks * BLOCK, FLAT), f32),
            pltpu.VMEM((blocks * BLOCK, FLAT), f32),
            pltpu.VMEM((8, FLAT), f32),
        ]

    query_rows, grad_rows, bias, *own_stage = pl.pallas_call(
        functools.partial(own_kernel, slots),
        out_shape=[pltpu.VMEM((FLAT, HEAD_DIM), bf16)] * 2 + [pltpu.VMEM((window, FLAT), f32)] + stage(1),
        in_specs=[HBM, HBM, HBM, VMEM],
        out_specs=[VMEM] * 6,
        scratch_shapes=[
            pltpu.SMEM(doc_ids.shape, jnp.int32),
            pltpu.SemaphoreType.DMA,
            pltpu.SemaphoreType.DMA((2, HEADS)),
        ],
        compiler_params=params,
        cost_estimate=cost(1, 2),
        name="own_scores",
    )(in_hbm(doc_ids), in_hbm(queries), in_hbm(out_grad), own)

    lins[0], lins[1], own_stage[2] = lax.optimization_barrier((lins[0], lins[1], own_stage[2]))
    sibs = [swapped(block) for block in lins[: half - 2]]
    held = {("lin", k): block for k, block in zip(slots.arrival[:-1], lins)}

    def next_stage(at, before):
        group = slots.stages[at]
        first = sum(len(earlier) for earlier in slots.stages[1:at])
        return list(
            pl.pallas_call(
                functools.partial(stage_kernel, first, len(group)),
                out_shape=stage(len(group)),
                in_specs=[VMEM] * (4 + len(group)),
                out_specs=[VMEM] * 3,
                compiler_params=params,
                cost_estimate=cost(len(group), 2),
                name="stage_scores",
            )(bias, query_rows, grad_rows, before, *[held[slot] for slot in group])
        )

    middle_stage = next_stage(1, own_stage[2])
    lins[half - 1], lins[half - 2], middle_stage[2] = lax.optimization_barrier(
        (lins[half - 1], lins[half - 2], middle_stage[2])
    )
    sibs.append(swapped(lins[half - 2]))
    held |= {"own": own, "last": lins[-1]}
    for k, block, swap in zip(slots.arrival, lins, sibs):
        held["lin", k] = block
        held["sib", k] = swap
    closing_stage = next_stage(2, middle_stage[2])

    sib, far, near = held[slots.late[0]], held["last"], sib_own
    weights = [pltpu.VMEM((half * BLOCK, FLAT), bf16)] * 2
    *keep, final, swap_weights, swap_score_grad, far_out, rest_out, lin_out = pl.pallas_call(
        functools.partial(late_kernel, slots),
        out_shape=stage(1)
        + weights
        + [pltpu.VMEM((blocks, 2 * BLOCK, HEAD_DIM), bf16) for blocks in (2, half - 2)]
        + [pltpu.VMEM((2 * BLOCK, HEAD_DIM), f32)],
        in_specs=[VMEM] * 9,
        out_specs=[VMEM] * 8,
        scratch_shapes=[pltpu.VMEM((2 * BLOCK, HEAD_DIM), bf16)],
        compiler_params=params,
        cost_estimate=cost(window, 2),
        name="late_scores",
    )(bias, query_rows, grad_rows, *closing_stage, sib, far, near)
    far_from_sib, rest_from_sib = swapped(far_out), swapped(rest_out)

    mine_weights, mine_score_grad, mine = pl.pallas_call(
        functools.partial(mine_kernel, slots),
        out_shape=weights + [pltpu.VMEM((half, 2 * BLOCK, HEAD_DIM), f32)],
        in_specs=[VMEM] * 11,
        out_specs=[VMEM] * 3,
        compiler_params=params,
        cost_estimate=cost(half, 2),
        name="other_grads",
    )(query_rows, grad_rows, final, *own_stage, *middle_stage, *keep)

    attended, query_grad = pl.pallas_call(
        functools.partial(query_side_kernel, slots),
        out_shape=[shape(queries.shape, bf16)] * 2,
        in_specs=[VMEM] * (5 + 2 * half),
        out_specs=[HBM] * 2,
        scratch_shapes=[
            pltpu.VMEM((2 * BLOCK, HEAD_DIM), bf16),
            pltpu.VMEM((2 * BLOCK, HEAD_DIM), bf16),
            pltpu.VMEM(queries.shape, bf16),
            pltpu.VMEM(queries.shape, bf16),
            pltpu.SemaphoreType.DMA((2,)),
        ],
        compiler_params=params,
        cost_estimate=cost(window, 2),
        name="query_side",
    )(
        *[in_vmem(part) for part in (swap_weights, swap_score_grad, mine_weights, mine_score_grad)],
        *[held[slot] for slot in slots.closing + ["own"] + slots.middle],
        sib, far, near,
    )

    block = pltpu.VMEM((2 * BLOCK, HEAD_DIM), bf16)
    sent_far = pl.pallas_call(
        merge_far_kernel,
        out_shape=pltpu.VMEM((4 * BLOCK, HEAD_DIM), bf16),
        in_specs=[VMEM] * 3,
        out_specs=VMEM,
        compiler_params=small,
        name="merge_far",
    )(mine, lin_out, far_from_sib)
    sent = pl.pallas_call(
        merge_rest_kernel,
        out_shape=[block] * (half - 2),
        in_specs=[VMEM] * 2,
        out_specs=[VMEM] * (half - 2),
        compiler_params=small,
        name="merge_rest",
    )(mine, rest_from_sib)
    back_far = back_mixed(sent_far)
    passed = swapped(
        pl.pallas_call(
            pass_kernel,
            out_shape=block,
            in_specs=[VMEM],
            out_specs=VMEM,
            compiler_params=small,
            name="pass_on",
        )(back_far)
    )
    back = [ahead(sent[m - 1], m, back=True) for m in range(1, half - 1)]
    key_grad, value_grad = pl.pallas_call(
        total_kernel,
        out_shape=[shape((BLOCK, HEAD_DIM), bf16)] * 2,
        in_specs=[VMEM] * (2 + half),
        out_specs=[VMEM] * 2,
        compiler_params=small,
        name="total_grads",
    )(mine, far_from_sib, back_far, passed, *back)
    return attended, query_grad, key_grad, value_grad


def solution(mesh):
    split = P(AXES, None)
    devices = mesh.shape["pb"] * mesh.shape["kv"]
    return jax.shard_map(
        functools.partial(local, devices),
        mesh=mesh,
        in_specs=(split, split, split, split, P()),
        out_specs=(split, split, split, split),
        check_vma=False,
    )
```

```python
import functools
import math

import jax
import jax.numpy as jnp
from jax import lax
from jax.experimental import pallas as pl
from jax.experimental.pallas import tpu as pltpu
from jax.sharding import PartitionSpec as P

HEADS = 8
HEAD_DIM = 128
BLOCK = 128
FLAT = HEADS * BLOCK
AXES = ("pb", "kv")
SCALE = HEAD_DIM ** (-0.5)
SCALE_LOG2 = SCALE / math.log(2.0)
FAR = 1e30
COLS = 256
MIB = 2**20

VMEM = pl.BlockSpec(memory_space=pltpu.VMEM)
HBM = pl.BlockSpec(memory_space=pltpu.HBM)


def dot(left, right, left_dim, right_dim):
    return lax.dot_general(
        left, right, (((left_dim,), (right_dim,)), ((), ())), preferred_element_type=jnp.float32
    )


def rows_of(block):
    return slice(block * BLOCK, (block + 1) * BLOCK)


class Slots:
    def __init__(self, window):
        self.window = window
        self.half = half = window // 2
        self.arrival = list(range(1, half))
        lins = [("lin", k) for k in self.arrival]
        sibs = [("sib", k) for k in self.arrival]
        self.middle = lins[:-1]
        self.closing = sibs[:-1] + lins[-1:]
        self.late = [sibs[-1], "last"]
        self.stages = [["own"], self.middle, self.closing, self.late]
        self.swapped = self.closing[:-1] + ["swap"] + self.closing[-1:]
        self.mine = ["own"] + self.middle + ["keep"]

    def place(self, slot):
        for at, group in enumerate([*self.stages[:-1], ["keep"]]):
            if slot in group:
                return at, rows_of(group.index(slot))

    def distance(self, slot):
        _, chip, core = position()
        if slot == "last":
            return jnp.where(core == 0, self.window - 1, 1)
        kind, m = slot
        chips = lax.rem(chip - lax.bitwise_xor(chip, m) + self.half, self.half)
        return 2 * chips if kind == "lin" else 2 * chips - 1 + 2 * core


def position():
    column = lax.axis_index("kv")
    return lax.axis_index("pb") * lax.axis_size("kv") + column, column // 2, lax.rem(column, 2)


def reached(doc_ref, slots, slot):
    me, _, _ = position()
    at = me - slots.distance(slot)
    return (at >= 0) & (doc_ref[jnp.maximum(at, 0)] == doc_ref[me])


def stacked(refs, part):
    return jnp.concatenate([ref[part * BLOCK : (part + 1) * BLOCK, :] for ref in refs], axis=0)


def tile_of(column):
    return slice(column * COLS, (column + 1) * COLS)


def absorb(parts, probs_grad, biases, top, total, mixed):
    new_top = top
    for part, bias in zip(parts, biases):
        new_top = jnp.maximum(new_top, jnp.max(part, axis=0, keepdims=True) * SCALE_LOG2 + bias)
    rescale = jnp.exp2(top - new_top)
    total, mixed = total * rescale, mixed * rescale
    powers = []
    for s, (part, bias) in enumerate(zip(parts, biases)):
        power = jnp.exp2(part * SCALE_LOG2 - (new_top - bias))
        powers.append(power)
        total = total + jnp.sum(power, axis=0, keepdims=True)
        mixed = mixed + jnp.sum(power * probs_grad[s * BLOCK : (s + 1) * BLOCK, :], axis=0, keepdims=True)
    return powers, new_top, total, mixed


def pair_kernel(key_ref, value_ref, pair_ref, sems):
    copies = [
        pltpu.make_async_copy(ref, pair_ref.at[part * BLOCK : (part + 1) * BLOCK, :], sems.at[part])
        for part, ref in enumerate((key_ref, value_ref))
    ]
    for copy in copies:
        copy.start()
    for copy in copies:
        copy.wait()


def own_kernel(
    slots, doc_hbm, query_ref, grad_ref, own_ref,
    query_rows, grad_rows, bias_ref, powers_ref, probs_ref, stats_ref, doc_ref, doc_sem, sems,
):
    copies = [pltpu.make_async_copy(doc_hbm, doc_ref, doc_sem)]
    for h in range(HEADS):
        rows = slice(h * BLOCK, (h + 1) * BLOCK)
        copies.append(pltpu.make_async_copy(query_ref.at[:, rows], query_rows.at[rows, :], sems.at[0, h]))
        copies.append(pltpu.make_async_copy(grad_ref.at[:, rows], grad_rows.at[rows, :], sems.at[1, h]))
    for copy in copies:
        copy.start()
    key_row = lax.broadcasted_iota(jnp.int32, (BLOCK, COLS), 0)
    token = lax.broadcasted_iota(jnp.int32, (BLOCK, COLS), 1) % BLOCK
    causal = key_row <= token
    for copy in copies:
        copy.wait()
    for row, slot in enumerate(slots.middle + slots.closing + slots.late):
        bias = jnp.where(reached(doc_ref, slots, slot), 0.0, -FAR)
        bias_ref[row : row + 1, :] = jnp.full((1, FLAT), bias, jnp.float32)
    for column in range(FLAT // COLS):
        cols = tile_of(column)
        scores = dot(own_ref[:BLOCK, :], query_rows[cols, :], 1, 1)
        probs_grad = dot(own_ref[BLOCK:, :], grad_rows[cols, :], 1, 1)
        scores = jnp.where(causal, scores, -FAR)
        start = jnp.full((1, COLS), -FAR, jnp.float32), jnp.zeros((1, COLS)), jnp.zeros((1, COLS))
        put_stage([scores], probs_grad, [0.0], start, column, powers_ref, probs_ref, stats_ref)


def put_stage(parts, probs_grad, biases, start, column, powers_ref, probs_ref, stats_ref):
    cols = tile_of(column)
    powers, top, total, mixed = absorb(parts, probs_grad, biases, *start)
    for s, power in enumerate(powers):
        powers_ref[s * BLOCK : (s + 1) * BLOCK, cols] = power
    probs_ref[:, cols] = probs_grad
    for row, value in enumerate((top, total, mixed)):
        stats_ref[row : row + 1, cols] = value


def stage_kernel(first, count, *refs):
    bias_ref, query_rows, grad_rows, before_ref = refs[:4]
    blocks = refs[4 : 4 + count]
    powers_ref, probs_ref, stats_ref = refs[4 + count :]
    keys, values = stacked(blocks, 0), stacked(blocks, 1)
    for column in range(FLAT // COLS):
        cols = tile_of(column)
        scores = dot(keys, query_rows[cols, :], 1, 1)
        probs_grad = dot(values, grad_rows[cols, :], 1, 1)
        parts = [scores[rows_of(s), :] for s in range(count)]
        start = tuple(before_ref[row : row + 1, cols] for row in range(3))
        biases = [bias_ref[row : row + 1, cols] for row in range(first, first + count)]
        put_stage(parts, probs_grad, biases, start, column, powers_ref, probs_ref, stats_ref)


def put_weights(slot_rows, cols, powers, factor, probs, delta, weights_ref, score_grad_ref):
    weights = powers * factor
    weights_ref[slot_rows, cols] = weights.astype(jnp.bfloat16)
    score_grad_ref[slot_rows, cols] = (weights * (probs - delta)).astype(jnp.bfloat16)


def put_grads(weights_ref, score_grad_ref, query_rows, grad_rows, out_ref):
    key_grad = dot(score_grad_ref[...], query_rows[...], 1, 0) * SCALE
    value_grad = dot(weights_ref[...], grad_rows[...], 1, 0)
    for k in range(out_ref.shape[0]):
        out_ref[k, :BLOCK, :] = key_grad[rows_of(k), :].astype(out_ref.dtype)
        out_ref[k, BLOCK:, :] = value_grad[rows_of(k), :].astype(out_ref.dtype)


def put_either(core, even, odd, ref):
    @pl.when(core == 0)
    def _():
        ref[...] = even[...]

    @pl.when(core == 1)
    def _():
        ref[...] = odd[...]


def late_kernel(slots, *refs):
    bias_ref, query_rows, grad_rows, powers_ref, probs_ref, before_ref = refs[:6]
    sib_ref, far_ref, sib_own_ref = refs[6:9]
    keep_powers, keep_probs, final_ref, weights_ref, score_grad_ref, far_out, rest_out, lin_ref, last_ref = refs[9:]
    _, _, core = position()
    even = core == 0
    half = slots.half
    put_either(core, far_ref, sib_own_ref, last_ref)
    blocks = [sib_ref, last_ref]
    keys, values = stacked(blocks, 0), stacked(blocks, 1)
    first = slots.window - 1 - len(blocks)
    for column in range(FLAT // COLS):
        cols = tile_of(column)
        scores = dot(keys, query_rows[cols, :], 1, 1)
        probs_grad = dot(values, grad_rows[cols, :], 1, 1)
        parts = [scores[rows_of(s), :] for s in range(2)]
        start = tuple(before_ref[row : row + 1, cols] for row in range(3))
        biases = [bias_ref[row : row + 1, cols] for row in range(first, first + 2)]
        powers, top, total, mixed = absorb(parts, probs_grad, biases, *start)
        inverse = 1.0 / total
        delta = mixed * inverse
        for row, value in enumerate((top, inverse, delta)):
            final_ref[row : row + 1, cols] = value
        sib_probs, last_probs = probs_grad[rows_of(0), :], probs_grad[rows_of(1), :]
        keep_powers[:, cols] = jnp.where(even, powers[1], powers[0])
        keep_probs[:, cols] = jnp.where(even, last_probs, sib_probs)
        factor = jnp.exp2(start[0] - top) * inverse
        for s, slot in enumerate(slots.swapped):
            if slot == "swap":
                piece = jnp.where(even, powers[0], powers[1]), inverse, jnp.where(even, sib_probs, last_probs)
            else:
                _, rows = slots.place(slot)
                piece = powers_ref[rows, cols], factor, probs_ref[rows, cols]
            put_weights(rows_of(s), cols, *piece, delta, weights_ref, score_grad_ref)
    key_grad = dot(score_grad_ref[...], query_rows[...], 1, 0) * SCALE
    value_grad = dot(weights_ref[...], grad_rows[...], 1, 0)
    for k in range(half):
        ref, at = (rest_out, k) if k < half - 2 else (far_out, k - (half - 2))
        ref[at, :BLOCK, :] = key_grad[rows_of(k), :].astype(jnp.bfloat16)
        ref[at, BLOCK:, :] = value_grad[rows_of(k), :].astype(jnp.bfloat16)
    lin_ref[:BLOCK, :] = key_grad[rows_of(half - 1), :]
    lin_ref[BLOCK:, :] = value_grad[rows_of(half - 1), :]


def mine_kernel(slots, *refs):
    query_rows, grad_rows, final_ref = refs[:3]
    stages = {0: refs[3:6], 1: refs[6:9], 3: (*refs[9:11], final_ref)}
    weights_ref, score_grad_ref, mine_ref = refs[11:]
    for column in range(FLAT // COLS):
        cols = tile_of(column)
        top, inverse, delta = (final_ref[row : row + 1, cols] for row in range(3))
        for s, slot in enumerate(slots.mine):
            at, rows = slots.place(slot)
            powers_ref, probs_ref, stats_ref = stages[at]
            factor = jnp.exp2(stats_ref[0:1, cols] - top) * inverse
            piece = powers_ref[rows, cols], factor, probs_ref[rows, cols]
            put_weights(rows_of(s), cols, *piece, delta, weights_ref, score_grad_ref)
    key_grad = dot(score_grad_ref[...], query_rows[...], 1, 0) * SCALE
    value_grad = dot(weights_ref[...], grad_rows[...], 1, 0)
    for k in range(slots.half):
        mine_ref[k, :BLOCK, :] = key_grad[rows_of(k), :]
        mine_ref[k, BLOCK:, :] = value_grad[rows_of(k), :]


def query_side_kernel(slots, *refs):
    half = slots.half
    swap_weights, swap_score_grad, mine_weights, mine_score_grad = refs[:4]
    swapped, mine = list(refs[4 : 3 + half]), list(refs[3 + half : 2 + 2 * half])
    sib_ref, far_ref, sib_own_ref, attended_out, query_grad_out = refs[2 + 2 * half : 7 + 2 * half]
    swap_ref, keep_ref, attended_ref, query_grad_ref, sems = refs[7 + 2 * half :]
    _, _, core = position()
    put_either(core, sib_ref, sib_own_ref, swap_ref)
    put_either(core, far_ref, sib_ref, keep_ref)
    swapped.insert(half - 2, swap_ref)
    mine.append(keep_ref)

    def mixed(part, swap_part, mine_part):
        return dot(stacked(swapped, part), swap_part[...], 0, 0) + dot(stacked(mine, part), mine_part[...], 0, 0)

    def put(result_t, ref, out, sem):
        for h in range(HEADS):
            ref[:, rows_of(h)] = result_t[:, rows_of(h)].T.astype(jnp.bfloat16)
        copy = pltpu.make_async_copy(ref, out, sem)
        copy.start()
        return copy

    attended_copy = put(mixed(1, swap_weights, mine_weights), attended_ref, attended_out, sems.at[0])
    query_grad_t = mixed(0, swap_score_grad, mine_score_grad) * SCALE
    query_grad_copy = put(query_grad_t, query_grad_ref, query_grad_out, sems.at[1])
    attended_copy.wait()
    query_grad_copy.wait()


def merge_far_kernel(mine_ref, lin_ref, from_sib_ref, sent_ref):
    _, _, core = position()
    keep = mine_ref[mine_ref.shape[0] - 1]
    far = jnp.where(core == 1, from_sib_ref[0].astype(jnp.float32) + lin_ref[...], keep)
    other = from_sib_ref[1].astype(jnp.float32) + keep
    sent_ref[: 2 * BLOCK, :] = far.astype(jnp.bfloat16)
    sent_ref[2 * BLOCK :, :] = other.astype(jnp.bfloat16)


def merge_rest_kernel(mine_ref, from_sib_ref, *sent_refs):
    for k, ref in enumerate(sent_refs):
        ref[...] = (mine_ref[k + 1] + from_sib_ref[k].astype(jnp.float32)).astype(jnp.bfloat16)


def pass_kernel(far_ref, out_ref):
    _, _, core = position()
    out_ref[...] = jnp.where(core == 1, far_ref[2 * BLOCK :, :], far_ref[: 2 * BLOCK, :])


def total_kernel(mine_ref, from_sib_ref, far_ref, *refs):
    back, passed_ref, (key_ref, value_ref) = refs[:-3], refs[-3], refs[-2:]
    _, _, core = position()
    total = mine_ref[0] + jnp.where(core == 0, from_sib_ref[0], far_ref[: 2 * BLOCK, :]).astype(jnp.float32)
    total = total + passed_ref[...].astype(jnp.float32)
    for ref in back:
        total = total + ref[...].astype(jnp.float32)
    key_ref[...] = total[:BLOCK].astype(jnp.bfloat16)
    value_ref[...] = total[BLOCK:].astype(jnp.bfloat16)


def in_vmem(array):
    return pltpu.with_memory_space_constraint(array, pltpu.VMEM)


def in_hbm(array):
    return pltpu.with_memory_space_constraint(array, pltpu.HBM)


def cost(blocks, products):
    flops = 2 * products * blocks * BLOCK * FLAT * HEAD_DIM
    return pl.CostEstimate(flops=flops, bytes_accessed=blocks * BLOCK * FLAT * 4, transcendentals=0)


def local(devices, queries, key_rows, value_rows, out_grad, doc_ids):
    window = lax.axis_size("kv")
    slots = Slots(window)
    half = slots.half
    bf16, f32 = jnp.bfloat16, jnp.float32
    shape = jax.ShapeDtypeStruct
    small = pltpu.CompilerParams(vmem_limit_bytes=window * MIB // 4)
    params = pltpu.CompilerParams(vmem_limit_bytes=window * MIB)

    def target(i, m):
        top = 1 << (m.bit_length() - 1)
        run, chip, core = i // window, i // 2 % half, i % 2
        run, to = (run, chip ^ m) if not chip & top else (run + 1, chip ^ m)
        if run * window == devices:
            run, to = 0, chip ^ top
        return run * window + 2 * to + core

    def ahead(block, m, back=False):
        route = [(i, target(i, m)) for i in range(devices)]
        return lax.ppermute(block, AXES, [pair[::-1] for pair in route] if back else route)

    def back_mixed(block):
        route = [(target(i, half - 1), i) for i in range(1, devices, 2)]
        route += [((i + window) % devices, i) for i in range(0, devices, 2)]
        return lax.ppermute(block, AXES, route)

    def ahead_odd(block):
        route = [(i, i + window if i + window < devices else i ^ 1) for i in range(1, devices, 2)]
        route += [(i, i - window if i >= window else i ^ 1) for i in range(0, devices, 2)]
        return lax.ppermute(block, AXES, route)

    def swapped(block):
        return lax.ppermute(block, AXES, [(i, i ^ 1) for i in range(devices)])

    own = pl.pallas_call(
        pair_kernel,
        out_shape=pltpu.VMEM((2 * BLOCK, HEAD_DIM), bf16),
        in_specs=[HBM, HBM],
        out_specs=VMEM,
        scratch_shapes=[pltpu.SemaphoreType.DMA((2,))],
        compiler_params=small,
        name="pair_up",
    )(in_hbm(key_rows), in_hbm(value_rows))
    lins = [ahead(own, k) for k in slots.arrival] + [ahead_odd(own)]
    sib_own = swapped(own)

    def stage(blocks):
        return [
            pltpu.VMEM((blocks * BLOCK, FLAT), f32),
            pltpu.VMEM((blocks * BLOCK, FLAT), f32),
            pltpu.VMEM((8, FLAT), f32),
        ]

    query_rows, grad_rows, bias, *own_stage = pl.pallas_call(
        functools.partial(own_kernel, slots),
        out_shape=[pltpu.VMEM((FLAT, HEAD_DIM), bf16)] * 2 + [pltpu.VMEM((window, FLAT), f32)] + stage(1),
        in_specs=[HBM, HBM, HBM, VMEM],
        out_specs=[VMEM] * 6,
        scratch_shapes=[
            pltpu.SMEM(doc_ids.shape, jnp.int32),
            pltpu.SemaphoreType.DMA,
            pltpu.SemaphoreType.DMA((2, HEADS)),
        ],
        compiler_params=params,
        cost_estimate=cost(1, 2),
        name="own_scores",
    )(in_hbm(doc_ids), in_hbm(queries), in_hbm(out_grad), own)

    lins[0], lins[1], own_stage[2] = lax.optimization_barrier((lins[0], lins[1], own_stage[2]))
    sibs = [swapped(block) for block in lins[: half - 2]]
    held = {("lin", k): block for k, block in zip(slots.arrival[:-1], lins)}

    def next_stage(at, before):
        group = slots.stages[at]
        first = sum(len(earlier) for earlier in slots.stages[1:at])
        return list(
            pl.pallas_call(
                functools.partial(stage_kernel, first, len(group)),
                out_shape=stage(len(group)),
                in_specs=[VMEM] * (4 + len(group)),
                out_specs=[VMEM] * 3,
                compiler_params=params,
                cost_estimate=cost(len(group), 2),
                name="stage_scores",
            )(bias, query_rows, grad_rows, before, *[held[slot] for slot in group])
        )

    middle_stage = next_stage(1, own_stage[2])
    lins[half - 1], lins[half - 2], middle_stage[2] = lax.optimization_barrier(
        (lins[half - 1], lins[half - 2], middle_stage[2])
    )
    sibs += [swapped(block) for block in lins[half - 2 :]]
    held |= {"own": own, "last": sibs[-1]}
    for k, block, swap in zip(slots.arrival, lins, sibs):
        held["lin", k] = block
        held["sib", k] = swap
    closing_stage = next_stage(2, middle_stage[2])

    sib, far, near = held[slots.late[0]], held["last"], sib_own
    weights = [pltpu.VMEM((half * BLOCK, FLAT), bf16)] * 2
    *keep, final, swap_weights, swap_score_grad, far_out, rest_out, lin_out = pl.pallas_call(
        functools.partial(late_kernel, slots),
        out_shape=stage(1)
        + weights
        + [pltpu.VMEM((blocks, 2 * BLOCK, HEAD_DIM), bf16) for blocks in (2, half - 2)]
        + [pltpu.VMEM((2 * BLOCK, HEAD_DIM), f32)],
        in_specs=[VMEM] * 9,
        out_specs=[VMEM] * 8,
        scratch_shapes=[pltpu.VMEM((2 * BLOCK, HEAD_DIM), bf16)],
        compiler_params=params,
        cost_estimate=cost(window, 2),
        name="late_scores",
    )(bias, query_rows, grad_rows, *closing_stage, sib, far, near)
    far_from_sib, rest_from_sib = swapped(far_out), swapped(rest_out)

    mine_weights, mine_score_grad, mine = pl.pallas_call(
        functools.partial(mine_kernel, slots),
        out_shape=weights + [pltpu.VMEM((half, 2 * BLOCK, HEAD_DIM), f32)],
        in_specs=[VMEM] * 11,
        out_specs=[VMEM] * 3,
        compiler_params=params,
        cost_estimate=cost(half, 2),
        name="other_grads",
    )(query_rows, grad_rows, final, *own_stage, *middle_stage, *keep)

    attended, query_grad = pl.pallas_call(
        functools.partial(query_side_kernel, slots),
        out_shape=[shape(queries.shape, bf16)] * 2,
        in_specs=[VMEM] * (5 + 2 * half),
        out_specs=[HBM] * 2,
        scratch_shapes=[
            pltpu.VMEM((2 * BLOCK, HEAD_DIM), bf16),
            pltpu.VMEM((2 * BLOCK, HEAD_DIM), bf16),
            pltpu.VMEM(queries.shape, bf16),
            pltpu.VMEM(queries.shape, bf16),
            pltpu.SemaphoreType.DMA((2,)),
        ],
        compiler_params=params,
        cost_estimate=cost(window, 2),
        name="query_side",
    )(
        *[in_vmem(part) for part in (swap_weights, swap_score_grad, mine_weights, mine_score_grad)],
        *[held[slot] for slot in slots.closing + ["own"] + slots.middle],
        sib, far, near,
    )

    block = pltpu.VMEM((2 * BLOCK, HEAD_DIM), bf16)
    sent_far = pl.pallas_call(
        merge_far_kernel,
        out_shape=pltpu.VMEM((4 * BLOCK, HEAD_DIM), bf16),
        in_specs=[VMEM] * 3,
        out_specs=VMEM,
        compiler_params=small,
        name="merge_far",
    )(mine, lin_out, far_from_sib)
    sent = pl.pallas_call(
        merge_rest_kernel,
        out_shape=[block] * (half - 2),
        in_specs=[VMEM] * 2,
        out_specs=[VMEM] * (half - 2),
        compiler_params=small,
        name="merge_rest",
    )(mine, rest_from_sib)
    back_far = back_mixed(sent_far)
    passed = swapped(
        pl.pallas_call(
            pass_kernel,
            out_shape=block,
            in_specs=[VMEM],
            out_specs=VMEM,
            compiler_params=small,
            name="pass_on",
        )(back_far)
    )
    back = [ahead(sent[m - 1], m, back=True) for m in range(half - 2, 0, -1)]
    key_grad, value_grad = pl.pallas_call(
        total_kernel,
        out_shape=[shape((BLOCK, HEAD_DIM), bf16)] * 2,
        in_specs=[VMEM] * (2 + half),
        out_specs=[VMEM] * 2,
        compiler_params=small,
        name="total_grads",
    )(mine, far_from_sib, back_far, *back, passed)
    return attended, query_grad, key_grad, value_grad


def solution(mesh):
    split = P(AXES, None)
    devices = mesh.shape["pb"] * mesh.shape["kv"]
    return jax.shard_map(
        functools.partial(local, devices),
        mesh=mesh,
        in_specs=(split, split, split, split, P()),
        out_specs=(split, split, split, split),
        check_vma=False,
    )
```
